32 devices in a mesh: dp: 8 (over z, y), mp: 4 (over x, core).
Axes of the slice: x: 2, y: 2, z: 4, core: 2. Of those that a mesh axis runs over, the one named last changes fastest.
Arguments:
- tokens: bfloat16 [16384, 1024], P(('dp', 'mp')), may hold values from -6 to 6
- segment_ids: int32 [16, 1024], P('dp'), may hold values from 0 to 15, never falling along the last dimension, each value on 1 to 128 neighbouring positions
- valid_mask: int32 [16, 1024], P('dp'), may hold values from 0 to 1, as said below
- patch_index: int32 [16, 1024], P('dp'), may hold values from 0 to 195
- gsd_index: int32 [16, 16], P('dp'), may hold values from 0 to 7
- w_qkv: bfloat16 [3, 1024, 1024], P(None, None, 'mp'), may hold values from -0.1875 to 0.1875
- bias_qv: bfloat16 [2, 1024], P(None, 'mp'), may hold values from -3 to 3
- w_out: bfloat16 [1024, 1024], P('mp'), may hold values from -0.75 to 0.75
- b_out: bfloat16 [1024], replicated, may hold values from -2 to 2
- gain_one: bfloat16 [1024], replicated, may hold values from 0.5 to 1.5
- shift_one: bfloat16 [1024], replicated, may hold values from -2 to 2
- gain_two: bfloat16 [1024], replicated, may hold values from 0.5 to 1.5
- shift_two: bfloat16 [1024], replicated, may hold values from -2 to 2
- w_up: bfloat16 [1024, 4096], P(None, 'mp'), may hold values from -0.1875 to 0.1875
- b_up: bfloat16 [4096], P('mp'), may hold values from -2 to 2
- w_down: bfloat16 [4096, 1024], P('mp'), may hold values from -0.125 to 0.125
- b_down: bfloat16 [1024], replicated, may hold values from -2 to 2
- cotangent: bfloat16 [16384, 1024], P(('dp', 'mp')), may hold values from -6 to 6
Outputs:
- layer_out: bfloat16 [16384, 1024], P(('dp', 'mp'))
- grad_tokens: bfloat16 [16384, 1024], P(('dp', 'mp'))
- grad_w_qkv: float32 [3, 1024, 1024], P(None, None, 'mp')
- grad_bias_qv: float32 [2, 1024], P(None, 'mp')
- grad_w_out: float32 [1024, 1024], P('mp')
- grad_b_out: float32 [1024], replicated
- grad_gain_one: float32 [1024], replicated
- grad_shift_one: float32 [1024], replicated
- grad_gain_two: float32 [1024], replicated
- grad_shift_two: float32 [1024], replicated
- grad_w_up: float32 [1024, 4096], P(None, 'mp')
- grad_b_up: float32 [4096], P('mp')
- grad_w_down: float32 [4096, 1024], P('mp')
- grad_b_down: float32 [1024], replicated
The draws below stay inside these ranges and needn't reach their ends.
Inputs may be any that keep to these rules, and one draw needn't show every extreme that they name: `segment_ids`: within a row segment numbers never fall; each image has 1 to 128 positions. `valid_mask`: A row's padded positions, if any, are its last ones.
All inputs are finite; a program needn't handle non-finite values.
Results may differ from the reference program's by a relative error of at most 0.02.
Values may be sent and summed in bfloat16 or wider, within the bound.
No kernel may reach another device: no remote copies, remote signals or barrier semaphores. Data moves between devices by JAX's collectives and lax.ppermute only.
A program may use at most 192 MiB of HBM per device.

```python
import math
import jax
import jax.numpy as jnp
import numpy as np
from jax import lax

D = 1024
HEADS = 16
HEAD = 64
FF = 4096
SEQ = 1024
SEGS = 16
MOST = 128
GRID = 14
GSDS = 8
NROWS = 16
TOKENS = 16384


def draw_valid_mask(key, part):
    key = jax.random.fold_in(key, 7)
    padding = jax.random.randint(key, (NROWS, 1), 0, SEQ // 8 + 1)
    position = jnp.arange(SEQ, dtype=jnp.int32)[None, :]
    return (position < SEQ - padding).astype(jnp.int32)


def set_ends(drawn, rng, least, high):
    shape = drawn.shape
    spot = [jax.random.randint(jax.random.fold_in(rng, axis), (), 0, shape[axis]) for axis in range(len(shape))]
    drawn = drawn.at[tuple(spot)].set(least)
    longest = shape.index(max(shape))
    spot[longest] = (spot[longest] + 1) % shape[longest]
    return drawn.at[tuple(spot)].set(high)


def levels(key, shape, cuts, least, largest):
    factor_of, own = 1.0, jax.random.fold_in(key, 6)
    for dim, parts in cuts:
        steps = jnp.exp(jax.random.uniform(jax.random.fold_in(own, dim), (parts,), jnp.float32, least / len(cuts), largest / len(cuts)))
        factor_of = factor_of * jnp.repeat(steps, shape[dim] // parts).reshape([-1 if axis == dim else 1 for axis in range(len(shape))])
    return factor_of


def length_profile(amount, total, limit, slope):
    loads = [(1 << 20) // math.isqrt(rank ** slope) + 1 for rank in range(2, amount + 1)]
    rest, given = total - limit - (amount - 1), [1] * (amount - 1)
    while rest > 0:
        free = [i for i in range(amount - 1) if given[i] < limit]
        pool, budget = sum([loads[i] for i in free]), rest
        for i in free:
            more = min(limit - given[i], max(1, budget * loads[i] // pool), rest)
            given[i] = given[i] + more
            rest = rest - more
    return np.array([limit] + given)


def uneven_parts(key, count, total, bound, slope):
    if count == 2:
        one = jax.random.randint(key, (), max(1, total - bound), min(bound, total - 1) + 1)
        return jnp.stack([one, total - one])
    tallies = jnp.asarray(length_profile(count, total, bound, slope), jnp.int32)
    pairs = (count - 1) // 2
    donor, taker = tallies[1:1 + 2 * pairs:2], tallies[2:2 + 2 * pairs:2]
    room = jnp.minimum(donor - 1, bound - taker)
    passed = jax.random.randint(jax.random.fold_in(key, 1), (pairs,), 0, 1 << 20) % (room + 1)
    tallies = tallies.at[1:1 + 2 * pairs:2].set(donor - passed).at[2:2 + 2 * pairs:2].set(taker + passed)
    return tallies[jax.random.permutation(jax.random.fold_in(key, 2), count)]


def noise(stream_key, shape, width, bound, split=(), held_as=jnp.bfloat16):
    result = width * jax.random.normal(stream_key, shape, jnp.float32)
    if split:
        result = result * levels(stream_key, shape, split, -0.22, 0.18)
    return jnp.clip(result, -bound, bound).astype(held_as)


def setup_inputs(seed: int = 0) -> dict:
    key_list = jax.random.split(jax.random.key(seed), 19)
    tokens = noise(key_list[0], (TOKENS, D), 1.0, 6.0, ((0, 32),))
    segment_ids = jax.vmap(lambda own: jnp.searchsorted(jnp.cumsum(uneven_parts(own, SEGS, SEQ, MOST, 1)), jnp.arange(SEQ), side="right"))(jax.random.split(key_list[1], NROWS)).reshape((NROWS, SEQ)).astype(jnp.int32)
    valid_mask = draw_valid_mask(jax.random.fold_in(key_list[18], 71), 0)
    patch_index = set_ends(jax.random.randint(key_list[3], (NROWS, SEQ), 0, GRID * GRID), jax.random.fold_in(key_list[3], 1), 0, (GRID * GRID) - 1).astype(jnp.int32)
    gsd_index = set_ends(jax.random.randint(key_list[4], (NROWS, SEGS), 0, GSDS), jax.random.fold_in(key_list[4], 1), 0, GSDS - 1).astype(jnp.int32)
    w_qkv = noise(key_list[5], (3, D, D), D ** -0.5, 0.1875, ((2, 4),))
    bias_qv = noise(key_list[6], (2, D), 0.5, 3.0, ((1, 4),))
    w_out = noise(key_list[7], (D, D), (D // 16) ** -0.5, 0.75, ((0, 4),))
    b_out = noise(key_list[8], (D,), 0.3, 2.0)
    gain_one = jnp.clip(1.0 + 0.1 * jax.random.normal(key_list[9], (D,), jnp.float32), 0.5, 1.5).astype(jnp.bfloat16)
    shift_one = noise(key_list[10], (D,), 0.3, 2.0)
    gain_two = jnp.clip(1.0 + 0.1 * jax.random.normal(key_list[11], (D,), jnp.float32), 0.5, 1.5).astype(jnp.bfloat16)
    shift_two = noise(key_list[12], (D,), 0.3, 2.0)
    w_up = noise(key_list[13], (D, FF), D ** -0.5, 0.1875, ((1, 4),))
    b_up = noise(key_list[14], (FF,), 0.3, 2.0, ((0, 4),))
    w_down = noise(key_list[15], (FF, D), (FF // 2) ** -0.5, 0.125, ((0, 4),))
    b_down = noise(key_list[16], (D,), 0.3, 2.0)
    cotangent = noise(key_list[17], (TOKENS, D), 1.0, 6.0, ((0, 32),))
    return {"tokens": tokens, "segment_ids": segment_ids, "valid_mask": valid_mask, "patch_index": patch_index, "gsd_index": gsd_index, "w_qkv": w_qkv, "bias_qv": bias_qv, "w_out": w_out, "b_out": b_out, "gain_one": gain_one, "shift_one": shift_one, "gain_two": gain_two, "shift_two": shift_two, "w_up": w_up, "b_up": b_up, "w_down": w_down, "b_down": b_down, "cotangent": cotangent}


EPSILON = 1e-06
MASKED = -1000000000.0
HIGH = lax.Precision.HIGHEST

@jax.custom_vjp
def low(v):
    return lax.optimization_barrier(v.astype(jnp.bfloat16)).astype(jnp.float32)

@jax.custom_vjp
def low_back(v):
    return v

def low_keep(v):
    return (low(v), None)

def low_pass(kept, grad):
    return (grad,)

def back_keep(v):
    return (v, None)

def back_low(kept, grad):
    return (low(grad),)
low.defvjp(low_keep, low_pass)
low_back.defvjp(back_keep, back_low)

def layer_norm(values, gain_vec, shift_vec):
    row_mean = lax.optimization_barrier(jnp.mean(values, axis=-1, keepdims=True))
    centred = values - row_mean
    row_var = lax.optimization_barrier(jnp.mean(centred * centred, axis=-1, keepdims=True))
    return centred * lax.rsqrt(row_var + EPSILON) * gain_vec + shift_vec

def ratios(segment_ids, gsd_index):
    ratio_table = 2.0 ** (0.5 * jnp.arange(GSDS, dtype=jnp.float32) - 1.0)
    image_ratio = lax.optimization_barrier(jnp.sum(jnp.where(gsd_index[..., None] == jnp.arange(GSDS, dtype=jnp.int32), ratio_table, 0.0), axis=-1))
    in_image = segment_ids[..., None] == jnp.arange(SEGS, dtype=jnp.int32)
    return lax.optimization_barrier(jnp.sum(jnp.where(in_image, image_ratio[:, None, :], 0.0), axis=-1))

def encode(patch_flat, ratio_flat):
    quarter = D // 4
    frequency = 1.0 / 10000.0 ** (jnp.arange(quarter, dtype=jnp.float32) / quarter)
    grid_row = (patch_flat // GRID).astype(jnp.float32) * ratio_flat
    grid_col = (patch_flat % GRID).astype(jnp.float32) * ratio_flat
    row_angle = grid_row[:, None] * frequency
    col_angle = grid_col[:, None] * frequency
    return jnp.concatenate([jnp.sin(row_angle), jnp.cos(row_angle), jnp.sin(col_angle), jnp.cos(col_angle)], axis=-1)

def attend(pieces):
    queries, key_rows, values, segments, valid = pieces
    scores = jnp.einsum('qhd,khd->hqk', queries, key_rows, precision=HIGH) * HEAD ** (-0.5)
    scores = low_back(scores)
    position = jnp.arange(SEQ, dtype=jnp.int32)
    allowed = (segments[:, None] == segments[None, :]) & ((valid[None, :] == 1) | (position[:, None] == position[None, :]))
    scores = jnp.where(allowed[None], scores, MASKED)
    row_max = lax.optimization_barrier(jnp.max(scores, axis=-1, keepdims=True))
    weight = jnp.exp(scores - row_max)
    attn_prob = low(weight / lax.optimization_barrier(jnp.sum(weight, axis=-1, keepdims=True)))
    return jnp.einsum('hqk,khd->qhd', attn_prob, values, precision=HIGH)

def forward(tokens, w_qkv, bias_qv, w_out, b_out, gain_one, shift_one, gain_two, shift_two, w_up, b_up, w_down, b_down, pos, segment_ids, valid_mask):
    start_sum = tokens + pos
    normed = low(layer_norm(start_sum, gain_one, shift_one))
    projected = jnp.einsum('td,cde->cte', normed, w_qkv, precision=HIGH)
    queries = low_back(low(projected[0] + bias_qv[0]))
    key_rows = low_back(low(projected[1]))
    values = low_back(low(projected[2] + bias_qv[1]))
    head_shape = (NROWS, SEQ, HEADS, HEAD)
    attn_mixed = lax.map(jax.checkpoint(attend), (queries.reshape(head_shape), key_rows.reshape(head_shape), values.reshape(head_shape), segment_ids, valid_mask))
    attn_mixed = low_back(low(attn_mixed.reshape(TOKENS, D)))
    attn = low_back(jnp.dot(attn_mixed, w_out, precision=HIGH))
    after_attn = start_sum + attn + b_out
    normed_two = low(layer_norm(after_attn, gain_two, shift_two))
    up = low_back(jnp.dot(normed_two, w_up, precision=HIGH) + b_up)
    act = low(jax.nn.gelu(up, approximate=False))
    down = low_back(jnp.dot(act, w_down, precision=HIGH))
    after_ffn = after_attn + down + b_down
    return after_ffn * valid_mask.reshape(TOKENS, 1).astype(jnp.float32)

def reference(tokens, segment_ids, valid_mask, patch_index, gsd_index, w_qkv, bias_qv, w_out, b_out, gain_one, shift_one, gain_two, shift_two, w_up, b_up, w_down, b_down, cotangent):
    pos = encode(patch_index.reshape(-1), ratios(segment_ids, gsd_index).reshape(-1))
    floats = tuple((item.astype(jnp.float32) for item in (tokens, w_qkv, bias_qv, w_out, b_out, gain_one, shift_one, gain_two, shift_two, w_up, b_up, w_down, b_down)))

    def wrapped(*params):
        return forward(*params, pos, segment_ids, valid_mask)
    layer_out, pullback = jax.vjp(wrapped, *floats)
    gradients = pullback(cotangent.astype(jnp.float32))
    return (layer_out.astype(jnp.bfloat16), gradients[0].astype(jnp.bfloat16), gradients[1], gradients[2], gradients[3], gradients[4], gradients[5], gradients[6], gradients[7], gradients[8], gradients[9], gradients[10], gradients[11], gradients[12])
```

```python
import functools
import jax
import jax.numpy as jnp
from jax import lax
from jax.experimental import pallas as pl
from jax.experimental.pallas import tpu as pltpu
from jax.sharding import PartitionSpec as P

D = 1024
HEAD = 64
SEGS = 16
GRID = 14
GSDS = 8
EPSILON = 1e-06
MASKED = -1000000000.0
SCALE = HEAD ** (-0.5)
BQ = 128
PAIR = 2 * HEAD
F32 = jnp.float32
BF16 = jnp.bfloat16
NN = (((1,), (0,)), ((), ()))
NT = (((1,), (1,)), ((), ()))
TN = (((0,), (0,)), ((), ()))


def mm(left, right, dims=NN):
    return lax.dot_general(left, right, dims, preferred_element_type=F32)


def ratios(segment_ids, gsd_index):
    ratio_table = 2.0 ** (0.5 * jnp.arange(GSDS, dtype=jnp.float32) - 1.0)
    image_ratio = jnp.sum(
        jnp.where(gsd_index[..., None] == jnp.arange(GSDS, dtype=jnp.int32), ratio_table, 0.0),
        axis=-1,
    )
    in_image = segment_ids[..., None] == jnp.arange(SEGS, dtype=jnp.int32)
    return jnp.sum(jnp.where(in_image, image_ratio[:, None, :], 0.0), axis=-1)


def encode(patch_flat, ratio_flat):
    quarter = D // 4
    frequency = 1.0 / 10000.0 ** (jnp.arange(quarter, dtype=jnp.float32) / quarter)
    grid_row = (patch_flat // GRID).astype(jnp.float32) * ratio_flat
    grid_col = (patch_flat % GRID).astype(jnp.float32) * ratio_flat
    row_angle = grid_row[:, None] * frequency
    col_angle = grid_col[:, None] * frequency
    return jnp.concatenate(
        [jnp.sin(row_angle), jnp.cos(row_angle), jnp.sin(col_angle), jnp.cos(col_angle)], axis=-1
    )


def normalize(values):
    row_mean = jnp.mean(values, axis=-1, keepdims=True)
    centred = values - row_mean
    row_var = jnp.mean(centred * centred, axis=-1, keepdims=True)
    rstd = lax.rsqrt(row_var + EPSILON)
    return centred * rstd, rstd


def norm_back(grad, gain, xhat, rstd):
    scaled = grad * gain
    mean_scaled = jnp.mean(scaled, axis=-1, keepdims=True)
    mean_along = jnp.mean(scaled * xhat, axis=-1, keepdims=True)
    return rstd * (scaled - mean_scaled - xhat * mean_along)


def window_start(block, seq, width):
    return min(max(block * BQ - BQ, 0), seq - width)


def fill_bias(seg_q_ref, seg_k_ref, bias_ref, seq, width):
    for block in range(seq // BQ):
        start = window_start(block, seq, width)
        seg_q = seg_q_ref[block * BQ:(block + 1) * BQ, :]
        seg_k = seg_k_ref[:, start:start + width]
        row = lax.broadcasted_iota(jnp.int32, (BQ, width), 0) + block * BQ
        col = lax.broadcasted_iota(jnp.int32, (BQ, width), 1) + start
        allowed = (seg_q == seg_k) | (row == col)
        bias_ref[block] = jnp.where(allowed, 0.0, MASKED)


def split_heads(tile):
    low = lax.broadcasted_iota(jnp.int32, tile.shape, 1) < HEAD
    zero = jnp.zeros_like(tile)
    return jnp.concatenate([jnp.where(low, tile, zero), jnp.where(low, zero, tile)], axis=0)


def join_heads(stacked):
    half = stacked.shape[0] // 2
    low = lax.broadcasted_iota(jnp.int32, (half, PAIR), 1) < HEAD
    return jnp.where(low, stacked[:half], stacked[half:])


def attend_forward(seg_q_ref, seg_k_ref, x_ref, w_ref, b_ref, qkv_ref, mixed_ref, lse_ref, bias_ref):
    seq = x_ref.shape[0]
    width = bias_ref.shape[2]
    wide = w_ref.shape[2]
    fill_bias(seg_q_ref, seg_k_ref, bias_ref, seq, width)
    for c in range(3):
        for r in range(0, seq, 256):
            out = mm(x_ref[r:r + 256, :], w_ref[c])
            if c != 1:
                out = out + b_ref[c // 2:c // 2 + 1, :].astype(F32)
            qkv_ref[c, r:r + 256, :] = out.astype(BF16)
    lane = lax.broadcasted_iota(jnp.int32, (BQ, PAIR), 1)
    for block in range(seq // BQ):
        start = window_start(block, seq, width)
        rows = slice(block * BQ, (block + 1) * BQ)
        keys = slice(start, start + width)
        lse_tile = jnp.zeros((BQ, PAIR), F32)
        bias = bias_ref[block]
        bias = jnp.concatenate([bias, bias], axis=0)
        for pair in range(wide // PAIR):
            lanes = slice(pair * PAIR, (pair + 1) * PAIR)
            queries = split_heads(qkv_ref[0, rows, lanes] * SCALE)
            scores = mm(queries, qkv_ref[1, keys, lanes], NT) + bias
            row_max = jnp.max(scores, axis=-1, keepdims=True)
            weight = jnp.exp(scores - row_max)
            total = jnp.sum(weight, axis=-1, keepdims=True)
            prob = (weight * (1.0 / total)).astype(BF16)
            mixed_ref[rows, lanes] = join_heads(mm(prob, qkv_ref[2, keys, lanes])).astype(BF16)
            lse = row_max + jnp.log(total)
            lse_tile = jnp.where(lane == 2 * pair, lse[:BQ], lse_tile)
            lse_tile = jnp.where(lane == 2 * pair + 1, lse[BQ:], lse_tile)
        lse_ref[rows, :] = lse_tile


def attend_backward(
    seg_q_ref, seg_k_ref, ga_ref, w_out_ref, qkv_ref, lse_ref, out_ref, sums_ref, bias_ref, gm_ref, acc_ref
):
    seq = ga_ref.shape[0]
    width = bias_ref.shape[2]
    wide = w_out_ref.shape[0]
    fill_bias(seg_q_ref, seg_k_ref, bias_ref, seq, width)
    for r in range(0, seq, 256):
        gm_ref[r:r + 256, :] = mm(ga_ref[r:r + 256, :], w_out_ref[...], NT).astype(BF16)
    acc_ref[...] = jnp.zeros_like(acc_ref)
    for block in range(seq // BQ):
        start = window_start(block, seq, width)
        rows = slice(block * BQ, (block + 1) * BQ)
        keys = slice(start, start + width)
        bias = bias_ref[block]
        bias = jnp.concatenate([bias, bias], axis=0)
        lse_tile = lse_ref[rows, :]
        for pair in range(wide // PAIR):
            lanes = slice(pair * PAIR, (pair + 1) * PAIR)
            queries = split_heads(qkv_ref[0, rows, lanes] * SCALE)
            grad_mixed = split_heads(gm_ref[rows, lanes])
            key_rows = qkv_ref[1, keys, lanes]
            scores = mm(queries, key_rows, NT) + bias
            lse = jnp.concatenate(
                [lse_tile[:, 2 * pair:2 * pair + 1], lse_tile[:, 2 * pair + 1:2 * pair + 2]], axis=0
            )
            prob = jnp.exp(scores - lse)
            grad_prob = mm(grad_mixed, qkv_ref[2, keys, lanes], NT)
            along = jnp.sum(prob * grad_prob, axis=-1, keepdims=True)
            grad_scores = (prob * (grad_prob - along)).astype(BF16)
            out_ref[0, rows, lanes] = (join_heads(mm(grad_scores, key_rows)) * SCALE).astype(BF16)
            acc_ref[0, keys, lanes] += mm(grad_scores, queries, TN)
            acc_ref[1, keys, lanes] += mm(prob.astype(BF16), grad_mixed, TN)
    out_ref[1] = acc_ref[0].astype(BF16)
    out_ref[2] = acc_ref[1].astype(BF16)
    for at, c in enumerate((0, 2)):
        total = jnp.sum(out_ref[c].astype(F32), axis=0, keepdims=True)
        sums_ref[4 * at:4 * at + 4, :] = jnp.concatenate([total, jnp.zeros((3, wide), F32)], axis=0)


def chained(kernel, count, extra=1):
    def body(*refs):
        kernel(*refs[:count], *refs[count + extra:])

    return body


def run(kernel, name, args, outs, after, scalars=0, grid=None, in_specs=None, out_specs=None, scratch=(), aliases=None, cost=15):
    vmem = pl.BlockSpec(memory_space=pltpu.VMEM)
    if in_specs is None:
        in_specs = [pl.BlockSpec(memory_space=pltpu.SMEM)] * scalars + [vmem] * (len(args) - scalars)
    if out_specs is None:
        out_specs = [vmem] * len(outs)
    if after is not None:
        behind = list(after) if isinstance(after, (list, tuple)) else [after]
        kernel = chained(kernel, len(args), len(behind))
        args = list(args) + behind
        in_specs = list(in_specs) + [pl.BlockSpec(memory_space=pl.ANY)] * len(behind)
    result = pl.pallas_call(
        kernel,
        name=name,
        grid=grid if grid is not None else (),
        out_shape=tuple(jax.ShapeDtypeStruct(shape, dtype) for shape, dtype in outs),
        in_specs=in_specs,
        out_specs=tuple(out_specs),
        scratch_shapes=list(scratch),
        input_output_aliases=aliases or {},
        compiler_params=pltpu.CompilerParams(vmem_limit_bytes=40 * 2**20),
        cost_estimate=pl.CostEstimate(flops=cost * 10**9, bytes_accessed=10**9, transcendentals=0),
    )(*args)
    return result if len(outs) > 1 else result[0]


def forward_call(seg_q, seg_k, x, w, b, after):
    seq, wide = x.shape[0], w.shape[2]
    width = min(3 * BQ, seq)
    return run(
        attend_forward,
        "attend_forward",
        [seg_q, seg_k, x, w, b],
        [((3, seq, wide), BF16), ((seq, wide), BF16), ((seq, PAIR), F32)],
        after,
        scratch=[pltpu.VMEM((seq // BQ, BQ, width), F32)],
    )


def backward_call(seg_q, seg_k, ga, w_out, qkv, lse, after):
    seq, wide = ga.shape[0], w_out.shape[0]
    width = min(3 * BQ, seq)
    return run(
        attend_backward,
        "attend_backward",
        [seg_q, seg_k, ga, w_out, qkv, lse],
        [((3, seq, wide), BF16), ((8, wide), F32)],
        after,
        scratch=[
            pltpu.VMEM((seq // BQ, BQ, width), F32),
            pltpu.VMEM((seq, wide), BF16),
            pltpu.VMEM((2, seq, wide), F32),
        ],
    )


def eight(values):
    return jnp.sum(values.reshape(values.shape[0] // 8, 8, values.shape[1]), axis=0)


def project_out(flip, core_ref, mixed_a_ref, mixed_b_ref, w_a_ref, w_b_ref, out_ref):
    rows = out_ref.shape[0]
    at = pl.ds(pl.multiple_of(jnp.bitwise_xor(core_ref[0], flip) * rows, rows), rows)
    out = mm(mixed_a_ref[at, :], w_a_ref[...]) + mm(mixed_b_ref[at, :], w_b_ref[...])
    out_ref[...] = out.astype(out_ref.dtype)


def second_norm(start_ref, own_ref, near_ref, b_ref, gain_ref, shift_ref, after_ref, n2_ref):
    value = start_ref[...] + (own_ref[...] + near_ref[...].astype(F32)) + b_ref[...]
    after_ref[...] = value
    xhat, _ = normalize(value)
    n2_ref[...] = (xhat * gain_ref[...] + shift_ref[...]).astype(BF16)


def second_norm_back(here_ref, near_ref, far_ref, after_ref, cot_ref, ok_ref, gain_ref, mid_ref, ga_ref, sums_ref):
    @pl.when(pl.program_id(0) == 0)
    def _():
        sums_ref[...] = jnp.zeros_like(sums_ref)

    grad = here_ref[...].astype(F32) + near_ref[...].astype(F32) + far_ref[...].astype(F32)
    xhat, rstd = normalize(after_ref[...])
    grad_after = cot_ref[...].astype(F32) * ok_ref[...]
    mid = grad_after + norm_back(grad, gain_ref[...], xhat, rstd)
    mid_ref[...] = mid
    ga_ref[...] = mid.astype(BF16)
    sums_ref[0] += eight(mid)
    sums_ref[1] += eight(grad * xhat)
    sums_ref[2] += eight(grad)
    sums_ref[3] += eight(grad_after)


def first_norm_back(own_ref, near_ref, start_ref, mid_ref, gain_ref, out_ref, sums_ref):
    @pl.when(pl.program_id(0) == 0)
    def _():
        sums_ref[...] = jnp.zeros_like(sums_ref)

    grad = own_ref[...] + near_ref[...].astype(F32)
    xhat, rstd = normalize(start_ref[...])
    out_ref[...] = (mid_ref[...] + norm_back(grad, gain_ref[...], xhat, rstd)).astype(BF16)
    sums_ref[0] += eight(grad * xhat)
    sums_ref[1] += eight(grad)


def down_out(act_n_ref, act_c_ref, w_ref, out_ref):
    out_ref[0] = mm(act_n_ref[...], w_ref[...]).astype(BF16)
    out_ref[1] = mm(act_c_ref[...], w_ref[...]).astype(BF16)


def down_in(act_o_ref, act_f_ref, after_ref, got_ref, b_ref, w_ref, base_ref, far_ref):
    down = mm(act_o_ref[...], w_ref[...]) + got_ref[0].astype(F32)
    base_ref[...] = after_ref[...] + down + b_ref[...]
    far_ref[...] = (mm(act_f_ref[...], w_ref[...]) + got_ref[1].astype(F32)).astype(BF16)


def finish(base_ref, far_ref, ok_ref, out_ref):
    out_ref[...] = ((base_ref[...] + far_ref[...].astype(F32)) * ok_ref[...]).astype(BF16)


def hand_on(in_ref, out_ref):
    out_ref[...] = in_ref[...]


def hand_on_all(*refs):
    count = len(refs) // 2
    for in_ref, out_ref in zip(refs[:count], refs[count:]):
        out_ref[...] = in_ref[...]


def handed(value, after):
    return run(hand_on, "hand_on", [value], [(value.shape, value.dtype)], after)


def small_first(two_ref, one_ref, out_ref):
    out_ref[...] = jnp.zeros_like(out_ref)
    rows = [two_ref[0], one_ref[0], one_ref[1], two_ref[1], two_ref[2], two_ref[3]]
    for at, part in enumerate(rows):
        out_ref[at:at + 1, :] = jnp.sum(part, axis=0, keepdims=True)


def small_second(own_ref, near_ref, bias_a_ref, bias_b_ref, send_ref, keep_ref):
    total = own_ref[...] + near_ref[...]
    wide = bias_a_ref.shape[1]
    for out_ref, bias_ref in ((send_ref, bias_b_ref), (keep_ref, bias_a_ref)):
        out_ref[...] = total
        out_ref[6:7, :wide] = bias_ref[0:1, :]
        out_ref[6:7, wide:2 * wide] = bias_ref[4:5, :]


def small_third(own_ref, far_ref, *refs):
    out_ref = refs[-1]
    out_ref[...] = own_ref[...] + far_ref[...]
    out_ref[7:8, :] = sum(jnp.sum(part[...], axis=0, keepdims=True) for part in refs[:-1])


def small_add(own_ref, far_ref, out_ref):
    out_ref[...] = own_ref[...] + far_ref[...]


def add_two(left_ref, right_ref, out_ref):
    out_ref[...] = add_low(left_ref[...], right_ref[...])


def token_products(count, based, side_ref, *refs):
    lefts, rights, rest = refs[:count], refs[count:2 * count], refs[2 * count:]
    total = sum(mm(left[...], right[...], TN) for left, right in zip(lefts, rights))
    if not based:
        rest[-1][...] = total
        return
    total = (total + rest[0][...]).astype(BF16)
    send_ref, keep_ref = rest[-2:]
    first = pl.program_id(0) < pl.num_programs(0) // 2

    @pl.when(first)
    def _():
        send_ref[...] = total

    @pl.when(jnp.logical_not(first))
    def _():
        keep_ref[...] = total


def token_call(sides, lefts, rights, base, after):
    tall, wide = lefts[0].shape[1], rights[0].shape[1]
    block = 256
    steps = tall // block

    def row(i, side_ref):
        return jnp.where(i < steps // 2, i + (1 - side_ref[0]) * (steps // 2), i - (1 - side_ref[0]) * (steps // 2))

    if base is None:
        outs = jax.ShapeDtypeStruct((tall, wide), F32)
        out_specs = pl.BlockSpec((block, wide), lambda i, side_ref: (row(i, side_ref), 0))
    else:
        outs = [jax.ShapeDtypeStruct((tall // 2, wide), BF16)] * 2
        out_specs = [
            pl.BlockSpec((block, wide), lambda i, _: (jnp.minimum(i, steps // 2 - 1), 0)),
            pl.BlockSpec((block, wide), lambda i, _: (jnp.maximum(i - steps // 2, 0), 0)),
        ]
    in_specs = [pl.BlockSpec((left.shape[0], block), lambda i, side_ref: (0, row(i, side_ref))) for left in lefts]
    in_specs += [pl.BlockSpec(right.shape, lambda i, _: (0, 0)) for right in rights]
    args = list(lefts) + list(rights)
    if base is not None:
        in_specs.append(pl.BlockSpec((block, wide), lambda i, side_ref: (row(i, side_ref), 0)))
        args.append(base)
    kernel = functools.partial(token_products, len(lefts), base is not None)
    return pl.pallas_call(
        chained(kernel, len(args) + 1),
        name="token_products",
        grid_spec=pltpu.PrefetchScalarGridSpec(
            num_scalar_prefetch=1,
            grid=(steps,),
            in_specs=in_specs + [pl.BlockSpec(memory_space=pl.ANY)],
            out_specs=out_specs,
        ),
        out_shape=outs,
        compiler_params=pltpu.CompilerParams(vmem_limit_bytes=40 * 2**20),
        cost_estimate=pl.CostEstimate(flops=60 * 10**9, bytes_accessed=10**9, transcendentals=0),
    )(sides, *args, after)


def three_products(x_ref, gp_ref, q_ref, kv_ref):
    q_ref[...] = mm(x_ref[...], gp_ref[0]).astype(BF16)
    for c in range(2):
        kv_ref[c] = mm(x_ref[...], gp_ref[c + 1]).astype(BF16)


def three_call(x_turned, gp, after):
    tall, seq = x_turned.shape
    wide = gp.shape[2]
    block = 256
    return run(
        three_products,
        "three_products",
        [x_turned, gp],
        [((tall, wide), BF16), ((2, tall, wide), BF16)],
        after,
        grid=(tall // block,),
        in_specs=[pl.BlockSpec((block, seq), lambda i: (i, 0)), pl.BlockSpec(gp.shape, lambda i: (0, 0, 0))],
        out_specs=[
            pl.BlockSpec((block, wide), lambda i: (i, 0)),
            pl.BlockSpec((2, block, wide), lambda i: (0, i, 0)),
        ],
    )


def turned_product(mixed_ref, ga_ref, out_ref):
    out_ref[...] = mm(ga_ref[...], mixed_ref[...], TN).astype(BF16)


def back_project(flip, core_ref, gp_a_ref, gp_b_ref, w_a_ref, w_b_ref, out_ref):
    rows = out_ref.shape[0]
    at = pl.ds(pl.multiple_of(jnp.bitwise_xor(core_ref[0], flip) * rows, rows), rows)
    out = sum(
        mm(gp_ref[c, at, :], w_ref[c], NT)
        for c in range(3)
        for gp_ref, w_ref in ((gp_a_ref, w_a_ref), (gp_b_ref, w_b_ref))
    )
    out_ref[...] = out.astype(out_ref.dtype)


def by_rows(kernel, name, args, outs, after, block=128):
    rows = args[0].shape[0]

    def spec(shape):
        if shape[0] == rows:
            return pl.BlockSpec((block,) + tuple(shape[1:]), lambda i: (i,) + (0,) * (len(shape) - 1))
        return pl.BlockSpec(tuple(shape), lambda i: (0,) * len(shape))

    return run(
        kernel,
        name,
        args,
        outs,
        after,
        grid=(rows // block,),
        in_specs=[spec(arg.shape) for arg in args],
        out_specs=[spec(shape) for shape, _ in outs],
    )


def fold(bit, last, side_ref, cur_ref, got_ref, *out_refs):
    if last:
        out_refs[0][...] = add_low(cur_ref[...], got_ref[...])
        return
    half = got_ref.shape[0] // 2
    for side, out_ref in ((1 - side_ref[bit], out_refs[0]), (side_ref[bit], out_refs[1])):
        at = pl.ds(pl.multiple_of(side * half, half), half)
        out_ref[...] = add_low(cur_ref[at, :], got_ref[at, :])


def begin_pair(paired, side_ref, *refs):
    send_ref, keep_ref = refs[-2:]
    if paired:
        parts = [(refs[0].at[c], refs[1].at[c]) for c in range(2)]
    else:
        parts = [refs[0:2], refs[2:4]]
    for side in range(2):

        @pl.when(side_ref[0] == side)
        def _():
            send_ref[...] = add_low(parts[1 - side][0][...], parts[1 - side][1][...])
            keep_ref[...] = add_low(parts[side][0][...], parts[side][1][...])


def join(left_ref, right_ref, out_ref):
    rows = left_ref.shape[0]
    out_ref[:rows, :] = left_ref[...]
    out_ref[rows:, :] = right_ref[...]


def place(piece, spot_ref, own_ref, other_ref, out_ref):
    count = own_ref.shape[0] // piece
    steps = out_ref.shape[0] // piece
    for at in range(steps):
        apart = jnp.bitwise_xor(pl.program_id(0) * steps + at, spot_ref[0])
        rows = pl.ds(pl.multiple_of(jnp.bitwise_and(apart, count - 1) * piece, piece), piece)
        far_side = apart >= count
        into = slice(at * piece, (at + 1) * piece)

        @pl.when(far_side)
        def _():
            out_ref[into, :] = other_ref[rows, :].astype(F32)

        @pl.when(jnp.logical_not(far_side))
        def _():
            out_ref[into, :] = own_ref[rows, :].astype(F32)


def pieces(count, spot, own_ref, other_ref, first, steps):
    piece = own_ref.shape[0] // count
    for at in range(steps):
        apart = jnp.bitwise_xor(first + at, spot)
        rows = pl.ds(pl.multiple_of(jnp.bitwise_and(apart, count - 1) * piece, piece), piece)
        mine, others = own_ref[rows, :].astype(F32), other_ref[rows, :].astype(F32)
        yield at * piece, piece, jnp.where(apart >= count, others, mine)


def place_turned(count, spot_ref, own_ref, other_ref, w_out_ref, part_ref):
    for at, piece, value in pieces(count, spot_ref[0], own_ref, other_ref, 0, count):
        w_out_ref[:, at:at + piece] = value.T
    for at, piece, value in pieces(count, spot_ref[0], own_ref, other_ref, count, count):
        part_ref[at:at + piece, :] = value


def place_two(count, spot_ref, own_ref, other_ref, _, out_ref):
    for at, piece, value in pieces(count, spot_ref[0], own_ref, other_ref, pl.program_id(0) * count, count):
        out_ref[at:at + piece, :] = value


class Sum:
    def __init__(self, size, height):
        self.size, self.bits, self.height = size, size.bit_length() - 1, height
        me = lax.axis_index("dp")
        sides = [(me // (1 << b)) % 2 for b in range(self.bits)]
        self.sides = jnp.stack(sides).astype(jnp.int32)
        self.spot = sum(side << (self.bits - 1 - b) for b, side in enumerate(sides))

    def begin(self, send, keep):
        self.keep, self.step = keep, 0
        self.sent = swap(send, "dp", self.size, 1)

    def begin_pairs(self, arrays, after):
        shape = arrays[0].shape[-2:]
        send, keep = run(
            functools.partial(begin_pair, len(arrays) == 2), "begin_pair", [self.sides] + list(arrays),
            [(shape, BF16)] * 2, after, scalars=1,
        )
        self.begin(send, keep)
        return keep

    def fold(self, after):
        if self.step >= self.bits:
            return after
        self.step += 1
        last = self.step == self.bits
        rows, columns = self.sent.shape
        kernel = functools.partial(fold, self.step, last)
        outs = [((rows, columns), BF16)] if last else [((rows // 2, columns), BF16)] * 2
        out = run(kernel, "fold", [self.sides, self.keep, self.sent], outs, after, scalars=1)
        self.keep = out if last else out[1]
        send = out if last else out[0]
        self.sent = swap(send, "dp", self.size, 1 << min(self.step, self.bits - 1))
        return self.keep

    def spread(self, after):
        if self.step < self.bits:
            return after
        bit = 2 * self.bits - 2 - self.step
        rows, columns = self.keep.shape
        self.keep = run(join, "join", [self.keep, self.sent], [((2 * rows, columns), BF16)], after)
        self.sent = swap(self.keep, "dp", self.size, 1 << bit)
        self.step += 1
        return self.keep

    def complete(self, after):
        while self.step < self.bits:
            after = self.fold(after)
        while self.step < 2 * self.bits - 1:
            after = self.spread(after)
        return after

    def place(self, after):
        after = self.complete(after)
        rows, columns = self.keep.shape
        piece = rows * 2 // self.size
        return run(
            functools.partial(place, piece),
            "place",
            [self.spot.reshape(1).astype(jnp.int32), self.keep, self.sent],
            [((2 * rows, columns), F32)],
            after,
            grid=(2,),
            in_specs=[
                pl.BlockSpec(memory_space=pltpu.SMEM),
                pl.BlockSpec((rows, columns), lambda i: (0, 0)),
                pl.BlockSpec((rows, columns), lambda i: (0, 0)),
            ],
            out_specs=[pl.BlockSpec((rows, columns), lambda i: (i, 0))],
        )[: self.height]

    def place_out(self, after):
        after = self.complete(after)
        rows, columns = self.keep.shape
        return run(
            functools.partial(place_turned, self.size // 2),
            "place_turned",
            [self.spot.reshape(1).astype(jnp.int32), self.keep, self.sent],
            [((columns, rows), F32), ((3 * rows, columns), F32)],
            after,
            grid=(1,),
            in_specs=[pl.BlockSpec(memory_space=pltpu.SMEM)]
            + [pl.BlockSpec((rows, columns), lambda i: (0, 0))] * 2,
            out_specs=[
                pl.BlockSpec((columns, rows), lambda i: (0, 0)),
                pl.BlockSpec((rows, columns), lambda i: (0, 0)),
            ],
        )

    def place_rest(self, into, after):
        after = self.complete(after)
        rows, columns = self.keep.shape
        return run(
            functools.partial(place_two, self.size // 2),
            "place_two",
            [self.spot.reshape(1).astype(jnp.int32), self.keep, self.sent, into],
            [((3 * rows, columns), F32)],
            after,
            grid=(2,),
            in_specs=[pl.BlockSpec(memory_space=pltpu.SMEM)]
            + [pl.BlockSpec((rows, columns), lambda i: (0, 0))] * 2
            + [pl.BlockSpec(memory_space=pl.ANY)],
            out_specs=[pl.BlockSpec((rows, columns), lambda i: (i + 1, 0))],
            aliases={3: 0},
        )


def gelu_and_slope(up):
    size = jnp.abs(up)
    t = 1.0 / (1.0 + (0.3275911 * 0.7071067811865476) * size)
    bell = jnp.exp(-0.5 * up * up)
    poly = t * (
        0.5 * 0.254829592
        + t * (0.5 * -0.284496736 + t * (0.5 * 1.421413741 + t * (0.5 * -1.453152027 + t * (0.5 * 1.061405429))))
    )
    tail = poly * bell
    cdf = jnp.where(up >= 0.0, 1.0 - tail, tail)
    return up * cdf, cdf + up * bell * 0.3989422804014327


def feed(n2_ref, gd_ref, ok_ref, w_up_ref, b_up_ref, w_down_ref, gn2_ref, act_ref, gup_ref, gb_ref):
    hidden = w_up_ref.shape[1]
    rows = n2_ref.shape[0]
    step = 256
    n2 = n2_ref[...]
    gd = gd_ref[...]
    ok = ok_ref[...]

    @pl.when(pl.program_id(0) == 0)
    def _():
        gb_ref[...] = jnp.zeros_like(gb_ref)

    for at in range(0, hidden, step):
        part = slice(at, at + step)
        up = mm(n2, w_up_ref[:, part]) + b_up_ref[:, part]
        grad_act = mm(gd, w_down_ref[part, :], NT)
        act, slope = gelu_and_slope(up)
        grad_up = (slope * (grad_act * ok)).astype(BF16)
        act_ref[:, part] = (act * ok).astype(BF16)
        gup_ref[:, part] = grad_up
        gb_ref[:, part] += jnp.sum(grad_up.astype(F32).reshape(rows // 8, 8, step), axis=0)
    gn2_ref[...] = mm(gup_ref[...], w_up_ref[...], NT).astype(BF16)


def feed_call(n2, gd, ok, w_up, b_up, w_down, after):
    rows, hidden = n2.shape[0], w_up.shape[1]
    block = 256
    tokens = pl.BlockSpec((block, D), lambda i: (i, 0))
    tall = pl.BlockSpec((block, hidden), lambda i: (i, 0))

    def fixed(shape):
        return pl.BlockSpec(shape, lambda i: (0, 0))

    return run(
        feed,
        "feed",
        [n2, gd, ok, w_up, b_up, w_down],
        [((rows, D), BF16), ((rows, hidden), BF16), ((rows, hidden), BF16), ((8, hidden), F32)],
        after,
        grid=(rows // block,),
        in_specs=[tokens, tokens, pl.BlockSpec((block, 1), lambda i: (i, 0)), fixed((D, hidden)), fixed((1, hidden)), fixed((hidden, D))],
        out_specs=[tokens, tall, tall, fixed((8, hidden))],
    )


def swap(value, axis, size, flip):
    return lax.ppermute(value, axis, [(i, i ^ flip) for i in range(size)])


def add_low(left, right):
    return (left.astype(F32) + right.astype(F32)).astype(BF16)


def sum_over(value, axis, size):
    flip = 1
    while flip < size:
        value = value + swap(value, axis, size, flip)
        flip *= 2
    return value


def on_device(
    dp_size,
    mp_size,
    tokens,
    segment_ids,
    valid_mask,
    patch_index,
    gsd_index,
    w_qkv,
    bias_qv,
    w_out,
    b_out,
    gain_one,
    shift_one,
    gain_two,
    shift_two,
    w_up,
    b_up,
    w_down,
    b_down,
    cotangent,
):
    own_rows = tokens.shape[0]
    mp = lax.axis_index("mp")
    core = mp % 2
    row = mp // 2

    def near(value):
        return swap(value, "mp", mp_size, 1)

    def far(value):
        return swap(value, "mp", mp_size, 2)

    def in_order(own, other):
        return jnp.where(core == 0, jnp.concatenate([own, other]), jnp.concatenate([other, own]))

    far_bias = far(bias_qv)
    far_qkv = far(w_qkv)
    cot_near = near(cotangent)

    inputs = [tokens, segment_ids, valid_mask, patch_index, gsd_index]
    tokens, segment_ids, valid_mask, patch_index, gsd_index = run(
        hand_on_all, "hand_on_all", inputs, [(part.shape, part.dtype) for part in inputs], cot_near
    )
    ratio_flat = ratios(segment_ids, gsd_index).reshape(-1)
    own_start = mp * own_rows
    own_ratio = lax.dynamic_slice_in_dim(ratio_flat, own_start, own_rows)
    own_patch = lax.dynamic_slice_in_dim(patch_index.reshape(-1), own_start, own_rows)
    all_valid = valid_mask.reshape(-1, 1).astype(F32)

    def valid_of(flip):
        at = jnp.bitwise_xor(mp, flip) * own_rows
        return lax.dynamic_slice_in_dim(all_valid, at, own_rows)

    own_valid = valid_of(0)
    gain_first, shift_first = gain_one.astype(F32), shift_one.astype(F32)
    gain_second, shift_second = gain_two.astype(F32), shift_two.astype(F32)

    row_seg = lax.dynamic_index_in_dim(segment_ids, row, 0, keepdims=True)
    row_ok = lax.dynamic_index_in_dim(valid_mask, row, 0, keepdims=True)
    seg_k = jnp.where(row_ok == 1, row_seg, -1)
    seg_q = row_seg.reshape(-1, 1)

    start_sum = tokens.astype(F32) + encode(own_patch, own_ratio)
    xhat_one, _ = normalize(start_sum)
    normed = (xhat_one * gain_first + shift_first).astype(BF16)
    w_out_sent, cot_sent = run(
        hand_on_all, "hand_on_all", [w_out, cotangent], [(w_out.shape, BF16), (cotangent.shape, BF16)], normed, cost=60
    )
    normed_row = in_order(normed, near(normed))

    x_turned = normed_row.T
    core_s = core.reshape(1).astype(jnp.int32)
    half = (own_rows, D)
    down_sum, up_sum = Sum(dp_size, w_down.shape[0]), Sum(dp_size, w_up.shape[0])
    first_sum, second_sum = Sum(dp_size, 2 * D), Sum(dp_size, 2 * D)
    sides = down_sum.sides

    qkv_a, mixed_a, lse_a = forward_call(seg_q, seg_k, normed_row, w_qkv, bias_qv, cot_sent)
    far_out, cot_far = far(w_out_sent), far(cot_sent)
    qkv_b, mixed_b, lse_b = forward_call(seg_q, seg_k, normed_row, far_qkv, far_bias, [lse_a, x_turned])
    operands = [core_s, mixed_a, mixed_b, w_out, far_out]
    attn_near = run(functools.partial(project_out, 1), "project_out", operands, [(half, BF16)], lse_b, scalars=1)
    attn_own = run(functools.partial(project_out, 0), "project_out", operands, [(half, F32)], attn_near, scalars=1)
    after_attn, n2 = by_rows(
        second_norm, "second_norm",
        [start_sum, attn_own, near(attn_near), b_out.astype(F32)[None], gain_second[None], shift_second[None]],
        [(half, F32), (half, BF16)], attn_own,
    )
    n2_far = far(n2)
    n2_near = near(n2)

    b_up_row = b_up.astype(F32)[None, :]
    gn2_o, act_o, gup_o, gb_o = feed_call(n2, cotangent, own_valid, w_up, b_up_row, w_down, n2)
    gn2_n, act_n, gup_n, gb_n = feed_call(n2_near, cot_near, valid_of(1), w_up, b_up_row, w_down, gb_o)
    from_near = near(gn2_n)
    down_here = token_call(sides, (act_o, act_n), (cotangent, cot_near), None, gb_n)
    cot_pass = handed(cot_far, [down_here, from_near])
    cot_cross = near(cot_pass)
    up_here = token_call(sides, (n2, n2_near), (gup_o, gup_n), None, cot_pass)
    n2_pass = handed(n2_far, up_here)
    n2_cross = near(n2_pass)
    gn2_f, act_f, gup_f, gb_f = feed_call(n2_pass, cot_pass, valid_of(2), w_up, b_up_row, w_down, n2_pass)
    gn2_c, act_c, gup_c, gb_c = feed_call(n2_cross, cot_cross, valid_of(3), w_up, b_up_row, w_down, gb_f)
    cross_gn2 = near(gn2_c)
    down_send, down_keep = token_call(sides, (act_f, act_c), (cot_pass, cot_cross), down_here, gb_c)
    down_sum.begin(down_send, down_keep)
    to_far = by_rows(add_two, "add_two", [gn2_f, cross_gn2], [(half, BF16)], down_keep)
    from_far = far(to_far)
    down_sent = run(down_out, "down_out", [act_n, act_c, w_down], [((2,) + half, BF16)], to_far)
    up_send, up_keep = token_call(sides, (n2_pass, n2_cross), (gup_f, gup_c), up_here, down_sent)
    up_sum.begin(up_send, up_keep)

    down_base, down_far = run(
        down_in, "down_in",
        [act_o, act_f, after_attn, near(down_sent), b_down.astype(F32)[None], w_down],
        [(half, F32), (half, BF16)], up_keep,
    )
    mid, ga, sums_two = by_rows(
        second_norm_back, "second_norm_back",
        [gn2_o, from_near, from_far, after_attn, cotangent, own_valid, gain_second[None]],
        [(half, F32), (half, BF16), ((4, 8, D), F32)], down_base,
    )
    last = down_sum.fold(ga)
    ga_row = in_order(ga, near(ga))
    wide = w_qkv.shape[2]
    turned = [((D, wide), BF16)]
    gw_out_b = run(turned_product, "turned_product", [mixed_b, ga_row], turned, last)
    far_out_grad = far(gw_out_b)
    gp_b, bias_b = backward_call(seg_q, seg_k, ga_row, far_out, qkv_b, lse_b, gw_out_b)
    q_b, kv_b = three_call(x_turned, gp_b, bias_b)
    far_q, far_kv = far(q_b), far(kv_b)
    last = up_sum.fold(q_b)
    last = down_sum.fold(last)
    gp_a, bias_a = backward_call(seg_q, seg_k, ga_row, w_out, qkv_a, lse_a, last)
    last = down_sum.fold(bias_a)
    last = up_sum.fold(last)
    gw_out_a = run(turned_product, "turned_product", [mixed_a, ga_row], turned, last)
    q_a, kv_a = three_call(x_turned, gp_a, gw_out_a)
    last = first_sum.begin_pairs([gw_out_a, far_out_grad, q_a, far_q], q_a)
    operands = [core_s, gp_a, gp_b, w_qkv, far_qkv]
    gn_near = run(functools.partial(back_project, 1), "back_project", operands, [(half, BF16)], last, scalars=1)
    gn_own = run(functools.partial(back_project, 0), "back_project", operands, [(half, F32)], gn_near, scalars=1)
    last = down_sum.spread(gn_own)
    last = up_sum.fold(last)
    last = second_sum.begin_pairs([kv_a, far_kv], last)
    last = first_sum.fold(last)
    grad_tokens, sums_one = by_rows(
        first_norm_back, "first_norm_back",
        [gn_own, near(gn_near), start_sum, mid, gain_first[None]],
        [(half, BF16), ((2, 8, D), F32)], last,
    )
    down_got = far(handed(down_far, sums_one))
    tile = [((8, D), F32)]
    small = run(small_first, "small_first", [sums_two, sums_one], tile, sums_one)
    small_got = near(small)
    last = down_sum.spread(small)
    last = up_sum.spread(last)
    last = first_sum.fold(last)
    last = second_sum.fold(last)
    send, small = run(small_second, "small_second", [small, small_got, bias_a, bias_b], tile * 2, last)
    small_got = far(send)
    last = first_sum.fold(small)
    last = second_sum.fold(last)
    layer_out = by_rows(finish, "finish", [down_base, down_got, own_valid], [(half, BF16)], last)
    small = run(small_third, "small_third", [small, small_got, gb_o, gb_n, gb_f, gb_c], tile, layer_out)
    flips = [1 << b for b in range(dp_size.bit_length() - 1)]
    small_got = swap(small, "dp", dp_size, flips[0])
    last = up_sum.spread(small)
    last = first_sum.spread(last)
    last = second_sum.fold(last)
    small = run(small_add, "small_add", [small, small_got], tile, last)
    small_got = swap(small, "dp", dp_size, flips[1])
    last = first_sum.spread(small)
    last = second_sum.spread(last)
    grad_w_down = down_sum.place(last)
    small = run(small_add, "small_add", [small, small_got], tile, grad_w_down)
    small_got = swap(small, "dp", dp_size, flips[2])
    last = second_sum.spread(small)
    grad_w_up = up_sum.place(last)
    for flip in flips[3:]:
        small = run(small_add, "small_add", [small, small_got], tile, grad_w_up)
        small_got = swap(small, "dp", dp_size, flip)
    small = run(small_add, "small_add", [small, small_got], tile, grad_w_up)
    grad_w_out, grad_w_qkv = first_sum.place_out(small)
    grad_w_qkv = second_sum.place_rest(grad_w_qkv, grad_w_out).reshape(w_qkv.shape)
    grad_bias_qv = small[6, : 2 * wide].reshape(2, wide)
    grad_b_up = small[7]
    return (
        layer_out,
        grad_tokens,
        grad_w_qkv,
        grad_bias_qv,
        grad_w_out,
        small[0],
        small[1],
        small[2],
        small[3],
        small[4],
        grad_w_up,
        grad_b_up,
        grad_w_down,
        small[5],
    )


def solution(mesh):
    return jax.shard_map(
        functools.partial(on_device, mesh.shape["dp"], mesh.shape["mp"]),
        mesh=mesh,
        in_specs=(
            P(("dp", "mp"), None),
            P("dp", None),
            P("dp", None),
            P("dp", None),
            P("dp", None),
            P(None, None, "mp"),
            P(None, "mp"),
            P("mp", None),
            P(),
            P(),
            P(),
            P(),
            P(),
            P(None, "mp"),
            P("mp"),
            P("mp", None),
            P(),
            P(("dp", "mp"), None),
        ),
        out_specs=(
            P(("dp", "mp"), None),
            P(("dp", "mp"), None),
            P(None, None, "mp"),
            P(None, "mp"),
            P("mp", None),
            P(),
            P(),
            P(),
            P(),
            P(),
            P(None, "mp"),
            P("mp"),
            P("mp", None),
            P(),
        ),
        check_vma=False,
    )
```

```python
import functools
import jax
import jax.numpy as jnp
from jax import lax
from jax.experimental import pallas as pl
from jax.experimental.pallas import tpu as pltpu
from jax.sharding import PartitionSpec as P

D = 1024
HEAD = 64
SEGS = 16
GRID = 14
GSDS = 8
EPSILON = 1e-06
MASKED = -1000000000.0
SCALE = HEAD ** (-0.5)
BQ = 128
PAIR = 2 * HEAD
F32 = jnp.float32
BF16 = jnp.bfloat16
NN = (((1,), (0,)), ((), ()))
NT = (((1,), (1,)), ((), ()))
TN = (((0,), (0,)), ((), ()))


def mm(left, right, dims=NN):
    return lax.dot_general(left, right, dims, preferred_element_type=F32)


def image_levels(segment_ids, gsd_index):
    in_image = segment_ids[..., None] == jnp.arange(SEGS, dtype=jnp.int32)
    return jnp.sum(jnp.where(in_image, gsd_index[:, None, :], 0), axis=-1)


def code_table():
    quarter = D // 4
    frequency = 1.0 / 10000.0 ** (jnp.arange(quarter, dtype=jnp.float32) / quarter)
    ratio = 2.0 ** (0.5 * jnp.arange(GSDS, dtype=jnp.float32) - 1.0)
    place = jnp.arange(16, dtype=jnp.float32)
    angle = (place[:, None] * ratio[None, :]).reshape(-1, 1) * frequency
    return jnp.concatenate([jnp.sin(angle), jnp.cos(angle)], axis=-1)


def front(tokens_ref, row_ref, col_ref, table_ref, gain_ref, shift_ref, start_ref, normed_ref):
    high = table_ref[...].astype(BF16)
    rest = table_ref[...] - high.astype(F32)
    middle = rest.astype(BF16)
    low = (rest - middle.astype(F32)).astype(BF16)
    spots = lax.broadcasted_iota(jnp.int32, (tokens_ref.shape[0], table_ref.shape[0]), 1)
    half = table_ref.shape[1]
    for at, index_ref in ((0, row_ref), (half, col_ref)):
        chosen = (spots == index_ref[...]).astype(F32).astype(BF16)
        code = (mm(chosen, low) + mm(chosen, middle)) + mm(chosen, high)
        start_ref[:, at:at + half] = tokens_ref[:, at:at + half].astype(F32) + code
    xhat, _ = normalize(start_ref[...])
    normed_ref[...] = (xhat * gain_ref[...].astype(F32) + shift_ref[...].astype(F32)).astype(BF16)


def normalize(values):
    row_mean = jnp.mean(values, axis=-1, keepdims=True)
    centred = values - row_mean
    row_var = jnp.mean(centred * centred, axis=-1, keepdims=True)
    rstd = lax.rsqrt(row_var + EPSILON)
    return centred * rstd, rstd


def norm_back(grad, gain, xhat, rstd):
    scaled = grad * gain
    mean_scaled = jnp.mean(scaled, axis=-1, keepdims=True)
    mean_along = jnp.mean(scaled * xhat, axis=-1, keepdims=True)
    return rstd * (scaled - mean_scaled - xhat * mean_along)


def window_start(block, seq, width):
    return min(max(block * BQ - BQ, 0), seq - width)


def fill_bias(seg_q_ref, seg_k_ref, bias_ref, seq, width):
    for block in range(seq // BQ):
        start = window_start(block, seq, width)
        seg_q = seg_q_ref[block * BQ:(block + 1) * BQ, :]
        seg_k = seg_k_ref[:, start:start + width]
        row = lax.broadcasted_iota(jnp.int32, (BQ, width), 0) + block * BQ
        col = lax.broadcasted_iota(jnp.int32, (BQ, width), 1) + start
        allowed = (seg_q == seg_k) | (row == col)
        bias_ref[block] = jnp.where(allowed, 0.0, MASKED)


def split_heads(tile):
    low = lax.broadcasted_iota(jnp.int32, tile.shape, 1) < HEAD
    zero = jnp.zeros_like(tile)
    return jnp.concatenate([jnp.where(low, tile, zero), jnp.where(low, zero, tile)], axis=0)


def join_heads(stacked):
    half = stacked.shape[0] // 2
    low = lax.broadcasted_iota(jnp.int32, (half, PAIR), 1) < HEAD
    return jnp.where(low, stacked[:half], stacked[half:])


def piece_places(side_ref, w_refs, depth):
    if len(w_refs) == 1:
        return [(slice(None), w_refs[0])]
    rows = depth // 4
    starts = [side_ref[0] * 2, side_ref[0] * 2 + 1, (1 - side_ref[0]) * 2, (1 - side_ref[0]) * 2 + 1]
    return [(pl.ds(pl.multiple_of(at * rows, rows), rows), w_ref) for at, w_ref in zip(starts, w_refs)]


def assemble(side_ref, *refs):
    out_ref = refs[-1]
    for at, w_ref in piece_places(side_ref, refs[:-1], out_ref.shape[1]):
        out_ref[:, at, :] = w_ref[...]


def turn(in_ref, out_ref):
    out_ref[...] = in_ref[...].T


def cut(side_ref, w_ref, *refs):
    extra = len(refs) // 2 - 1
    rows = w_ref.shape[1] // 4
    for piece in range(2):
        at = pl.ds(pl.multiple_of((side_ref[0] * 2 + piece) * rows, rows), rows)
        refs[extra + piece][...] = w_ref[:, at, :]
    for in_ref, out_ref in zip(refs[:extra], refs[extra + 2:]):
        out_ref[...] = in_ref[...]


def in_row(core_ref, own_ref, other_ref, out_ref):
    rows = own_ref.shape[0]
    for side, in_ref in ((core_ref[0], own_ref), (1 - core_ref[0], other_ref)):
        out_ref[pl.ds(pl.multiple_of(side * rows, rows), rows), :] = in_ref[...]


def attend_forward(side_ref, seg_q_ref, seg_k_ref, x_ref, b_ref, *refs):
    w_refs, (qkv_ref, mixed_ref, lse_ref, bias_ref) = refs[:-4], refs[-4:]
    seq = x_ref.shape[0]
    width = bias_ref.shape[2]
    wide = w_refs[0].shape[2]
    fill_bias(seg_q_ref, seg_k_ref, bias_ref, seq, width)
    for c in range(3):
        for r in range(0, seq, 256):
            out = sum(
                mm(x_ref[r:r + 256, at], w_ref[c]) for at, w_ref in piece_places(side_ref, w_refs, x_ref.shape[1])
            )
            if c != 1:
                out = out + b_ref[c // 2:c // 2 + 1, :].astype(F32)
            qkv_ref[c, r:r + 256, :] = out.astype(BF16)
    lane = lax.broadcasted_iota(jnp.int32, (BQ, PAIR), 1)
    for block in range(seq // BQ):
        start = window_start(block, seq, width)
        rows = slice(block * BQ, (block + 1) * BQ)
        keys = slice(start, start + width)
        lse_tile = jnp.zeros((BQ, PAIR), F32)
        bias = bias_ref[block]
        bias = jnp.concatenate([bias, bias], axis=0)
        for pair in range(wide // PAIR):
            lanes = slice(pair * PAIR, (pair + 1) * PAIR)
            queries = split_heads(qkv_ref[0, rows, lanes] * SCALE)
            scores = mm(queries, qkv_ref[1, keys, lanes], NT) + bias
            row_max = jnp.max(scores, axis=-1, keepdims=True)
            weight = jnp.exp(scores - row_max)
            total = jnp.sum(weight, axis=-1, keepdims=True)
            prob = (weight * (1.0 / total)).astype(BF16)
            mixed_ref[rows, lanes] = join_heads(mm(prob, qkv_ref[2, keys, lanes])).astype(BF16)
            lse = row_max + jnp.log(total)
            lse_tile = jnp.where(lane == 2 * pair, lse[:BQ], lse_tile)
            lse_tile = jnp.where(lane == 2 * pair + 1, lse[BQ:], lse_tile)
        lse_ref[rows, :] = lse_tile


def attend_backward(
    seg_q_ref, seg_k_ref, ga_ref, w_out_ref, qkv_ref, lse_ref, out_ref, sums_ref, bias_ref, gm_ref, acc_ref
):
    seq = ga_ref.shape[0]
    width = bias_ref.shape[2]
    wide = w_out_ref.shape[0]
    fill_bias(seg_q_ref, seg_k_ref, bias_ref, seq, width)
    for r in range(0, seq, 256):
        gm_ref[r:r + 256, :] = mm(ga_ref[r:r + 256, :], w_out_ref[...], NT).astype(BF16)
    acc_ref[...] = jnp.zeros_like(acc_ref)
    for block in range(seq // BQ):
        start = window_start(block, seq, width)
        rows = slice(block * BQ, (block + 1) * BQ)
        keys = slice(start, start + width)
        bias = bias_ref[block]
        bias = jnp.concatenate([bias, bias], axis=0)
        lse_tile = lse_ref[rows, :]
        for pair in range(wide // PAIR):
            lanes = slice(pair * PAIR, (pair + 1) * PAIR)
            queries = split_heads(qkv_ref[0, rows, lanes] * SCALE)
            grad_mixed = split_heads(gm_ref[rows, lanes])
            key_rows = qkv_ref[1, keys, lanes]
            scores = mm(queries, key_rows, NT) + bias
            lse = jnp.concatenate(
                [lse_tile[:, 2 * pair:2 * pair + 1], lse_tile[:, 2 * pair + 1:2 * pair + 2]], axis=0
            )
            prob = jnp.exp(scores - lse)
            grad_prob = mm(grad_mixed, qkv_ref[2, keys, lanes], NT)
            along = jnp.sum(prob * grad_prob, axis=-1, keepdims=True)
            grad_scores = (prob * (grad_prob - along)).astype(BF16)
            out_ref[0, rows, lanes] = (join_heads(mm(grad_scores, key_rows)) * SCALE).astype(BF16)
            acc_ref[0, keys, lanes] += mm(grad_scores, queries, TN)
            acc_ref[1, keys, lanes] += mm(prob.astype(BF16), grad_mixed, TN)
    out_ref[1] = acc_ref[0].astype(BF16)
    out_ref[2] = acc_ref[1].astype(BF16)
    for at, c in enumerate((0, 2)):
        total = jnp.sum(out_ref[c].astype(F32), axis=0, keepdims=True)
        sums_ref[4 * at:4 * at + 4, :] = jnp.concatenate([total, jnp.zeros((3, wide), F32)], axis=0)


def chained(kernel, count, extra=1):
    def body(*refs):
        kernel(*refs[:count], *refs[count + extra:])

    return body


def run(kernel, name, args, outs, after, scalars=0, grid=None, in_specs=None, out_specs=None, scratch=(), aliases=None, cost=15, size=10**9):
    vmem = pl.BlockSpec(memory_space=pltpu.VMEM)
    if in_specs is None:
        in_specs = [pl.BlockSpec(memory_space=pltpu.SMEM)] * scalars + [vmem] * (len(args) - scalars)
    if out_specs is None:
        out_specs = [vmem] * len(outs)
    if after is not None:
        behind = list(after) if isinstance(after, (list, tuple)) else [after]
        kernel = chained(kernel, len(args), len(behind))
        args = list(args) + behind
        in_specs = list(in_specs) + [pl.BlockSpec(memory_space=pl.ANY)] * len(behind)
    result = pl.pallas_call(
        kernel,
        name=name,
        grid=grid if grid is not None else (),
        out_shape=tuple(jax.ShapeDtypeStruct(shape, dtype) for shape, dtype in outs),
        in_specs=in_specs,
        out_specs=tuple(out_specs),
        scratch_shapes=list(scratch),
        input_output_aliases=aliases or {},
        compiler_params=pltpu.CompilerParams(vmem_limit_bytes=40 * 2**20),
        cost_estimate=pl.CostEstimate(flops=cost * 10**9, bytes_accessed=size, transcendentals=0),
    )(*args)
    return result if len(outs) > 1 else result[0]


def forward_call(sides, seg_q, seg_k, x, b, pieces_of, after):
    seq, wide = x.shape[0], pieces_of[0].shape[2]
    width = min(3 * BQ, seq)
    return run(
        attend_forward,
        "attend_forward",
        [sides, seg_q, seg_k, x, b] + list(pieces_of),
        [((3, seq, wide), BF16), ((seq, wide), BF16), ((seq, PAIR), F32)],
        after,
        cost=60,
        scalars=1,
        scratch=[pltpu.VMEM((seq // BQ, BQ, width), F32)],
    )


def backward_call(seg_q, seg_k, ga, w_out, qkv, lse, after):
    seq, wide = ga.shape[0], w_out.shape[0]
    width = min(3 * BQ, seq)
    return run(
        attend_backward,
        "attend_backward",
        [seg_q, seg_k, ga, w_out, qkv, lse],
        [((3, seq, wide), BF16), ((8, wide), F32)],
        after,
        scratch=[
            pltpu.VMEM((seq // BQ, BQ, width), F32),
            pltpu.VMEM((seq, wide), BF16),
            pltpu.VMEM((2, seq, wide), F32),
        ],
    )


def eight(values):
    return jnp.sum(values.reshape(values.shape[0] // 8, 8, values.shape[1]), axis=0)


def project_out(flip, core_ref, mixed_a_ref, mixed_b_ref, w_a_ref, w_b_ref, out_ref):
    rows = out_ref.shape[0]
    at = pl.ds(pl.multiple_of(jnp.bitwise_xor(core_ref[0], flip) * rows, rows), rows)
    out = mm(mixed_a_ref[at, :], w_a_ref[...]) + mm(mixed_b_ref[at, :], w_b_ref[...])
    out_ref[...] = out.astype(out_ref.dtype)


def second_norm(start_ref, own_ref, near_ref, b_ref, gain_ref, shift_ref, after_ref, n2_ref):
    value = start_ref[...] + (own_ref[...] + near_ref[...].astype(F32)) + b_ref[...].astype(F32)
    after_ref[...] = value
    xhat, _ = normalize(value)
    n2_ref[...] = (xhat * gain_ref[...].astype(F32) + shift_ref[...].astype(F32)).astype(BF16)


def second_norm_back(here_ref, near_ref, far_ref, after_ref, cot_ref, ok_ref, gain_ref, mid_ref, ga_ref, sums_ref):
    @pl.when(pl.program_id(0) == 0)
    def _():
        sums_ref[...] = jnp.zeros_like(sums_ref)

    grad = here_ref[...].astype(F32) + near_ref[...].astype(F32) + far_ref[...].astype(F32)
    xhat, rstd = normalize(after_ref[...])
    grad_after = cot_ref[...].astype(F32) * ok_ref[...]
    mid = grad_after + norm_back(grad, gain_ref[...].astype(F32), xhat, rstd)
    mid_ref[...] = mid
    ga_ref[...] = mid.astype(BF16)
    sums_ref[0] += eight(mid)
    sums_ref[1] += eight(grad * xhat)
    sums_ref[2] += eight(grad)
    sums_ref[3] += eight(grad_after)


def first_norm_back(own_ref, near_ref, start_ref, mid_ref, gain_ref, out_ref, sums_ref):
    @pl.when(pl.program_id(0) == 0)
    def _():
        sums_ref[...] = jnp.zeros_like(sums_ref)

    grad = own_ref[...] + near_ref[...].astype(F32)
    xhat, rstd = normalize(start_ref[...])
    out_ref[...] = (mid_ref[...] + norm_back(grad, gain_ref[...].astype(F32), xhat, rstd)).astype(BF16)
    sums_ref[0] += eight(grad * xhat)
    sums_ref[1] += eight(grad)


def down_out(act_n_ref, act_c_ref, w_ref, out_ref):
    out_ref[0] = mm(act_n_ref[...], w_ref[...]).astype(BF16)
    out_ref[1] = mm(act_c_ref[...], w_ref[...]).astype(BF16)


def down_in(act_o_ref, act_f_ref, after_ref, got_ref, b_ref, w_ref, base_ref, far_ref):
    down = mm(act_o_ref[...], w_ref[...]) + got_ref[0].astype(F32)
    base_ref[...] = after_ref[...] + down + b_ref[...].astype(F32)
    far_ref[...] = (mm(act_f_ref[...], w_ref[...]) + got_ref[1].astype(F32)).astype(BF16)


def finish(base_ref, far_ref, ok_ref, out_ref):
    out_ref[...] = ((base_ref[...] + far_ref[...].astype(F32)) * ok_ref[...]).astype(BF16)


def hand_on(in_ref, out_ref):
    out_ref[...] = in_ref[...]


def hand_on_all(*refs):
    count = len(refs) // 2
    for in_ref, out_ref in zip(refs[:count], refs[count:]):
        out_ref[...] = in_ref[...]


def handed(value, after):
    return run(hand_on, "hand_on", [value], [(value.shape, value.dtype)], after)


def small_first(two_ref, one_ref, out_ref):
    out_ref[...] = jnp.zeros_like(out_ref)
    rows = [two_ref[0], one_ref[0], one_ref[1], two_ref[1], two_ref[2], two_ref[3]]
    for at, part in enumerate(rows):
        out_ref[at:at + 1, :] = jnp.sum(part, axis=0, keepdims=True)


def small_second(own_ref, near_ref, bias_a_ref, bias_b_ref, send_ref, keep_ref):
    total = own_ref[...] + near_ref[...]
    wide = bias_a_ref.shape[1]
    for out_ref, bias_ref in ((send_ref, bias_b_ref), (keep_ref, bias_a_ref)):
        out_ref[...] = total
        out_ref[6:7, :wide] = bias_ref[0:1, :]
        out_ref[6:7, wide:2 * wide] = bias_ref[4:5, :]


def small_third(own_ref, far_ref, *refs):
    out_ref = refs[-1]
    out_ref[...] = own_ref[...] + far_ref[...]
    out_ref[7:8, :] = sum(jnp.sum(part[...], axis=0, keepdims=True) for part in refs[:-1])


def small_add(own_ref, far_ref, out_ref):
    out_ref[...] = own_ref[...] + far_ref[...]


def add_two(left_ref, right_ref, out_ref):
    out_ref[...] = add_low(left_ref[...], right_ref[...])


def token_products(count, based, side_ref, *refs):
    lefts, rights, rest = refs[:count], refs[count:2 * count], refs[2 * count:]
    total = sum(mm(left[...], right[...], TN) for left, right in zip(lefts, rights))
    if not based:
        rest[-1][...] = total
        return
    total = (total + rest[0][...]).astype(BF16)
    send_ref, keep_ref = rest[-2:]
    first = pl.program_id(0) < pl.num_programs(0) // 2

    @pl.when(first)
    def _():
        send_ref[...] = total

    @pl.when(jnp.logical_not(first))
    def _():
        keep_ref[...] = total


def token_call(sides, lefts, rights, base, after):
    tall, wide = lefts[0].shape[1], rights[0].shape[1]
    block = 256
    steps = tall // block

    def row(i, side_ref):
        return jnp.where(i < steps // 2, i + (1 - side_ref[0]) * (steps // 2), i - (1 - side_ref[0]) * (steps // 2))

    if base is None:
        outs = jax.ShapeDtypeStruct((tall, wide), F32)
        out_specs = pl.BlockSpec((block, wide), lambda i, side_ref: (row(i, side_ref), 0))
    else:
        outs = [jax.ShapeDtypeStruct((tall // 2, wide), BF16)] * 2
        out_specs = [
            pl.BlockSpec((block, wide), lambda i, _: (jnp.minimum(i, steps // 2 - 1), 0)),
            pl.BlockSpec((block, wide), lambda i, _: (jnp.maximum(i - steps // 2, 0), 0)),
        ]
    in_specs = [pl.BlockSpec((left.shape[0], block), lambda i, side_ref: (0, row(i, side_ref))) for left in lefts]
    in_specs += [pl.BlockSpec(right.shape, lambda i, _: (0, 0)) for right in rights]
    args = list(lefts) + list(rights)
    if base is not None:
        in_specs.append(pl.BlockSpec((block, wide), lambda i, side_ref: (row(i, side_ref), 0)))
        args.append(base)
    kernel = functools.partial(token_products, len(lefts), base is not None)
    return pl.pallas_call(
        chained(kernel, len(args) + 1),
        name="token_products",
        grid_spec=pltpu.PrefetchScalarGridSpec(
            num_scalar_prefetch=1,
            grid=(steps,),
            in_specs=in_specs + [pl.BlockSpec(memory_space=pl.ANY)],
            out_specs=out_specs,
        ),
        out_shape=outs,
        compiler_params=pltpu.CompilerParams(vmem_limit_bytes=40 * 2**20),
        cost_estimate=pl.CostEstimate(flops=60 * 10**9, bytes_accessed=10**9, transcendentals=0),
    )(sides, *args, after)


def three_products(x_ref, gp_ref, q_ref, kv_ref):
    q_ref[...] = mm(x_ref[...], gp_ref[0]).astype(BF16)
    for c in range(2):
        kv_ref[c] = mm(x_ref[...], gp_ref[c + 1]).astype(BF16)


def three_call(x_turned, gp, after):
    tall, seq = x_turned.shape
    wide = gp.shape[2]
    block = 256
    return run(
        three_products,
        "three_products",
        [x_turned, gp],
        [((tall, wide), BF16), ((2, tall, wide), BF16)],
        after,
        grid=(tall // block,),
        in_specs=[pl.BlockSpec((block, seq), lambda i: (i, 0)), pl.BlockSpec(gp.shape, lambda i: (0, 0, 0))],
        out_specs=[
            pl.BlockSpec((block, wide), lambda i: (i, 0)),
            pl.BlockSpec((2, block, wide), lambda i: (0, i, 0)),
        ],
    )


def turned_product(mixed_ref, ga_ref, out_ref):
    out_ref[...] = mm(ga_ref[...], mixed_ref[...], TN).astype(BF16)


def back_project(flip, core_ref, gp_a_ref, gp_b_ref, w_a_ref, w_b_ref, out_ref):
    rows = out_ref.shape[0]
    at = pl.ds(pl.multiple_of(jnp.bitwise_xor(core_ref[0], flip) * rows, rows), rows)
    out = sum(
        mm(gp_ref[c, at, :], w_ref[c], NT)
        for c in range(3)
        for gp_ref, w_ref in ((gp_a_ref, w_a_ref), (gp_b_ref, w_b_ref))
    )
    out_ref[...] = out.astype(out_ref.dtype)


def by_rows(kernel, name, args, outs, after, block=128):
    rows = args[0].shape[0]

    def spec(shape):
        if shape[0] == rows:
            return pl.BlockSpec((block,) + tuple(shape[1:]), lambda i: (i,) + (0,) * (len(shape) - 1))
        return pl.BlockSpec(tuple(shape), lambda i: (0,) * len(shape))

    return run(
        kernel,
        name,
        args,
        outs,
        after,
        grid=(rows // block,),
        in_specs=[spec(arg.shape) for arg in args],
        out_specs=[spec(shape) for shape, _ in outs],
        size=1,
    )


def fold(bit, last, side_ref, cur_ref, got_ref, *out_refs):
    if last:
        out_refs[0][...] = add_low(cur_ref[...], got_ref[...])
        return
    half = got_ref.shape[0] // 2
    for side, out_ref in ((1 - side_ref[bit], out_refs[0]), (side_ref[bit], out_refs[1])):
        at = pl.ds(pl.multiple_of(side * half, half), half)
        out_ref[...] = add_low(cur_ref[at, :], got_ref[at, :])


def begin_pair(paired, side_ref, *refs):
    send_ref, keep_ref = refs[-2:]
    if paired:
        parts = [(refs[0].at[c], refs[1].at[c]) for c in range(2)]
    else:
        parts = [refs[0:2], refs[2:4]]
    for side in range(2):

        @pl.when(side_ref[0] == side)
        def _():
            send_ref[...] = add_low(parts[1 - side][0][...], parts[1 - side][1][...])
            keep_ref[...] = add_low(parts[side][0][...], parts[side][1][...])


def join(left_ref, right_ref, out_ref):
    rows = left_ref.shape[0]
    out_ref[:rows, :] = left_ref[...]
    out_ref[rows:, :] = right_ref[...]


def place(piece, spot_ref, own_ref, other_ref, out_ref):
    count = own_ref.shape[0] // piece
    steps = out_ref.shape[0] // piece
    for at in range(steps):
        apart = jnp.bitwise_xor(pl.program_id(0) * steps + at, spot_ref[0])
        rows = pl.ds(pl.multiple_of(jnp.bitwise_and(apart, count - 1) * piece, piece), piece)
        far_side = apart >= count
        into = slice(at * piece, (at + 1) * piece)

        @pl.when(far_side)
        def _():
            out_ref[into, :] = other_ref[rows, :].astype(F32)

        @pl.when(jnp.logical_not(far_side))
        def _():
            out_ref[into, :] = own_ref[rows, :].astype(F32)


def pieces(count, spot, own_ref, other_ref, first, steps):
    piece = own_ref.shape[0] // count
    for at in range(steps):
        apart = jnp.bitwise_xor(first + at, spot)
        rows = pl.ds(pl.multiple_of(jnp.bitwise_and(apart, count - 1) * piece, piece), piece)
        mine, others = own_ref[rows, :].astype(F32), other_ref[rows, :].astype(F32)
        yield at * piece, piece, jnp.where(apart >= count, others, mine)


def place_turned(count, spot_ref, own_ref, other_ref, w_out_ref, part_ref):
    for at, piece, value in pieces(count, spot_ref[0], own_ref, other_ref, 0, count):
        w_out_ref[:, at:at + piece] = value.T
    for at, piece, value in pieces(count, spot_ref[0], own_ref, other_ref, count, count):
        part_ref[at:at + piece, :] = value


def place_two(count, spot_ref, own_ref, other_ref, _, out_ref):
    for at, piece, value in pieces(count, spot_ref[0], own_ref, other_ref, pl.program_id(0) * count, count):
        out_ref[at:at + piece, :] = value


class Sum:
    def __init__(self, size, height):
        self.size, self.bits, self.height = size, size.bit_length() - 1, height
        me = lax.axis_index("dp")
        sides = [(me // (1 << b)) % 2 for b in range(self.bits)]
        self.sides = jnp.stack(sides).astype(jnp.int32)
        self.spot = sum(side << (self.bits - 1 - b) for b, side in enumerate(sides))

    def begin(self, send, keep):
        self.keep, self.step = keep, 0
        self.sent = swap(send, "dp", self.size, 1)

    def begin_pairs(self, arrays, after):
        shape = arrays[0].shape[-2:]
        send, keep = run(
            functools.partial(begin_pair, len(arrays) == 2), "begin_pair", [self.sides] + list(arrays),
            [(shape, BF16)] * 2, after, scalars=1,
        )
        self.begin(send, keep)
        return keep

    def fold(self, after):
        if self.step >= self.bits:
            return after
        self.step += 1
        last = self.step == self.bits
        rows, columns = self.sent.shape
        kernel = functools.partial(fold, self.step, last)
        outs = [((rows, columns), BF16)] if last else [((rows // 2, columns), BF16)] * 2
        out = run(kernel, "fold", [self.sides, self.keep, self.sent], outs, after, scalars=1)
        self.keep = out if last else out[1]
        send = out if last else out[0]
        self.sent = swap(send, "dp", self.size, 1 << min(self.step, self.bits - 1))
        return self.keep

    def spread(self, after):
        if self.step < self.bits:
            return after
        bit = 2 * self.bits - 2 - self.step
        rows, columns = self.keep.shape
        self.keep = run(join, "join", [self.keep, self.sent], [((2 * rows, columns), BF16)], after)
        self.sent = swap(self.keep, "dp", self.size, 1 << bit)
        self.step += 1
        return self.keep

    def complete(self, after):
        while self.step < self.bits:
            after = self.fold(after)
        while self.step < 2 * self.bits - 1:
            after = self.spread(after)
        return after

    def place(self, after):
        after = self.complete(after)
        rows, columns = self.keep.shape
        piece = rows * 2 // self.size
        return run(
            functools.partial(place, piece),
            "place",
            [self.spot.reshape(1).astype(jnp.int32), self.keep, self.sent],
            [((2 * rows, columns), F32)],
            after,
            grid=(2,),
            in_specs=[
                pl.BlockSpec(memory_space=pltpu.SMEM),
                pl.BlockSpec((rows, columns), lambda i: (0, 0)),
                pl.BlockSpec((rows, columns), lambda i: (0, 0)),
            ],
            out_specs=[pl.BlockSpec((rows, columns), lambda i: (i, 0))],
        )[: self.height]

    def place_out(self, after):
        after = self.complete(after)
        rows, columns = self.keep.shape
        return run(
            functools.partial(place_turned, self.size // 2),
            "place_turned",
            [self.spot.reshape(1).astype(jnp.int32), self.keep, self.sent],
            [((columns, rows), F32), ((3 * rows, columns), F32)],
            after,
            grid=(1,),
            in_specs=[pl.BlockSpec(memory_space=pltpu.SMEM)]
            + [pl.BlockSpec((rows, columns), lambda i: (0, 0))] * 2,
            out_specs=[
                pl.BlockSpec((columns, rows), lambda i: (0, 0)),
                pl.BlockSpec((rows, columns), lambda i: (0, 0)),
            ],
        )

    def place_rest(self, into, after):
        after = self.complete(after)
        rows, columns = self.keep.shape
        return run(
            functools.partial(place_two, self.size // 2),
            "place_two",
            [self.spot.reshape(1).astype(jnp.int32), self.keep, self.sent, into],
            [((3 * rows, columns), F32)],
            after,
            grid=(2,),
            in_specs=[pl.BlockSpec(memory_space=pltpu.SMEM)]
            + [pl.BlockSpec((rows, columns), lambda i: (0, 0))] * 2
            + [pl.BlockSpec(memory_space=pl.ANY)],
            out_specs=[pl.BlockSpec((rows, columns), lambda i: (i + 1, 0))],
            aliases={3: 0},
        )


def gelu_and_slope(up):
    size = jnp.abs(up)
    t = 1.0 / (1.0 + (0.3275911 * 0.7071067811865476) * size)
    bell = jnp.exp(-0.5 * up * up)
    poly = t * (
        0.5 * 0.254829592
        + t * (0.5 * -0.284496736 + t * (0.5 * 1.421413741 + t * (0.5 * -1.453152027 + t * (0.5 * 1.061405429))))
    )
    tail = poly * bell
    cdf = jnp.where(up >= 0.0, 1.0 - tail, tail)
    return up * cdf, cdf + up * bell * 0.3989422804014327


def feed(n2_ref, gd_ref, ok_ref, w_up_ref, b_up_ref, w_down_ref, gn2_ref, act_ref, gup_ref, gb_ref):
    hidden = w_up_ref.shape[1]
    rows = n2_ref.shape[0]
    step = 256
    n2 = n2_ref[...]
    gd = gd_ref[...]
    ok = ok_ref[...]

    @pl.when(pl.program_id(0) == 0)
    def _():
        gb_ref[...] = jnp.zeros_like(gb_ref)

    for at in range(0, hidden, step):
        part = slice(at, at + step)
        up = mm(n2, w_up_ref[:, part]) + b_up_ref[:, part].astype(F32)
        grad_act = mm(gd, w_down_ref[part, :], NT)
        act, slope = gelu_and_slope(up)
        grad_up = (slope * (grad_act * ok)).astype(BF16)
        act_ref[:, part] = (act * ok).astype(BF16)
        gup_ref[:, part] = grad_up
        gb_ref[:, part] += jnp.sum(grad_up.astype(F32).reshape(rows // 8, 8, step), axis=0)
    gn2_ref[...] = mm(gup_ref[...], w_up_ref[...], NT).astype(BF16)


def feed_call(n2, gd, ok, w_up, b_up, w_down, after):
    rows, hidden = n2.shape[0], w_up.shape[1]
    block = 256
    tokens = pl.BlockSpec((block, D), lambda i: (i, 0))
    tall = pl.BlockSpec((block, hidden), lambda i: (i, 0))

    def fixed(shape):
        return pl.BlockSpec(shape, lambda i: (0, 0))

    return run(
        feed,
        "feed",
        [n2, gd, ok, w_up, b_up, w_down],
        [((rows, D), BF16), ((rows, hidden), BF16), ((rows, hidden), BF16), ((8, hidden), F32)],
        after,
        grid=(rows // block,),
        in_specs=[tokens, tokens, pl.BlockSpec((block, 1), lambda i: (i, 0)), fixed((D, hidden)), fixed((1, hidden)), fixed((hidden, D))],
        out_specs=[tokens, tall, tall, fixed((8, hidden))],
    )


def swap(value, axis, size, flip):
    return lax.ppermute(value, axis, [(i, i ^ flip) for i in range(size)])


def add_low(left, right):
    return (left.astype(F32) + right.astype(F32)).astype(BF16)


def sum_over(value, axis, size):
    flip = 1
    while flip < size:
        value = value + swap(value, axis, size, flip)
        flip *= 2
    return value


def on_device(
    dp_size,
    mp_size,
    tokens,
    segment_ids,
    valid_mask,
    patch_index,
    gsd_index,
    w_qkv,
    bias_qv,
    w_out,
    b_out,
    gain_one,
    shift_one,
    gain_two,
    shift_two,
    w_up,
    b_up,
    w_down,
    b_down,
    cotangent,
):
    own_rows = tokens.shape[0]
    mp = lax.axis_index("mp")
    core = mp % 2
    row = mp // 2

    def near(value):
        return swap(value, "mp", mp_size, 1)

    def far(value):
        return swap(value, "mp", mp_size, 2)

    core_s = core.reshape(1).astype(jnp.int32)
    down_sum, up_sum = Sum(dp_size, w_down.shape[0]), Sum(dp_size, w_up.shape[0])
    first_sum, second_sum = Sum(dp_size, 2 * D), Sum(dp_size, 2 * D)
    sides = down_sum.sides

    cot_near = near(cotangent)
    inputs = [segment_ids, valid_mask, patch_index, gsd_index]
    shape = (3, D // 4, w_qkv.shape[2])
    piece_a, piece_b, segment_ids, valid_mask, patch_index, gsd_index = run(
        cut, "cut", [sides, w_qkv] + inputs, [(shape, BF16)] * 2 + [(part.shape, part.dtype) for part in inputs],
        None, scalars=1,
    )
    far_bias = far(bias_qv)
    far_a, far_b = far(piece_a), far(piece_b)

    own_start = mp * own_rows
    level = image_levels(segment_ids, gsd_index)
    codes = jnp.stack([patch_index // GRID, patch_index % GRID]) * GSDS + level
    own_codes = lax.dynamic_slice_in_dim(codes.reshape(2, -1, 1), own_start, own_rows, axis=1)
    all_valid = valid_mask.reshape(-1, 1).astype(F32)

    def valid_of(flip):
        at = jnp.bitwise_xor(mp, flip) * own_rows
        return lax.dynamic_slice_in_dim(all_valid, at, own_rows)

    own_valid = valid_of(0)

    row_seg = lax.dynamic_index_in_dim(segment_ids, row, 0, keepdims=True)
    row_ok = lax.dynamic_index_in_dim(valid_mask, row, 0, keepdims=True)
    seg_k = jnp.where(row_ok == 1, row_seg, -1)
    seg_q = row_seg.reshape(-1, 1)

    start_sum, normed = by_rows(
        front, "front",
        [tokens, own_codes[0], own_codes[1], code_table(), gain_one[None], shift_one[None]],
        [(tokens.shape, F32), (tokens.shape, BF16)], [piece_b, cot_near],
    )
    half = (own_rows, D)
    w_out_sent, a_pass = run(
        hand_on_all, "hand_on_all", [w_out, far_a], [(w_out.shape, BF16), (far_a.shape, BF16)], normed, cost=60
    )
    far_out = far(w_out_sent)
    other_a = swap(a_pass, "dp", dp_size, 1)
    normed_row = run(in_row, "in_row", [core_s, normed, near(normed)], [((2 * own_rows, D), BF16)], a_pass, scalars=1)
    b_pass, cot_sent = run(
        hand_on_all, "hand_on_all", [far_b, cotangent], [(far_b.shape, BF16), (half, BF16)], normed_row
    )
    other_b = swap(b_pass, "dp", dp_size, 1)
    cot_far = far(cot_sent)

    qkv_a, mixed_a, lse_a = forward_call(sides, seg_q, seg_k, normed_row, bias_qv, [w_qkv], cot_sent)
    pieces_b = [a_pass, b_pass, other_a, other_b]
    qkv_b, mixed_b, lse_b = forward_call(sides, seg_q, seg_k, normed_row, far_bias, pieces_b, lse_a)
    operands = [core_s, mixed_a, mixed_b, w_out, far_out]
    attn_near = run(functools.partial(project_out, 1), "project_out", operands, [(half, BF16)], lse_b, scalars=1)
    attn_own = run(functools.partial(project_out, 0), "project_out", operands, [(half, F32)], attn_near, scalars=1)
    after_attn, n2 = by_rows(
        second_norm, "second_norm",
        [start_sum, attn_own, near(attn_near), b_out[None], gain_two[None], shift_two[None]],
        [(half, F32), (half, BF16)], attn_own,
    )
    n2_far = far(n2)
    n2_near = near(n2)

    b_up_row = b_up[None, :]
    gn2_o, act_o, gup_o, gb_o = feed_call(n2, cotangent, own_valid, w_up, b_up_row, w_down, n2)
    gn2_n, act_n, gup_n, gb_n = feed_call(n2_near, cot_near, valid_of(1), w_up, b_up_row, w_down, gb_o)
    from_near = near(gn2_n)
    down_here = token_call(sides, (act_o, act_n), (cotangent, cot_near), None, gb_n)
    cot_pass = handed(cot_far, [down_here, from_near])
    cot_cross = near(cot_pass)
    up_here = token_call(sides, (n2, n2_near), (gup_o, gup_n), None, cot_pass)
    n2_pass = handed(n2_far, up_here)
    n2_cross = near(n2_pass)
    gn2_f, act_f, gup_f, gb_f = feed_call(n2_pass, cot_pass, valid_of(2), w_up, b_up_row, w_down, n2_pass)
    gn2_c, act_c, gup_c, gb_c = feed_call(n2_cross, cot_cross, valid_of(3), w_up, b_up_row, w_down, gb_f)
    cross_gn2 = near(gn2_c)
    down_send, down_keep = token_call(sides, (act_f, act_c), (cot_pass, cot_cross), down_here, gb_c)
    down_sum.begin(down_send, down_keep)
    to_far = by_rows(add_two, "add_two", [gn2_f, cross_gn2], [(half, BF16)], down_keep)
    from_far = far(to_far)
    down_sent = run(down_out, "down_out", [act_n, act_c, w_down], [((2,) + half, BF16)], to_far)
    up_send, up_keep = token_call(sides, (n2_pass, n2_cross), (gup_f, gup_c), up_here, down_sent)
    up_sum.begin(up_send, up_keep)

    down_base, down_far = run(
        down_in, "down_in",
        [act_o, act_f, after_attn, near(down_sent), b_down[None], w_down],
        [(half, F32), (half, BF16)], up_keep,
    )
    x_turned = run(turn, "turn", [normed_row], [((D, 2 * own_rows), BF16)], down_base)
    far_qkv = run(assemble, "assemble", [sides] + pieces_b, [(w_qkv.shape, BF16)], x_turned, scalars=1)
    mid, ga, sums_two = by_rows(
        second_norm_back, "second_norm_back",
        [gn2_o, from_near, from_far, after_attn, cotangent, own_valid, gain_two[None]],
        [(half, F32), (half, BF16), ((4, 8, D), F32)], far_qkv,
    )
    last = down_sum.fold(ga)
    ga_row = run(in_row, "in_row", [core_s, ga, near(ga)], [((2 * own_rows, D), BF16)], last, scalars=1)
    wide = w_qkv.shape[2]
    turned = [((D, wide), BF16)]
    gw_out_b = run(turned_product, "turned_product", [mixed_b, ga_row], turned, ga_row)
    far_out_grad = far(gw_out_b)
    gp_b, bias_b = backward_call(seg_q, seg_k, ga_row, far_out, qkv_b, lse_b, gw_out_b)
    q_b, kv_b = three_call(x_turned, gp_b, bias_b)
    far_q, far_kv = far(q_b), far(kv_b)
    last = up_sum.fold(q_b)
    last = down_sum.fold(last)
    gp_a, bias_a = backward_call(seg_q, seg_k, ga_row, w_out, qkv_a, lse_a, last)
    last = down_sum.fold(bias_a)
    last = up_sum.fold(last)
    gw_out_a = run(turned_product, "turned_product", [mixed_a, ga_row], turned, last)
    q_a, kv_a = three_call(x_turned, gp_a, gw_out_a)
    last = first_sum.begin_pairs([gw_out_a, far_out_grad, q_a, far_q], q_a)
    operands = [core_s, gp_a, gp_b, w_qkv, far_qkv]
    gn_near = run(functools.partial(back_project, 1), "back_project", operands, [(half, BF16)], last, scalars=1)
    gn_own = run(functools.partial(back_project, 0), "back_project", operands, [(half, F32)], gn_near, scalars=1)
    last = down_sum.spread(gn_own)
    last = up_sum.fold(last)
    last = second_sum.begin_pairs([kv_a, far_kv], last)
    last = first_sum.fold(last)
    grad_tokens, sums_one = by_rows(
        first_norm_back, "first_norm_back",
        [gn_own, near(gn_near), start_sum, mid, gain_one[None]],
        [(half, BF16), ((2, 8, D), F32)], last,
    )
    down_got = far(handed(down_far, sums_one))
    tile = [((8, D), F32)]
    small = run(small_first, "small_first", [sums_two, sums_one], tile, sums_one)
    small_got = near(small)
    last = down_sum.spread(small)
    last = up_sum.spread(last)
    last = first_sum.fold(last)
    last = second_sum.fold(last)
    send, small = run(small_second, "small_second", [small, small_got, bias_a, bias_b], tile * 2, last)
    small_got = far(send)
    last = first_sum.fold(small)
    last = second_sum.fold(last)
    layer_out = by_rows(finish, "finish", [down_base, down_got, own_valid], [(half, BF16)], last)
    small = run(small_third, "small_third", [small, small_got, gb_o, gb_n, gb_f, gb_c], tile, layer_out)
    flips = [1 << b for b in range(dp_size.bit_length() - 1)]
    small_got = swap(small, "dp", dp_size, flips[0])
    last = up_sum.spread(small)
    last = first_sum.spread(last)
    last = second_sum.fold(last)
    small = run(small_add, "small_add", [small, small_got], tile, last)
    small_got = swap(small, "dp", dp_size, flips[1])
    last = first_sum.spread(small)
    last = second_sum.spread(last)
    grad_w_down = down_sum.place(last)
    small = run(small_add, "small_add", [small, small_got], tile, grad_w_down)
    small_got = swap(small, "dp", dp_size, flips[2])
    last = second_sum.spread(small)
    grad_w_up = up_sum.place(last)
    for flip in flips[3:]:
        small = run(small_add, "small_add", [small, small_got], tile, grad_w_up)
        small_got = swap(small, "dp", dp_size, flip)
    small = run(small_add, "small_add", [small, small_got], tile, grad_w_up)
    grad_w_out, grad_w_qkv = first_sum.place_out(small)
    grad_w_qkv = second_sum.place_rest(grad_w_qkv, grad_w_out).reshape(w_qkv.shape)
    grad_bias_qv = small[6, : 2 * wide].reshape(2, wide)
    grad_b_up = small[7]
    return (
        layer_out,
        grad_tokens,
        grad_w_qkv,
        grad_bias_qv,
        grad_w_out,
        small[0],
        small[1],
        small[2],
        small[3],
        small[4],
        grad_w_up,
        grad_b_up,
        grad_w_down,
        small[5],
    )


def solution(mesh):
    return jax.shard_map(
        functools.partial(on_device, mesh.shape["dp"], mesh.shape["mp"]),
        mesh=mesh,
        in_specs=(
            P(("dp", "mp"), None),
            P("dp", None),
            P("dp", None),
            P("dp", None),
            P("dp", None),
            P(None, None, "mp"),
            P(None, "mp"),
            P("mp", None),
            P(),
            P(),
            P(),
            P(),
            P(),
            P(None, "mp"),
            P("mp"),
            P("mp", None),
            P(),
            P(("dp", "mp"), None),
        ),
        out_specs=(
            P(("dp", "mp"), None),
            P(("dp", "mp"), None),
            P(None, None, "mp"),
            P(None, "mp"),
            P("mp", None),
            P(),
            P(),
            P(),
            P(),
            P(),
            P(None, "mp"),
            P("mp"),
            P("mp", None),
            P(),
        ),
        check_vma=False,
    )
```

```python
import functools
import jax
import jax.numpy as jnp
from jax import lax
from jax.experimental import pallas as pl
from jax.experimental.pallas import tpu as pltpu
from jax.sharding import PartitionSpec as P

D = 1024
HEAD = 64
SEGS = 16
GRID = 14
GSDS = 8
EPSILON = 1e-06
MASKED = -1000000000.0
SCALE = HEAD ** (-0.5)
BQ = 128
PAIR = 2 * HEAD
F32 = jnp.float32
BF16 = jnp.bfloat16
NN = (((1,), (0,)), ((), ()))
NT = (((1,), (1,)), ((), ()))
TN = (((0,), (0,)), ((), ()))


def mm(left, right, dims=NN):
    return lax.dot_general(left, right, dims, preferred_element_type=F32)


def image_levels(segment_ids, gsd_index):
    in_image = segment_ids[..., None] == jnp.arange(SEGS, dtype=jnp.int32)
    return jnp.sum(jnp.where(in_image, gsd_index[:, None, :], 0), axis=-1)


def code_table():
    quarter = D // 4
    frequency = 1.0 / 10000.0 ** (jnp.arange(quarter, dtype=jnp.float32) / quarter)
    ratio = 2.0 ** (0.5 * jnp.arange(GSDS, dtype=jnp.float32) - 1.0)
    place = jnp.arange(16, dtype=jnp.float32)
    angle = (place[:, None] * ratio[None, :]).reshape(-1, 1) * frequency
    return jnp.concatenate([jnp.sin(angle), jnp.cos(angle)], axis=-1)


def front(tokens_ref, row_ref, col_ref, table_ref, gain_ref, shift_ref, start_ref, normed_ref):
    high = table_ref[...].astype(BF16)
    rest = table_ref[...] - high.astype(F32)
    middle = rest.astype(BF16)
    low = (rest - middle.astype(F32)).astype(BF16)
    spots = lax.broadcasted_iota(jnp.int32, (tokens_ref.shape[0], table_ref.shape[0]), 1)
    half = table_ref.shape[1]
    for at, index_ref in ((0, row_ref), (half, col_ref)):
        chosen = (spots == index_ref[...]).astype(F32).astype(BF16)
        code = (mm(chosen, low) + mm(chosen, middle)) + mm(chosen, high)
        start_ref[:, at:at + half] = tokens_ref[:, at:at + half].astype(F32) + code
    xhat, _ = normalize(start_ref[...])
    normed_ref[...] = (xhat * gain_ref[...].astype(F32) + shift_ref[...].astype(F32)).astype(BF16)


def normalize(values):
    row_mean = jnp.mean(values, axis=-1, keepdims=True)
    centred = values - row_mean
    row_var = jnp.mean(centred * centred, axis=-1, keepdims=True)
    rstd = lax.rsqrt(row_var + EPSILON)
    return centred * rstd, rstd


def norm_back(grad, gain, xhat, rstd):
    scaled = grad * gain
    mean_scaled = jnp.mean(scaled, axis=-1, keepdims=True)
    mean_along = jnp.mean(scaled * xhat, axis=-1, keepdims=True)
    return rstd * (scaled - mean_scaled - xhat * mean_along)


def window_start(block, seq, width):
    return min(max(block * BQ - BQ, 0), seq - width)


def fill_bias(seg_q_ref, seg_k_ref, bias_ref, seq, width):
    for block in range(seq // BQ):
        start = window_start(block, seq, width)
        seg_q = seg_q_ref[block * BQ:(block + 1) * BQ, :]
        seg_k = seg_k_ref[:, start:start + width]
        row = lax.broadcasted_iota(jnp.int32, (BQ, width), 0) + block * BQ
        col = lax.broadcasted_iota(jnp.int32, (BQ, width), 1) + start
        allowed = (seg_q == seg_k) | (row == col)
        bias_ref[block] = jnp.where(allowed, 0.0, MASKED)


def split_heads(tile):
    low = lax.broadcasted_iota(jnp.int32, tile.shape, 1) < HEAD
    zero = jnp.zeros_like(tile)
    return jnp.concatenate([jnp.where(low, tile, zero), jnp.where(low, zero, tile)], axis=0)


def join_heads(stacked):
    half = stacked.shape[0] // 2
    low = lax.broadcasted_iota(jnp.int32, (half, PAIR), 1) < HEAD
    return jnp.where(low, stacked[:half], stacked[half:])


def piece_places(side_ref, w_refs, depth):
    if len(w_refs) == 1:
        return [(slice(None), w_refs[0])]
    rows = depth // 4
    starts = [side_ref[0] * 2, side_ref[0] * 2 + 1, (1 - side_ref[0]) * 2, (1 - side_ref[0]) * 2 + 1]
    return [(pl.ds(pl.multiple_of(at * rows, rows), rows), w_ref) for at, w_ref in zip(starts, w_refs)]


def assemble(side_ref, *refs):
    out_ref = refs[-1]
    for at, w_ref in piece_places(side_ref, refs[:-1], out_ref.shape[1]):
        out_ref[:, at, :] = w_ref[...]


def turn(in_ref, out_ref):
    out_ref[...] = in_ref[...].T


def cut(side_ref, w_ref, *out_refs):
    rows = w_ref.shape[1] // 4
    for piece, out_ref in enumerate(out_refs):
        at = pl.ds(pl.multiple_of((side_ref[0] * 2 + piece) * rows, rows), rows)
        out_ref[...] = w_ref[:, at, :]


def in_row(core_ref, own_ref, other_ref, out_ref):
    rows = own_ref.shape[0]
    for side, in_ref in ((core_ref[0], own_ref), (1 - core_ref[0], other_ref)):
        out_ref[pl.ds(pl.multiple_of(side * rows, rows), rows), :] = in_ref[...]


def attend_forward(side_ref, seg_q_ref, seg_k_ref, x_ref, b_ref, *refs):
    w_refs, (qkv_ref, mixed_ref, lse_ref, bias_ref) = refs[:-4], refs[-4:]
    seq = x_ref.shape[0]
    width = bias_ref.shape[2]
    wide = w_refs[0].shape[2]
    fill_bias(seg_q_ref, seg_k_ref, bias_ref, seq, width)
    for c in range(3):
        for r in range(0, seq, 256):
            out = sum(
                mm(x_ref[r:r + 256, at], w_ref[c]) for at, w_ref in piece_places(side_ref, w_refs, x_ref.shape[1])
            )
            if c != 1:
                out = out + b_ref[c // 2:c // 2 + 1, :].astype(F32)
            qkv_ref[c, r:r + 256, :] = out.astype(BF16)
    lane = lax.broadcasted_iota(jnp.int32, (BQ, PAIR), 1)
    pairs = range(wide // PAIR)
    for block in range(seq // BQ):
        start = window_start(block, seq, width)
        rows = slice(block * BQ, (block + 1) * BQ)
        keys = slice(start, start + width)
        bias = bias_ref[block]
        bias = jnp.concatenate([bias, bias], axis=0)
        lanes = [slice(pair * PAIR, (pair + 1) * PAIR) for pair in pairs]
        queries = [split_heads(qkv_ref[0, rows, at] * SCALE) for at in lanes]
        scores = [mm(queries[p], qkv_ref[1, keys, lanes[p]], NT) + bias for p in pairs]
        row_max = [jnp.max(part, axis=-1, keepdims=True) for part in scores]
        weight = [jnp.exp(scores[p] - row_max[p]) for p in pairs]
        mixed = [mm(weight[p].astype(BF16), qkv_ref[2, keys, lanes[p]]) for p in pairs]
        total = [jnp.sum(part, axis=-1, keepdims=True) for part in weight]
        lse_tile = jnp.zeros((BQ, PAIR), F32)
        for p in pairs:
            mixed_ref[rows, lanes[p]] = join_heads(mixed[p] * (1.0 / total[p])).astype(BF16)
            lse = row_max[p] + jnp.log(total[p])
            lse_tile = jnp.where(lane == 2 * p, lse[:BQ], lse_tile)
            lse_tile = jnp.where(lane == 2 * p + 1, lse[BQ:], lse_tile)
        lse_ref[rows, :] = lse_tile


def attend_backward(
    seg_q_ref, seg_k_ref, ga_ref, w_out_ref, qkv_ref, lse_ref, out_ref, sums_ref, bias_ref, gm_ref, acc_ref
):
    seq = ga_ref.shape[0]
    width = bias_ref.shape[2]
    wide = w_out_ref.shape[0]
    fill_bias(seg_q_ref, seg_k_ref, bias_ref, seq, width)
    for r in range(0, seq, 256):
        gm_ref[r:r + 256, :] = mm(ga_ref[r:r + 256, :], w_out_ref[...], NT).astype(BF16)
    acc_ref[...] = jnp.zeros_like(acc_ref)
    for block in range(seq // BQ):
        start = window_start(block, seq, width)
        rows = slice(block * BQ, (block + 1) * BQ)
        keys = slice(start, start + width)
        bias = bias_ref[block]
        bias = jnp.concatenate([bias, bias], axis=0)
        lse_tile = lse_ref[rows, :]
        pairs = range(wide // PAIR)
        lanes = [slice(pair * PAIR, (pair + 1) * PAIR) for pair in pairs]
        queries = [split_heads(qkv_ref[0, rows, at] * SCALE) for at in lanes]
        grad_mixed = [split_heads(gm_ref[rows, at]) for at in lanes]
        key_rows = [qkv_ref[1, keys, at] for at in lanes]
        scores = [mm(queries[p], key_rows[p], NT) + bias for p in pairs]
        grad_prob = [mm(grad_mixed[p], qkv_ref[2, keys, lanes[p]], NT) for p in pairs]
        lse = [
            jnp.concatenate([lse_tile[:, 2 * p:2 * p + 1], lse_tile[:, 2 * p + 1:2 * p + 2]], axis=0)
            for p in pairs
        ]
        prob = [jnp.exp(scores[p] - lse[p]) for p in pairs]
        along = [jnp.sum(prob[p] * grad_prob[p], axis=-1, keepdims=True) for p in pairs]
        grad_scores = [(prob[p] * (grad_prob[p] - along[p])).astype(BF16) for p in pairs]
        for p in pairs:
            acc_ref[1, keys, lanes[p]] += mm(prob[p].astype(BF16), grad_mixed[p], TN)
        for p in pairs:
            out_ref[0, rows, lanes[p]] = (join_heads(mm(grad_scores[p], key_rows[p])) * SCALE).astype(BF16)
            acc_ref[0, keys, lanes[p]] += mm(grad_scores[p], queries[p], TN)
    out_ref[1] = acc_ref[0].astype(BF16)
    out_ref[2] = acc_ref[1].astype(BF16)
    for at, c in enumerate((0, 2)):
        total = jnp.sum(out_ref[c].astype(F32), axis=0, keepdims=True)
        sums_ref[4 * at:4 * at + 4, :] = jnp.concatenate([total, jnp.zeros((3, wide), F32)], axis=0)


def chained(kernel, count, extra=1):
    def body(*refs):
        kernel(*refs[:count], *refs[count + extra:])

    return body


def run(kernel, name, args, outs, after, scalars=0, grid=None, in_specs=None, out_specs=None, scratch=(), aliases=None, cost=15, size=10**9):
    vmem = pl.BlockSpec(memory_space=pltpu.VMEM)
    if in_specs is None:
        in_specs = [pl.BlockSpec(memory_space=pltpu.SMEM)] * scalars + [vmem] * (len(args) - scalars)
    if out_specs is None:
        out_specs = [vmem] * len(outs)
    if after is not None:
        behind = list(after) if isinstance(after, (list, tuple)) else [after]
        kernel = chained(kernel, len(args), len(behind))
        args = list(args) + behind
        in_specs = list(in_specs) + [pl.BlockSpec(memory_space=pl.ANY)] * len(behind)
    result = pl.pallas_call(
        kernel,
        name=name,
        grid=grid if grid is not None else (),
        out_shape=tuple(jax.ShapeDtypeStruct(shape, dtype) for shape, dtype in outs),
        in_specs=in_specs,
        out_specs=tuple(out_specs),
        scratch_shapes=list(scratch),
        input_output_aliases=aliases or {},
        compiler_params=pltpu.CompilerParams(vmem_limit_bytes=40 * 2**20),
        cost_estimate=pl.CostEstimate(flops=cost * 10**9, bytes_accessed=size, transcendentals=0),
    )(*args)
    return result if len(outs) > 1 else result[0]


def forward_call(sides, seg_q, seg_k, x, b, pieces_of, after):
    seq, wide = x.shape[0], pieces_of[0].shape[2]
    width = min(3 * BQ, seq)
    return run(
        attend_forward,
        "attend_forward",
        [sides, seg_q, seg_k, x, b] + list(pieces_of),
        [((3, seq, wide), BF16), ((seq, wide), BF16), ((seq, PAIR), F32)],
        after,
        cost=60,
        scalars=1,
        scratch=[pltpu.VMEM((seq // BQ, BQ, width), F32)],
    )


def backward_call(seg_q, seg_k, ga, w_out, qkv, lse, after):
    seq, wide = ga.shape[0], w_out.shape[0]
    width = min(3 * BQ, seq)
    return run(
        attend_backward,
        "attend_backward",
        [seg_q, seg_k, ga, w_out, qkv, lse],
        [((3, seq, wide), BF16), ((8, wide), F32)],
        after,
        scratch=[
            pltpu.VMEM((seq // BQ, BQ, width), F32),
            pltpu.VMEM((seq, wide), BF16),
            pltpu.VMEM((2, seq, wide), F32),
        ],
    )


def eight(values):
    return jnp.sum(values.reshape(values.shape[0] // 8, 8, values.shape[1]), axis=0)


def project_out(flip, core_ref, mixed_a_ref, mixed_b_ref, w_a_ref, w_b_ref, out_ref):
    rows = out_ref.shape[0]
    at = pl.ds(pl.multiple_of(jnp.bitwise_xor(core_ref[0], flip) * rows, rows), rows)
    out = mm(mixed_a_ref[at, :], w_a_ref[...]) + mm(mixed_b_ref[at, :], w_b_ref[...])
    out_ref[...] = out.astype(out_ref.dtype)


def second_norm(start_ref, own_ref, near_ref, b_ref, gain_ref, shift_ref, after_ref, n2_ref):
    value = start_ref[...] + (own_ref[...] + near_ref[...].astype(F32)) + b_ref[...].astype(F32)
    after_ref[...] = value
    xhat, _ = normalize(value)
    n2_ref[...] = (xhat * gain_ref[...].astype(F32) + shift_ref[...].astype(F32)).astype(BF16)


def second_norm_back(here_ref, near_ref, far_ref, after_ref, cot_ref, ok_ref, gain_ref, mid_ref, ga_ref, sums_ref):
    @pl.when(pl.program_id(0) == 0)
    def _():
        sums_ref[...] = jnp.zeros_like(sums_ref)

    grad = here_ref[...].astype(F32) + near_ref[...].astype(F32) + far_ref[...].astype(F32)
    xhat, rstd = normalize(after_ref[...])
    grad_after = cot_ref[...].astype(F32) * ok_ref[...]
    mid = grad_after + norm_back(grad, gain_ref[...].astype(F32), xhat, rstd)
    mid_ref[...] = mid
    ga_ref[...] = mid.astype(BF16)
    sums_ref[0] += eight(mid)
    sums_ref[1] += eight(grad * xhat)
    sums_ref[2] += eight(grad)
    sums_ref[3] += eight(grad_after)


def first_norm_back(own_ref, near_ref, start_ref, mid_ref, gain_ref, out_ref, sums_ref):
    @pl.when(pl.program_id(0) == 0)
    def _():
        sums_ref[...] = jnp.zeros_like(sums_ref)

    grad = own_ref[...] + near_ref[...].astype(F32)
    xhat, rstd = normalize(start_ref[...])
    out_ref[...] = (mid_ref[...] + norm_back(grad, gain_ref[...].astype(F32), xhat, rstd)).astype(BF16)
    sums_ref[0] += eight(grad * xhat)
    sums_ref[1] += eight(grad)


def down_out(act_n_ref, act_c_ref, w_ref, out_ref):
    out_ref[0] = mm(act_n_ref[...], w_ref[...]).astype(BF16)
    out_ref[1] = mm(act_c_ref[...], w_ref[...]).astype(BF16)


def down_in(act_o_ref, act_f_ref, after_ref, got_ref, b_ref, w_ref, base_ref, far_ref):
    down = mm(act_o_ref[...], w_ref[...]) + got_ref[0].astype(F32)
    base_ref[...] = after_ref[...] + down + b_ref[...].astype(F32)
    far_ref[...] = (mm(act_f_ref[...], w_ref[...]) + got_ref[1].astype(F32)).astype(BF16)


def finish(base_ref, far_ref, ok_ref, out_ref):
    out_ref[...] = ((base_ref[...] + far_ref[...].astype(F32)) * ok_ref[...]).astype(BF16)


def hand_on(in_ref, out_ref):
    out_ref[...] = in_ref[...]


def hand_on_all(*refs):
    count = len(refs) // 2
    for in_ref, out_ref in zip(refs[:count], refs[count:]):
        out_ref[...] = in_ref[...]


def handed(value, after):
    return run(hand_on, "hand_on", [value], [(value.shape, value.dtype)], after)


def small_first(two_ref, one_ref, out_ref):
    out_ref[...] = jnp.zeros_like(out_ref)
    rows = [two_ref[0], one_ref[0], one_ref[1], two_ref[1], two_ref[2], two_ref[3]]
    for at, part in enumerate(rows):
        out_ref[at:at + 1, :] = jnp.sum(part, axis=0, keepdims=True)


def small_second(own_ref, near_ref, bias_a_ref, bias_b_ref, send_ref, keep_ref):
    total = own_ref[...] + near_ref[...]
    wide = bias_a_ref.shape[1]
    for out_ref, bias_ref in ((send_ref, bias_b_ref), (keep_ref, bias_a_ref)):
        out_ref[...] = total
        out_ref[6:7, :wide] = bias_ref[0:1, :]
        out_ref[6:7, wide:2 * wide] = bias_ref[4:5, :]


def small_third(own_ref, far_ref, *refs):
    out_ref = refs[-1]
    out_ref[...] = own_ref[...] + far_ref[...]
    out_ref[7:8, :] = sum(jnp.sum(part[...], axis=0, keepdims=True) for part in refs[:-1])


def small_add(own_ref, far_ref, out_ref):
    out_ref[...] = own_ref[...] + far_ref[...]


def add_two(left_ref, right_ref, out_ref):
    out_ref[...] = add_low(left_ref[...], right_ref[...])


def token_products(count, based, side_ref, *refs):
    lefts, rights, rest = refs[:count], refs[count:2 * count], refs[2 * count:]
    total = sum(mm(left[...], right[...], TN) for left, right in zip(lefts, rights))
    if not based:
        rest[-1][...] = total
        return
    total = (total + rest[0][...]).astype(BF16)
    send_ref, keep_ref = rest[-2:]
    first = pl.program_id(0) < pl.num_programs(0) // 2

    @pl.when(first)
    def _():
        send_ref[...] = total

    @pl.when(jnp.logical_not(first))
    def _():
        keep_ref[...] = total


def token_call(sides, lefts, rights, base, after):
    tall, wide = lefts[0].shape[1], rights[0].shape[1]
    block = 256
    steps = tall // block

    def row(i, side_ref):
        return jnp.where(i < steps // 2, i + (1 - side_ref[0]) * (steps // 2), i - (1 - side_ref[0]) * (steps // 2))

    if base is None:
        outs = jax.ShapeDtypeStruct((tall, wide), F32)
        out_specs = pl.BlockSpec((block, wide), lambda i, side_ref: (row(i, side_ref), 0))
    else:
        outs = [jax.ShapeDtypeStruct((tall // 2, wide), BF16)] * 2
        out_specs = [
            pl.BlockSpec((block, wide), lambda i, _: (jnp.minimum(i, steps // 2 - 1), 0)),
            pl.BlockSpec((block, wide), lambda i, _: (jnp.maximum(i - steps // 2, 0), 0)),
        ]
    in_specs = [pl.BlockSpec((left.shape[0], block), lambda i, side_ref: (0, row(i, side_ref))) for left in lefts]
    in_specs += [pl.BlockSpec(right.shape, lambda i, _: (0, 0)) for right in rights]
    args = list(lefts) + list(rights)
    if base is not None:
        in_specs.append(pl.BlockSpec((block, wide), lambda i, side_ref: (row(i, side_ref), 0)))
        args.append(base)
    kernel = functools.partial(token_products, len(lefts), base is not None)
    return pl.pallas_call(
        chained(kernel, len(args) + 1),
        name="token_products",
        grid_spec=pltpu.PrefetchScalarGridSpec(
            num_scalar_prefetch=1,
            grid=(steps,),
            in_specs=in_specs + [pl.BlockSpec(memory_space=pl.ANY)],
            out_specs=out_specs,
        ),
        out_shape=outs,
        compiler_params=pltpu.CompilerParams(vmem_limit_bytes=40 * 2**20),
        cost_estimate=pl.CostEstimate(flops=60 * 10**9, bytes_accessed=10**9, transcendentals=0),
    )(sides, *args, after)


def three_products(x_ref, gp_ref, q_ref, kv_ref):
    q_ref[...] = mm(x_ref[...], gp_ref[0]).astype(BF16)
    for c in range(2):
        kv_ref[c] = mm(x_ref[...], gp_ref[c + 1]).astype(BF16)


def three_call(x_turned, gp, after):
    tall, seq = x_turned.shape
    wide = gp.shape[2]
    block = 256
    return run(
        three_products,
        "three_products",
        [x_turned, gp],
        [((tall, wide), BF16), ((2, tall, wide), BF16)],
        after,
        grid=(tall // block,),
        in_specs=[pl.BlockSpec((block, seq), lambda i: (i, 0)), pl.BlockSpec(gp.shape, lambda i: (0, 0, 0))],
        out_specs=[
            pl.BlockSpec((block, wide), lambda i: (i, 0)),
            pl.BlockSpec((2, block, wide), lambda i: (0, i, 0)),
        ],
    )


def turned_product(mixed_ref, ga_ref, out_ref):
    out_ref[...] = mm(ga_ref[...], mixed_ref[...], TN).astype(BF16)


def back_project(flip, core_ref, gp_a_ref, gp_b_ref, w_a_ref, w_b_ref, out_ref):
    rows = out_ref.shape[0]
    at = pl.ds(pl.multiple_of(jnp.bitwise_xor(core_ref[0], flip) * rows, rows), rows)
    out = sum(
        mm(gp_ref[c, at, :], w_ref[c], NT)
        for c in range(3)
        for gp_ref, w_ref in ((gp_a_ref, w_a_ref), (gp_b_ref, w_b_ref))
    )
    out_ref[...] = out.astype(out_ref.dtype)


def by_rows(kernel, name, args, outs, after, block=128):
    rows = args[0].shape[0]

    def spec(shape):
        if shape[0] == rows:
            return pl.BlockSpec((block,) + tuple(shape[1:]), lambda i: (i,) + (0,) * (len(shape) - 1))
        return pl.BlockSpec(tuple(shape), lambda i: (0,) * len(shape))

    return run(
        kernel,
        name,
        args,
        outs,
        after,
        grid=(rows // block,),
        in_specs=[spec(arg.shape) for arg in args],
        out_specs=[spec(shape) for shape, _ in outs],
        size=1,
    )


def fold(bit, last, side_ref, cur_ref, got_ref, *out_refs):
    if last:
        out_refs[0][...] = add_low(cur_ref[...], got_ref[...])
        return
    half = got_ref.shape[0] // 2
    for side, out_ref in ((1 - side_ref[bit], out_refs[0]), (side_ref[bit], out_refs[1])):
        at = pl.ds(pl.multiple_of(side * half, half), half)
        out_ref[...] = add_low(cur_ref[at, :], got_ref[at, :])


def begin_pair(paired, side_ref, *refs):
    send_ref, keep_ref = refs[-2:]
    if paired:
        parts = [(refs[0].at[c], refs[1].at[c]) for c in range(2)]
    else:
        parts = [refs[0:1], refs[1:3]]
    for side in range(2):

        @pl.when(side_ref[0] == side)
        def _():
            for part, out_ref in ((parts[1 - side], send_ref), (parts[side], keep_ref)):
                out_ref[...] = part[0][...] if len(part) == 1 else add_low(part[0][...], part[1][...])


def join(left_ref, right_ref, out_ref):
    rows = left_ref.shape[0]
    out_ref[:rows, :] = left_ref[...]
    out_ref[rows:, :] = right_ref[...]


def place(piece, spot_ref, own_ref, other_ref, out_ref):
    count = own_ref.shape[0] // piece
    steps = out_ref.shape[0] // piece
    for at in range(steps):
        apart = jnp.bitwise_xor(pl.program_id(0) * steps + at, spot_ref[0])
        rows = pl.ds(pl.multiple_of(jnp.bitwise_and(apart, count - 1) * piece, piece), piece)
        far_side = apart >= count
        into = slice(at * piece, (at + 1) * piece)

        @pl.when(far_side)
        def _():
            out_ref[into, :] = other_ref[rows, :].astype(F32)

        @pl.when(jnp.logical_not(far_side))
        def _():
            out_ref[into, :] = own_ref[rows, :].astype(F32)


def pieces(count, spot, own_ref, other_ref, first, steps):
    piece = own_ref.shape[0] // count
    for at in range(steps):
        apart = jnp.bitwise_xor(first + at, spot)
        rows = pl.ds(pl.multiple_of(jnp.bitwise_and(apart, count - 1) * piece, piece), piece)
        mine, others = own_ref[rows, :].astype(F32), other_ref[rows, :].astype(F32)
        yield at * piece, piece, jnp.where(apart >= count, others, mine)


def place_turned(count, spot_ref, own_ref, other_ref, w_out_ref, part_ref):
    for at, piece, value in pieces(count, spot_ref[0], own_ref, other_ref, 0, count):
        w_out_ref[:, at:at + piece] = value.T
    for at, piece, value in pieces(count, spot_ref[0], own_ref, other_ref, count, count):
        part_ref[at:at + piece, :] = value


def place_two(count, spot_ref, own_ref, other_ref, _, out_ref):
    for at, piece, value in pieces(count, spot_ref[0], own_ref, other_ref, pl.program_id(0) * count, count):
        out_ref[at:at + piece, :] = value


class Sum:
    def __init__(self, size, height, first=0):
        self.size, self.bits, self.height = size, size.bit_length() - 1, height
        me = lax.axis_index("dp")
        order = [(first + step) % self.bits for step in range(self.bits)]
        self.flips = [1 << b for b in order]
        sides = [(me // flip) % 2 for flip in self.flips]
        self.sides = jnp.stack(sides).astype(jnp.int32)
        self.spot = sum(side << (self.bits - 1 - step) for step, side in enumerate(sides))

    def begin(self, send, keep):
        self.keep, self.step = keep, 0
        self.sent = swap(send, "dp", self.size, self.flips[0])

    def begin_pairs(self, arrays, after):
        shape = arrays[0].shape[-2:]
        send, keep = run(
            functools.partial(begin_pair, len(arrays) == 2), "begin_pair", [self.sides] + list(arrays),
            [(shape, BF16)] * 2, after, scalars=1,
        )
        self.begin(send, keep)
        return keep

    def fold(self, after):
        if self.step >= self.bits:
            return after
        self.step += 1
        last = self.step == self.bits
        rows, columns = self.sent.shape
        kernel = functools.partial(fold, self.step, last)
        outs = [((rows, columns), BF16)] if last else [((rows // 2, columns), BF16)] * 2
        out = run(kernel, "fold", [self.sides, self.keep, self.sent], outs, after, scalars=1, cost=60)
        self.keep = out if last else out[1]
        send = out if last else out[0]
        self.sent = swap(send, "dp", self.size, self.flips[min(self.step, self.bits - 1)])
        return self.keep

    def spread(self, after):
        if self.step < self.bits:
            return after
        bit = 2 * self.bits - 2 - self.step
        rows, columns = self.keep.shape
        self.keep = run(join, "join", [self.keep, self.sent], [((2 * rows, columns), BF16)], after)
        self.sent = swap(self.keep, "dp", self.size, self.flips[bit])
        self.step += 1
        return self.keep

    def complete(self, after):
        while self.step < self.bits:
            after = self.fold(after)
        while self.step < 2 * self.bits - 1:
            after = self.spread(after)
        return after

    def place(self, after):
        after = self.complete(after)
        rows, columns = self.keep.shape
        piece = rows * 2 // self.size
        return run(
            functools.partial(place, piece),
            "place",
            [self.spot.reshape(1).astype(jnp.int32), self.keep, self.sent],
            [((2 * rows, columns), F32)],
            after,
            grid=(2,),
            size=1,
            in_specs=[
                pl.BlockSpec(memory_space=pltpu.SMEM),
                pl.BlockSpec((rows, columns), lambda i: (0, 0)),
                pl.BlockSpec((rows, columns), lambda i: (0, 0)),
            ],
            out_specs=[pl.BlockSpec((rows, columns), lambda i: (i, 0))],
        )[: self.height]

    def place_out(self, after):
        after = self.complete(after)
        rows, columns = self.keep.shape
        return run(
            functools.partial(place_turned, self.size // 2),
            "place_turned",
            [self.spot.reshape(1).astype(jnp.int32), self.keep, self.sent],
            [((columns, rows), F32), ((3 * rows, columns), F32)],
            after,
            grid=(1,),
            size=1,
            in_specs=[pl.BlockSpec(memory_space=pltpu.SMEM)]
            + [pl.BlockSpec((rows, columns), lambda i: (0, 0))] * 2,
            out_specs=[
                pl.BlockSpec((columns, rows), lambda i: (0, 0)),
                pl.BlockSpec((rows, columns), lambda i: (0, 0)),
            ],
        )

    def place_rest(self, into, after):
        after = self.complete(after)
        rows, columns = self.keep.shape
        return run(
            functools.partial(place_two, self.size // 2),
            "place_two",
            [self.spot.reshape(1).astype(jnp.int32), self.keep, self.sent, into],
            [((3 * rows, columns), F32)],
            after,
            grid=(2,),
            size=1,
            in_specs=[pl.BlockSpec(memory_space=pltpu.SMEM)]
            + [pl.BlockSpec((rows, columns), lambda i: (0, 0))] * 2
            + [pl.BlockSpec(memory_space=pl.ANY)],
            out_specs=[pl.BlockSpec((rows, columns), lambda i: (i + 1, 0))],
            aliases={3: 0},
        )


def gelu_and_slope(up):
    size = jnp.abs(up)
    t = 1.0 / (1.0 + (0.3275911 * 0.7071067811865476) * size)
    bell = jnp.exp(-0.5 * up * up)
    poly = t * (
        0.5 * 0.254829592
        + t * (0.5 * -0.284496736 + t * (0.5 * 1.421413741 + t * (0.5 * -1.453152027 + t * (0.5 * 1.061405429))))
    )
    tail = poly * bell
    cdf = jnp.where(up >= 0.0, 1.0 - tail, tail)
    return up * cdf, cdf + up * bell * 0.3989422804014327


def feed(n2_ref, gd_ref, ok_ref, w_up_ref, b_up_ref, w_down_ref, gn2_ref, act_ref, gup_ref, gb_ref):
    hidden = w_up_ref.shape[1]
    rows = n2_ref.shape[0]
    step = 256
    n2 = n2_ref[...]
    gd = gd_ref[...]
    ok = ok_ref[...]

    @pl.when(pl.program_id(0) == 0)
    def _():
        gb_ref[...] = jnp.zeros_like(gb_ref)

    for at in range(0, hidden, step):
        part = slice(at, at + step)
        up = mm(n2, w_up_ref[:, part]) + b_up_ref[:, part].astype(F32)
        grad_act = mm(gd, w_down_ref[part, :], NT)
        act, slope = gelu_and_slope(up)
        grad_up = (slope * (grad_act * ok)).astype(BF16)
        act_ref[:, part] = (act * ok).astype(BF16)
        gup_ref[:, part] = grad_up
        gb_ref[:, part] += jnp.sum(grad_up.astype(F32).reshape(rows // 8, 8, step), axis=0)
    gn2_ref[...] = mm(gup_ref[...], w_up_ref[...], NT).astype(BF16)


def feed_call(n2, gd, ok, w_up, b_up, w_down, after):
    rows, hidden = n2.shape[0], w_up.shape[1]
    block = 256
    tokens = pl.BlockSpec((block, D), lambda i: (i, 0))
    tall = pl.BlockSpec((block, hidden), lambda i: (i, 0))

    def fixed(shape):
        return pl.BlockSpec(shape, lambda i: (0, 0))

    return run(
        feed,
        "feed",
        [n2, gd, ok, w_up, b_up, w_down],
        [((rows, D), BF16), ((rows, hidden), BF16), ((rows, hidden), BF16), ((8, hidden), F32)],
        after,
        grid=(rows // block,),
        in_specs=[tokens, tokens, pl.BlockSpec((block, 1), lambda i: (i, 0)), fixed((D, hidden)), fixed((1, hidden)), fixed((hidden, D))],
        out_specs=[tokens, tall, tall, fixed((8, hidden))],
    )


def swap(value, axis, size, flip):
    return lax.ppermute(value, axis, [(i, i ^ flip) for i in range(size)])


def add_low(left, right):
    return (left.astype(F32) + right.astype(F32)).astype(BF16)


def sum_over(value, axis, size):
    flip = 1
    while flip < size:
        value = value + swap(value, axis, size, flip)
        flip *= 2
    return value


def on_device(
    dp_size,
    mp_size,
    tokens,
    segment_ids,
    valid_mask,
    patch_index,
    gsd_index,
    w_qkv,
    bias_qv,
    w_out,
    b_out,
    gain_one,
    shift_one,
    gain_two,
    shift_two,
    w_up,
    b_up,
    w_down,
    b_down,
    cotangent,
):
    own_rows = tokens.shape[0]
    mp = lax.axis_index("mp")
    core = mp % 2
    row = mp // 2

    def near(value):
        return swap(value, "mp", mp_size, 1)

    def far(value):
        return swap(value, "mp", mp_size, 2)

    core_s = core.reshape(1).astype(jnp.int32)
    down_sum, up_sum = Sum(dp_size, w_down.shape[0]), Sum(dp_size, w_up.shape[0])
    first_sum, second_sum = Sum(dp_size, 2 * D), Sum(dp_size, 2 * D)
    sides = down_sum.sides

    cot_near = near(cotangent)
    inputs = [segment_ids, valid_mask, patch_index, gsd_index]
    shape = (3, D // 4, w_qkv.shape[2])
    piece_a, piece_b = run(cut, "cut", [sides, w_qkv], [(shape, BF16)] * 2, None, scalars=1, size=1)
    segment_ids, valid_mask, patch_index, gsd_index = run(
        hand_on_all, "hand_on_all", inputs, [(part.shape, part.dtype) for part in inputs], piece_b, size=1
    )
    far_bias = far(bias_qv)
    far_a, far_b = far(piece_a), far(piece_b)

    own_start = mp * own_rows
    level = image_levels(segment_ids, gsd_index)
    codes = jnp.stack([patch_index // GRID, patch_index % GRID]) * GSDS + level
    own_codes = lax.dynamic_slice_in_dim(codes.reshape(2, -1, 1), own_start, own_rows, axis=1)
    all_valid = valid_mask.reshape(-1, 1).astype(F32)

    def valid_of(flip):
        at = jnp.bitwise_xor(mp, flip) * own_rows
        return lax.dynamic_slice_in_dim(all_valid, at, own_rows)

    own_valid = valid_of(0)

    row_seg = lax.dynamic_index_in_dim(segment_ids, row, 0, keepdims=True)
    row_ok = lax.dynamic_index_in_dim(valid_mask, row, 0, keepdims=True)
    seg_k = jnp.where(row_ok == 1, row_seg, -1)
    seg_q = row_seg.reshape(-1, 1)

    start_sum, normed = by_rows(
        front, "front",
        [tokens, own_codes[0], own_codes[1], code_table(), gain_one[None], shift_one[None]],
        [(tokens.shape, F32), (tokens.shape, BF16)], [segment_ids, cot_near],
    )
    half = (own_rows, D)
    w_out_sent, a_pass = run(
        hand_on_all, "hand_on_all", [w_out, far_a], [(w_out.shape, BF16), (far_a.shape, BF16)], normed, cost=60
    )
    far_out = far(w_out_sent)
    other_a = swap(a_pass, "dp", dp_size, 1)
    normed_row = run(in_row, "in_row", [core_s, normed, near(normed)], [((2 * own_rows, D), BF16)], a_pass, scalars=1)
    b_pass, cot_sent = run(
        hand_on_all, "hand_on_all", [far_b, cotangent], [(far_b.shape, BF16), (half, BF16)], normed_row
    )
    other_b = swap(b_pass, "dp", dp_size, 1)
    cot_far = far(cot_sent)

    qkv_a, mixed_a, lse_a = forward_call(sides, seg_q, seg_k, normed_row, bias_qv, [w_qkv], cot_sent)
    pieces_b = [a_pass, b_pass, other_a, other_b]
    qkv_b, mixed_b, lse_b = forward_call(sides, seg_q, seg_k, normed_row, far_bias, pieces_b, lse_a)
    operands = [core_s, mixed_a, mixed_b, w_out, far_out]
    attn_near = run(functools.partial(project_out, 1), "project_out", operands, [(half, BF16)], lse_b, scalars=1)
    attn_own = run(functools.partial(project_out, 0), "project_out", operands, [(half, F32)], attn_near, scalars=1)
    after_attn, n2 = by_rows(
        second_norm, "second_norm",
        [start_sum, attn_own, near(attn_near), b_out[None], gain_two[None], shift_two[None]],
        [(half, F32), (half, BF16)], attn_own,
    )
    n2_far = far(n2)
    n2_near = near(n2)

    b_up_row = b_up[None, :]
    gn2_o, act_o, gup_o, gb_o = feed_call(n2, cotangent, own_valid, w_up, b_up_row, w_down, n2)
    gn2_n, act_n, gup_n, gb_n = feed_call(n2_near, cot_near, valid_of(1), w_up, b_up_row, w_down, gb_o)
    from_near = near(gn2_n)
    down_here = token_call(sides, (act_o, act_n), (cotangent, cot_near), None, gb_n)
    cot_pass = handed(cot_far, [down_here, from_near])
    cot_cross = near(cot_pass)
    up_here = token_call(sides, (n2, n2_near), (gup_o, gup_n), None, cot_pass)
    n2_pass = handed(n2_far, up_here)
    n2_cross = near(n2_pass)
    gn2_f, act_f, gup_f, gb_f = feed_call(n2_pass, cot_pass, valid_of(2), w_up, b_up_row, w_down, n2_pass)
    gn2_c, act_c, gup_c, gb_c = feed_call(n2_cross, cot_cross, valid_of(3), w_up, b_up_row, w_down, gb_f)
    cross_gn2 = near(gn2_c)
    down_send, down_keep = token_call(sides, (act_f, act_c), (cot_pass, cot_cross), down_here, gb_c)
    down_sum.begin(down_send, down_keep)
    to_far = by_rows(add_two, "add_two", [gn2_f, cross_gn2], [(half, BF16)], down_keep)
    from_far = far(to_far)
    up_send, up_keep = token_call(sides, (n2_pass, n2_cross), (gup_f, gup_c), up_here, to_far)
    up_sum.begin(up_send, up_keep)
    down_sent = run(down_out, "down_out", [act_n, act_c, w_down], [((2,) + half, BF16)], up_keep)
    far_qkv = run(assemble, "assemble", [sides] + pieces_b, [(w_qkv.shape, BF16)], down_sent, scalars=1, cost=60)

    down_base, down_far = run(
        down_in, "down_in",
        [act_o, act_f, after_attn, near(down_sent), b_down[None], w_down],
        [(half, F32), (half, BF16)], far_qkv,
    )
    x_turned = run(turn, "turn", [normed_row], [((D, 2 * own_rows), BF16)], down_base)
    wide = w_qkv.shape[2]
    turned = [((D, wide), BF16)]
    tile = [((8, D), F32)]
    flips = [1 << b for b in range(dp_size.bit_length() - 1)]
    operands = [core_s, None, None, w_qkv, far_qkv]
    last = x_turned
    mid, ga, sums_two = by_rows(
        second_norm_back, "second_norm_back",
        [gn2_o, from_near, from_far, after_attn, cotangent, own_valid, gain_two[None]],
        [(half, F32), (half, BF16), ((4, 8, D), F32)], last,
    )
    last = ga
    last = down_sum.fold(last)
    last = ga_row = run(in_row, "in_row", [core_s, ga, near(ga)], [((2 * own_rows, D), BF16)], last, scalars=1)
    last = gw_out_b = run(turned_product, "turned_product", [mixed_b, ga_row], turned, last)
    far_out_grad = far(gw_out_b)
    last = gw_out_a = run(turned_product, "turned_product", [mixed_a, ga_row], turned, last)
    gp_b, bias_b = backward_call(seg_q, seg_k, ga_row, far_out, qkv_b, lse_b, last)
    last = bias_b
    q_b, kv_b = three_call(x_turned, gp_b, last)
    far_q, far_kv = far(q_b), far(kv_b)
    last = q_b
    last = out_both = by_rows(add_two, "add_two", [gw_out_a, far_out_grad], [((D, wide), BF16)], last, block=512)
    last = down_sum.fold(last)
    last = up_sum.fold(last)
    gp_a, bias_a = backward_call(seg_q, seg_k, ga_row, w_out, qkv_a, lse_a, last)
    last = bias_a
    last = down_sum.fold(last)
    q_a, kv_a = three_call(x_turned, gp_a, last)
    last = q_a
    last = first_sum.begin_pairs([out_both, q_a, far_q], last)
    operands[1:3] = gp_a, gp_b
    last = gn_near = run(functools.partial(back_project, 1), "back_project", operands, [(half, BF16)], last, scalars=1)
    last = up_sum.fold(last)
    last = down_sum.spread(last)
    last = gn_own = run(functools.partial(back_project, 0), "back_project", operands, [(half, F32)], last, scalars=1)
    last = second_sum.begin_pairs([kv_a, far_kv], last)
    grad_tokens, sums_one = by_rows(
        first_norm_back, "first_norm_back",
        [gn_own, near(gn_near), start_sum, mid, gain_one[None]],
        [(half, BF16), ((2, 8, D), F32)], last,
    )
    last = sums_one
    last = up_sum.fold(last)
    last = first_sum.fold(last)
    last = down_sum.spread(last)
    last = small = run(small_first, "small_first", [sums_two, sums_one], tile, last)
    small_got = near(small)
    last = second_sum.fold(last)
    last = up_sum.spread(last)
    send, small = run(small_second, "small_second", [small, small_got, bias_a, bias_b], tile * 2, last)
    small_got = far(send)
    last = small
    last = first_sum.fold(last)
    last = second_sum.fold(last)
    last = small = run(small_third, "small_third", [small, small_got, gb_o, gb_n, gb_f, gb_c], tile, last)
    small_got = swap(small, "dp", dp_size, flips[0])
    last = up_sum.spread(last)
    last = first_sum.fold(last)
    last = grad_w_down = down_sum.place(last)
    last = second_sum.fold(last)
    last = first_sum.spread(last)
    last = down_sent = handed(down_far, last)
    down_got = far(down_sent)
    last = first_sum.spread(last)
    last = second_sum.spread(last)
    last = grad_w_up = up_sum.place(last)
    last = small = run(small_add, "small_add", [small, small_got], tile, last)
    small_got = swap(small, "dp", dp_size, flips[1])
    last = second_sum.spread(last)
    last = small = run(small_add, "small_add", [small, small_got], tile, last)
    small_got = swap(small, "dp", dp_size, flips[2])
    last = layer_out = by_rows(finish, "finish", [down_base, down_got, own_valid], [(half, BF16)], last)
    for flip in flips[3:]:
        last = small = run(small_add, "small_add", [small, small_got], tile, last)
        small_got = swap(small, "dp", dp_size, flip)
    last = small = run(small_add, "small_add", [small, small_got], tile, last)
    grad_w_out, grad_w_qkv = first_sum.place_out(last)
    last = grad_w_out
    grad_w_qkv = second_sum.place_rest(grad_w_qkv, last).reshape(w_qkv.shape)
    grad_bias_qv = small[6, : 2 * wide].reshape(2, wide)
    grad_b_up = small[7]
    return (
        layer_out,
        grad_tokens,
        grad_w_qkv,
        grad_bias_qv,
        grad_w_out,
        small[0],
        small[1],
        small[2],
        small[3],
        small[4],
        grad_w_up,
        grad_b_up,
        grad_w_down,
        small[5],
    )


def solution(mesh):
    return jax.shard_map(
        functools.partial(on_device, mesh.shape["dp"], mesh.shape["mp"]),
        mesh=mesh,
        in_specs=(
            P(("dp", "mp"), None),
            P("dp", None),
            P("dp", None),
            P("dp", None),
            P("dp", None),
            P(None, None, "mp"),
            P(None, "mp"),
            P("mp", None),
            P(),
            P(),
            P(),
            P(),
            P(),
            P(None, "mp"),
            P("mp"),
            P("mp", None),
            P(),
            P(("dp", "mp"), None),
        ),
        out_specs=(
            P(("dp", "mp"), None),
            P(("dp", "mp"), None),
            P(None, None, "mp"),
            P(None, "mp"),
            P("mp", None),
            P(),
            P(),
            P(),
            P(),
            P(),
            P(None, "mp"),
            P("mp"),
            P("mp", None),
            P(),
        ),
        check_vma=False,
    )
```

```python
import functools
import jax
import jax.numpy as jnp
from jax import lax
from jax.experimental import pallas as pl
from jax.experimental.pallas import tpu as pltpu
from jax.sharding import PartitionSpec as P

D = 1024
HEAD = 64
SEGS = 16
GRID = 14
GSDS = 8
EPSILON = 1e-06
MASKED = -1000000000.0
SCALE = HEAD ** (-0.5)
BQ = 128
PAIR = 2 * HEAD
F32 = jnp.float32
BF16 = jnp.bfloat16
NN = (((1,), (0,)), ((), ()))
NT = (((1,), (1,)), ((), ()))
TN = (((0,), (0,)), ((), ()))


def mm(left, right, dims=NN):
    return lax.dot_general(left, right, dims, preferred_element_type=F32)


def image_levels(segment_ids, gsd_index):
    in_image = segment_ids[..., None] == jnp.arange(SEGS, dtype=jnp.int32)
    return jnp.sum(jnp.where(in_image, gsd_index[:, None, :], 0), axis=-1)


def code_table():
    quarter = D // 4
    frequency = 1.0 / 10000.0 ** (jnp.arange(quarter, dtype=jnp.float32) / quarter)
    ratio = 2.0 ** (0.5 * jnp.arange(GSDS, dtype=jnp.float32) - 1.0)
    place = jnp.arange(16, dtype=jnp.float32)
    angle = (place[:, None] * ratio[None, :]).reshape(-1, 1) * frequency
    return jnp.concatenate([jnp.sin(angle), jnp.cos(angle)], axis=-1)


def front(tokens_ref, row_ref, col_ref, table_ref, gain_ref, shift_ref, start_ref, normed_ref):
    high = table_ref[...].astype(BF16)
    rest = table_ref[...] - high.astype(F32)
    middle = rest.astype(BF16)
    low = (rest - middle.astype(F32)).astype(BF16)
    spots = lax.broadcasted_iota(jnp.int32, (tokens_ref.shape[0], table_ref.shape[0]), 1)
    half = table_ref.shape[1]
    for at, index_ref in ((0, row_ref), (half, col_ref)):
        chosen = (spots == index_ref[...]).astype(F32).astype(BF16)
        code = (mm(chosen, low) + mm(chosen, middle)) + mm(chosen, high)
        start_ref[:, at:at + half] = tokens_ref[:, at:at + half].astype(F32) + code
    xhat, _ = normalize(start_ref[...])
    normed_ref[...] = (xhat * gain_ref[...].astype(F32) + shift_ref[...].astype(F32)).astype(BF16)


def normalize(values):
    row_mean = jnp.mean(values, axis=-1, keepdims=True)
    centred = values - row_mean
    row_var = jnp.mean(centred * centred, axis=-1, keepdims=True)
    rstd = lax.rsqrt(row_var + EPSILON)
    return centred * rstd, rstd


def norm_back(grad, gain, xhat, rstd):
    scaled = grad * gain
    mean_scaled = jnp.mean(scaled, axis=-1, keepdims=True)
    mean_along = jnp.mean(scaled * xhat, axis=-1, keepdims=True)
    return rstd * (scaled - mean_scaled - xhat * mean_along)


def window_start(block, seq, width):
    return min(max(block * BQ - BQ, 0), seq - width)


def fill_bias(seg_q_ref, seg_k_ref, bias_ref, seq, width):
    for block in range(seq // BQ):
        start = window_start(block, seq, width)
        seg_q = seg_q_ref[block * BQ:(block + 1) * BQ, :]
        seg_k = seg_k_ref[:, start:start + width]
        row = lax.broadcasted_iota(jnp.int32, (BQ, width), 0) + block * BQ
        col = lax.broadcasted_iota(jnp.int32, (BQ, width), 1) + start
        allowed = (seg_q == seg_k) | (row == col)
        bias_ref[block] = jnp.where(allowed, 0.0, MASKED)


def split_heads(tile):
    low = lax.broadcasted_iota(jnp.int32, tile.shape, 1) < HEAD
    zero = jnp.zeros_like(tile)
    return jnp.concatenate([jnp.where(low, tile, zero), jnp.where(low, zero, tile)], axis=0)


def join_heads(stacked):
    half = stacked.shape[0] // 2
    low = lax.broadcasted_iota(jnp.int32, (half, PAIR), 1) < HEAD
    return jnp.where(low, stacked[:half], stacked[half:])


def piece_places(side_ref, w_refs, depth):
    if len(w_refs) == 1:
        return [(slice(None), w_refs[0])]
    rows = depth // 4
    starts = [side_ref[0] * 2, side_ref[0] * 2 + 1, (1 - side_ref[0]) * 2, (1 - side_ref[0]) * 2 + 1]
    return [(pl.ds(pl.multiple_of(at * rows, rows), rows), w_ref) for at, w_ref in zip(starts, w_refs)]


def assemble(side_ref, *refs):
    out_ref = refs[-1]
    for at, w_ref in piece_places(side_ref, refs[:-1], out_ref.shape[1]):
        out_ref[:, at, :] = w_ref[...]


def turn(in_ref, out_ref):
    out_ref[...] = in_ref[...].T


def cut(side_ref, w_ref, *out_refs):
    rows = w_ref.shape[1] // 4
    for piece, out_ref in enumerate(out_refs):
        at = pl.ds(pl.multiple_of((side_ref[0] * 2 + piece) * rows, rows), rows)
        out_ref[...] = w_ref[:, at, :]


def in_row(core_ref, own_ref, other_ref, out_ref):
    rows = own_ref.shape[0]
    for side, in_ref in ((core_ref[0], own_ref), (1 - core_ref[0], other_ref)):
        out_ref[pl.ds(pl.multiple_of(side * rows, rows), rows), :] = in_ref[...]


def in_row_pieces(core_ref, own1_ref, own2_ref, other1_ref, other2_ref, out_ref):
    rows = own1_ref.shape[0]
    for side, refs in ((core_ref[0], (own1_ref, own2_ref)), (1 - core_ref[0], (other1_ref, other2_ref))):
        for piece, in_ref in enumerate(refs):
            at = (side * 2 + piece) * rows
            out_ref[pl.ds(pl.multiple_of(at, rows), rows), :] = in_ref[...]


def attend_forward(side_ref, seg_q_ref, seg_k_ref, x_ref, b_ref, *refs):
    w_refs, (qkv_ref, mixed_ref, lse_ref, bias_ref) = refs[:-4], refs[-4:]
    seq = x_ref.shape[0]
    width = bias_ref.shape[2]
    wide = w_refs[0].shape[2]
    fill_bias(seg_q_ref, seg_k_ref, bias_ref, seq, width)
    for c in range(3):
        for r in range(0, seq, 256):
            out = sum(
                mm(x_ref[r:r + 256, at], w_ref[c]) for at, w_ref in piece_places(side_ref, w_refs, x_ref.shape[1])
            )
            if c != 1:
                out = out + b_ref[c // 2:c // 2 + 1, :].astype(F32)
            qkv_ref[c, r:r + 256, :] = out.astype(BF16)
    lane = lax.broadcasted_iota(jnp.int32, (BQ, PAIR), 1)
    pairs = range(wide // PAIR)
    for block in range(seq // BQ):
        start = window_start(block, seq, width)
        rows = slice(block * BQ, (block + 1) * BQ)
        keys = slice(start, start + width)
        bias = bias_ref[block]
        bias = jnp.concatenate([bias, bias], axis=0)
        lanes = [slice(pair * PAIR, (pair + 1) * PAIR) for pair in pairs]
        queries = [split_heads(qkv_ref[0, rows, at] * SCALE) for at in lanes]
        scores = [mm(queries[p], qkv_ref[1, keys, lanes[p]], NT) + bias for p in pairs]
        row_max = [jnp.max(part, axis=-1, keepdims=True) for part in scores]
        weight = [jnp.exp(scores[p] - row_max[p]) for p in pairs]
        mixed = [mm(weight[p].astype(BF16), qkv_ref[2, keys, lanes[p]]) for p in pairs]
        total = [jnp.sum(part, axis=-1, keepdims=True) for part in weight]
        lse_tile = jnp.zeros((BQ, PAIR), F32)
        for p in pairs:
            mixed_ref[rows, lanes[p]] = join_heads(mixed[p] * (1.0 / total[p])).astype(BF16)
            lse = row_max[p] + jnp.log(total[p])
            lse_tile = jnp.where(lane == 2 * p, lse[:BQ], lse_tile)
            lse_tile = jnp.where(lane == 2 * p + 1, lse[BQ:], lse_tile)
        lse_ref[rows, :] = lse_tile


def attend_backward(
    seg_q_ref, seg_k_ref, ga_ref, w_out_ref, qkv_ref, lse_ref, out_ref, sums_ref, bias_ref, gm_ref, acc_ref
):
    seq = ga_ref.shape[0]
    width = bias_ref.shape[2]
    wide = w_out_ref.shape[0]
    fill_bias(seg_q_ref, seg_k_ref, bias_ref, seq, width)
    for r in range(0, seq, 256):
        gm_ref[r:r + 256, :] = mm(ga_ref[r:r + 256, :], w_out_ref[...], NT).astype(BF16)
    acc_ref[...] = jnp.zeros_like(acc_ref)
    for block in range(seq // BQ):
        start = window_start(block, seq, width)
        rows = slice(block * BQ, (block + 1) * BQ)
        keys = slice(start, start + width)
        bias = bias_ref[block]
        bias = jnp.concatenate([bias, bias], axis=0)
        lse_tile = lse_ref[rows, :]
        pairs = range(wide // PAIR)
        lanes = [slice(pair * PAIR, (pair + 1) * PAIR) for pair in pairs]
        queries = [split_heads(qkv_ref[0, rows, at] * SCALE) for at in lanes]
        grad_mixed = [split_heads(gm_ref[rows, at]) for at in lanes]
        key_rows = [qkv_ref[1, keys, at] for at in lanes]
        scores = [mm(queries[p], key_rows[p], NT) + bias for p in pairs]
        grad_prob = [mm(grad_mixed[p], qkv_ref[2, keys, lanes[p]], NT) for p in pairs]
        lse = [
            jnp.concatenate([lse_tile[:, 2 * p:2 * p + 1], lse_tile[:, 2 * p + 1:2 * p + 2]], axis=0)
            for p in pairs
        ]
        prob = [jnp.exp(scores[p] - lse[p]) for p in pairs]
        along = [jnp.sum(prob[p] * grad_prob[p], axis=-1, keepdims=True) for p in pairs]
        grad_scores = [(prob[p] * (grad_prob[p] - along[p])).astype(BF16) for p in pairs]
        for p in pairs:
            acc_ref[1, keys, lanes[p]] += mm(prob[p].astype(BF16), grad_mixed[p], TN)
        for p in pairs:
            out_ref[0, rows, lanes[p]] = (join_heads(mm(grad_scores[p], key_rows[p])) * SCALE).astype(BF16)
            acc_ref[0, keys, lanes[p]] += mm(grad_scores[p], queries[p], TN)
    out_ref[1] = acc_ref[0].astype(BF16)
    out_ref[2] = acc_ref[1].astype(BF16)
    for at, c in enumerate((0, 2)):
        total = jnp.sum(out_ref[c].astype(F32), axis=0, keepdims=True)
        sums_ref[4 * at:4 * at + 4, :] = jnp.concatenate([total, jnp.zeros((3, wide), F32)], axis=0)


def chained(kernel, count, extra=1):
    def body(*refs):
        kernel(*refs[:count], *refs[count + extra:])

    return body


def with_token(kernel):
    def body(*refs):
        kernel(*refs[:-1])
        refs[-1][...] = jnp.zeros_like(refs[-1])

    return body


def run(kernel, name, args, outs, after, scalars=0, grid=None, in_specs=None, out_specs=None, scratch=(), aliases=None, cost=15, size=10**9, token=False):
    vmem = pl.BlockSpec(memory_space=pltpu.VMEM)
    if in_specs is None:
        in_specs = [pl.BlockSpec(memory_space=pltpu.SMEM)] * scalars + [vmem] * (len(args) - scalars)
    if out_specs is None:
        out_specs = [vmem] * len(outs)
    outs, out_specs = list(outs), list(out_specs)
    if token:
        outs.append(((8, 128), F32))
        out_specs.append(pl.BlockSpec((8, 128), lambda *_: (0, 0)) if grid is not None else vmem)
        kernel = with_token(kernel)
    if after is not None:
        behind = list(after) if isinstance(after, (list, tuple)) else [after]
        kernel = chained(kernel, len(args), len(behind))
        args = list(args) + behind
        in_specs = list(in_specs) + [pl.BlockSpec(memory_space=pl.ANY)] * len(behind)
    result = pl.pallas_call(
        kernel,
        name=name,
        grid=grid if grid is not None else (),
        out_shape=tuple(jax.ShapeDtypeStruct(shape, dtype) for shape, dtype in outs),
        in_specs=in_specs,
        out_specs=tuple(out_specs),
        scratch_shapes=list(scratch),
        input_output_aliases=aliases or {},
        compiler_params=pltpu.CompilerParams(vmem_limit_bytes=26 * 2**20),
        cost_estimate=pl.CostEstimate(flops=cost * 10**9, bytes_accessed=size, transcendentals=0),
    )(*args)
    return result if len(outs) > 1 else result[0]


def forward_call(sides, seg_q, seg_k, x, b, pieces_of, after):
    seq, wide = x.shape[0], pieces_of[0].shape[2]
    width = min(3 * BQ, seq)
    return run(
        attend_forward,
        "attend_forward",
        [sides, seg_q, seg_k, x, b] + list(pieces_of),
        [((3, seq, wide), BF16), ((seq, wide), BF16), ((seq, PAIR), F32)],
        after,
        cost=60,
        scalars=1,
        scratch=[pltpu.VMEM((seq // BQ, BQ, width), F32)],
    )


def backward_call(seg_q, seg_k, ga, w_out, qkv, lse, after):
    seq, wide = ga.shape[0], w_out.shape[0]
    width = min(3 * BQ, seq)
    return run(
        attend_backward,
        "attend_backward",
        [seg_q, seg_k, ga, w_out, qkv, lse],
        [((3, seq, wide), BF16), ((8, wide), F32)],
        after,
        scratch=[
            pltpu.VMEM((seq // BQ, BQ, width), F32),
            pltpu.VMEM((seq, wide), BF16),
            pltpu.VMEM((2, seq, wide), F32),
        ],
    )


def eight(values):
    return jnp.sum(values.reshape(values.shape[0] // 8, 8, values.shape[1]), axis=0)


def project_out(flip, core_ref, mixed_a_ref, mixed_b_ref, w_a_ref, w_b_ref, out_ref):
    rows = out_ref.shape[0]
    at = pl.ds(pl.multiple_of(jnp.bitwise_xor(core_ref[0], flip) * rows, rows), rows)
    out = mm(mixed_a_ref[at, :], w_a_ref[...]) + mm(mixed_b_ref[at, :], w_b_ref[...])
    out_ref[...] = out.astype(out_ref.dtype)


def second_norm(start_ref, own_ref, near_ref, b_ref, gain_ref, shift_ref, after_ref, n2_ref):
    value = start_ref[...] + (own_ref[...] + near_ref[...].astype(F32)) + b_ref[...].astype(F32)
    after_ref[...] = value
    xhat, _ = normalize(value)
    n2_ref[...] = (xhat * gain_ref[...].astype(F32) + shift_ref[...].astype(F32)).astype(BF16)


def second_norm_back(here_ref, near_ref, far_ref, after_ref, cot_ref, ok_ref, gain_ref, mid_ref, ga_ref, sums_ref):
    @pl.when(pl.program_id(0) == 0)
    def _():
        sums_ref[...] = jnp.zeros_like(sums_ref)

    grad = here_ref[...].astype(F32) + near_ref[...].astype(F32) + far_ref[...].astype(F32)
    xhat, rstd = normalize(after_ref[...])
    grad_after = cot_ref[...].astype(F32) * ok_ref[...]
    mid = grad_after + norm_back(grad, gain_ref[...].astype(F32), xhat, rstd)
    mid_ref[...] = mid
    ga_ref[...] = mid.astype(BF16)
    sums_ref[0] += eight(mid)
    sums_ref[1] += eight(grad * xhat)
    sums_ref[2] += eight(grad)
    sums_ref[3] += eight(grad_after)


def first_norm_back(own_ref, near_ref, start_ref, mid1_ref, mid2_ref, gain_ref, out_ref, sums_ref):
    @pl.when(pl.program_id(0) == 0)
    def _():
        sums_ref[...] = jnp.zeros_like(sums_ref)

    grad = own_ref[...] + near_ref[...].astype(F32)
    xhat, rstd = normalize(start_ref[...])
    mid = jnp.where(pl.program_id(0) * 2 < pl.num_programs(0), mid1_ref[...], mid2_ref[...])
    out_ref[...] = (mid + norm_back(grad, gain_ref[...].astype(F32), xhat, rstd)).astype(BF16)
    sums_ref[0] += eight(grad * xhat)
    sums_ref[1] += eight(grad)


def down_out(act_n_ref, act_c1_ref, act_c2_ref, w_ref, out_ref):
    half = act_c1_ref.shape[0]
    out_ref[0] = mm(act_n_ref[...], w_ref[...]).astype(BF16)
    out_ref[1, :half, :] = mm(act_c1_ref[...], w_ref[...]).astype(BF16)
    out_ref[1, half:, :] = mm(act_c2_ref[...], w_ref[...]).astype(BF16)


def down_in(act_o_ref, act_f1_ref, act_f2_ref, after1_ref, after2_ref, got_ref, b_ref, w_ref, base_ref, far_ref):
    half = act_f1_ref.shape[0]
    for piece, act_ref, after_ref in ((0, act_f1_ref, after1_ref), (1, act_f2_ref, after2_ref)):
        at = slice(piece * half, (piece + 1) * half)
        down = mm(act_o_ref[at, :], w_ref[...]) + got_ref[0, at, :].astype(F32)
        base_ref[at, :] = after_ref[...] + down + b_ref[...].astype(F32)
        far_ref[at, :] = (mm(act_ref[...], w_ref[...]) + got_ref[1, at, :].astype(F32)).astype(BF16)


def finish(base_ref, far_ref, ok_ref, out_ref):
    out_ref[...] = ((base_ref[...] + far_ref[...].astype(F32)) * ok_ref[...]).astype(BF16)


def hand_on(in_ref, out_ref):
    out_ref[...] = in_ref[...]


def hand_on_all(*refs):
    count = len(refs) // 2
    for in_ref, out_ref in zip(refs[:count], refs[count:]):
        out_ref[...] = in_ref[...]


def handed(value, after):
    return run(hand_on, "hand_on", [value], [(value.shape, value.dtype)], after)


def small_first(two_ref, more_ref, one_ref, out_ref):
    out_ref[...] = jnp.zeros_like(out_ref)
    two = [two_ref[at] + more_ref[at] for at in range(4)]
    rows = [two[0], one_ref[0], one_ref[1], two[1], two[2], two[3]]
    for at, part in enumerate(rows):
        out_ref[at:at + 1, :] = jnp.sum(part, axis=0, keepdims=True)


def small_second(own_ref, near_ref, bias_a_ref, bias_b_ref, send_ref, keep_ref):
    total = own_ref[...] + near_ref[...]
    wide = bias_a_ref.shape[1]
    for out_ref, bias_ref in ((send_ref, bias_b_ref), (keep_ref, bias_a_ref)):
        out_ref[...] = total
        out_ref[6:7, :wide] = bias_ref[0:1, :]
        out_ref[6:7, wide:2 * wide] = bias_ref[4:5, :]


def small_third(own_ref, far_ref, *refs):
    out_ref = refs[-1]
    out_ref[...] = own_ref[...] + far_ref[...]
    out_ref[7:8, :] = sum(jnp.sum(part[...], axis=0, keepdims=True) for part in refs[:-1])


def small_add(own_ref, far_ref, out_ref):
    out_ref[...] = own_ref[...] + far_ref[...]


def add_two(left_ref, right_ref, out_ref):
    out_ref[...] = add_low(left_ref[...], right_ref[...])


def token_products(pieces_of, form, side_ref, *refs):
    count = len(pieces_of)
    lefts, rights, rest = refs[:count], refs[count:2 * count], refs[2 * count:]
    block = 256
    steps = lefts[0].shape[1] // block
    for i in range(steps):
        first = i < steps // 2
        if form == "base":
            row = i
        else:
            row = i % (steps // 2) + (1 - side_ref[0] if first else side_ref[0]) * (steps // 2)
        at = pl.ds(row * block if form == "base" else pl.multiple_of(row * block, block), block)
        total = sum(
            mm(
                left[lp * tokens:(lp + 1) * tokens, at],
                right[rp * tokens:(rp + 1) * tokens, :],
                TN,
            )
            for left, right, (lp, rp, tokens) in zip(lefts, rights, pieces_of)
        )
        into = slice(i % (steps // 2) * block, (i % (steps // 2) + 1) * block)
        if form == "base":
            rest[0][at, :] = total
            continue
        if form == "based":
            total = total + rest[0][at, :]
        rest[-2 if first else -1][into, :] = total.astype(BF16)


def token_call(sides, pairs, base, after):
    tall, wide = pairs[0][0].shape[1], pairs[0][2].shape[1]
    form = "base" if base is True else "full" if base is None else "based"
    args = [sides] + [pair[0] for pair in pairs] + [pair[2] for pair in pairs]
    if form == "based":
        args.append(base)
    outs = [((tall, wide), F32)] if form == "base" else [((tall // 2, wide), BF16)] * 2
    pieces_of = [(pair[1], pair[3], pair[4]) for pair in pairs]
    kernel = functools.partial(token_products, pieces_of, form)
    return run(kernel, "token_products", args, outs, after, scalars=1, cost=60)


def three_products(x_ref, gp_ref, q_ref, kv_ref):
    q_ref[...] = mm(x_ref[...], gp_ref[0]).astype(BF16)
    for c in range(2):
        kv_ref[c] = mm(x_ref[...], gp_ref[c + 1]).astype(BF16)


def three_call(x_turned, gp, after):
    tall, seq = x_turned.shape
    wide = gp.shape[2]
    block = 256
    return run(
        three_products,
        "three_products",
        [x_turned, gp],
        [((tall, wide), BF16), ((2, tall, wide), BF16)],
        after,
        grid=(tall // block,),
        in_specs=[pl.BlockSpec((block, seq), lambda i: (i, 0)), pl.BlockSpec(gp.shape, lambda i: (0, 0, 0))],
        out_specs=[
            pl.BlockSpec((block, wide), lambda i: (i, 0)),
            pl.BlockSpec((2, block, wide), lambda i: (0, i, 0)),
        ],
    )


def turned_product(mixed_ref, ga_ref, out_ref):
    out_ref[...] = mm(ga_ref[...], mixed_ref[...], TN).astype(BF16)


def back_project(flip, core_ref, gp_a_ref, gp_b_ref, w_a_ref, w_b_ref, out_ref):
    rows = out_ref.shape[0]
    at = pl.ds(pl.multiple_of(jnp.bitwise_xor(core_ref[0], flip) * rows, rows), rows)
    out = sum(
        mm(gp_ref[c, at, :], w_ref[c], NT)
        for c in range(3)
        for gp_ref, w_ref in ((gp_a_ref, w_a_ref), (gp_b_ref, w_b_ref))
    )
    out_ref[...] = out.astype(out_ref.dtype)


def by_rows(kernel, name, args, outs, after, block=128, rows=None, piece=0, halves=(), token=False):
    rows = rows or args[0].shape[0]
    steps = rows // block

    def spec(shape, at=None):
        rest = (0,) * (len(shape) - 1)
        cut = (block,) + tuple(shape[1:])
        if at in halves:
            first = halves.index(at) * steps // 2
            return pl.BlockSpec(cut, lambda i: (jnp.clip(i - first, 0, steps // 2 - 1),) + rest)
        if shape[0] == rows:
            return pl.BlockSpec(cut, lambda i: (i,) + rest)
        if shape[0] == 2 * rows:
            return pl.BlockSpec(cut, lambda i: (i + piece * steps,) + rest)
        return pl.BlockSpec(tuple(shape), lambda i: (0,) * len(shape))

    return run(
        kernel,
        name,
        args,
        outs,
        after,
        grid=(steps,),
        in_specs=[spec(arg.shape, at) for at, arg in enumerate(args)],
        out_specs=[spec(shape) for shape, _ in outs],
        size=1,
        token=token,
    )


def fold(bit, last, side_ref, cur_ref, got_ref, *out_refs):
    if last:
        out_refs[0][...] = add_low(cur_ref[...], got_ref[...])
        return
    half = got_ref.shape[0] // 2
    for side, out_ref in ((1 - side_ref[bit], out_refs[0]), (side_ref[bit], out_refs[1])):
        at = pl.ds(pl.multiple_of(side * half, half), half)
        out_ref[...] = add_low(cur_ref[at, :], got_ref[at, :])


def begin_pair(paired, side_ref, *refs):
    send_ref, keep_ref = refs[-2:]
    if paired:
        parts = [(refs[0].at[c], refs[1].at[c]) for c in range(2)]
    else:
        parts = [refs[0:1], refs[1:3]]
    for side in range(2):

        @pl.when(side_ref[0] == side)
        def _():
            for part, out_ref in ((parts[1 - side], send_ref), (parts[side], keep_ref)):
                out_ref[...] = part[0][...] if len(part) == 1 else add_low(part[0][...], part[1][...])


def join(left_ref, right_ref, out_ref):
    rows = left_ref.shape[0]
    out_ref[:rows, :] = left_ref[...]
    out_ref[rows:, :] = right_ref[...]


def place(piece, spot_ref, own_ref, other_ref, out_ref):
    count = own_ref.shape[0] // piece
    steps = out_ref.shape[0] // piece
    for at in range(steps):
        apart = jnp.bitwise_xor(pl.program_id(0) * steps + at, spot_ref[0])
        rows = pl.ds(pl.multiple_of(jnp.bitwise_and(apart, count - 1) * piece, piece), piece)
        far_side = apart >= count
        into = slice(at * piece, (at + 1) * piece)

        @pl.when(far_side)
        def _():
            out_ref[into, :] = other_ref[rows, :].astype(F32)

        @pl.when(jnp.logical_not(far_side))
        def _():
            out_ref[into, :] = own_ref[rows, :].astype(F32)


def pieces(count, spot, own_ref, other_ref, first, steps):
    piece = own_ref.shape[0] // count
    for at in range(steps):
        apart = jnp.bitwise_xor(first + at, spot)
        rows = pl.ds(pl.multiple_of(jnp.bitwise_and(apart, count - 1) * piece, piece), piece)
        mine, others = own_ref[rows, :].astype(F32), other_ref[rows, :].astype(F32)
        yield at * piece, piece, jnp.where(apart >= count, others, mine)


def place_turned(count, spot_ref, own_ref, other_ref, w_out_ref, part_ref):
    for at, piece, value in pieces(count, spot_ref[0], own_ref, other_ref, 0, count):
        w_out_ref[:, at:at + piece] = value.T
    for at, piece, value in pieces(count, spot_ref[0], own_ref, other_ref, count, count):
        part_ref[at:at + piece, :] = value


def place_two(count, spot_ref, own_ref, other_ref, _, out_ref):
    for at, piece, value in pieces(count, spot_ref[0], own_ref, other_ref, pl.program_id(0) * count, count):
        out_ref[at:at + piece, :] = value


class Sum:
    def __init__(self, size, height, first=0):
        self.size, self.bits, self.height = size, size.bit_length() - 1, height
        me = lax.axis_index("dp")
        order = [(first + step) % self.bits for step in range(self.bits)]
        self.flips = [1 << b for b in order]
        sides = [(me // flip) % 2 for flip in self.flips]
        self.sides = jnp.stack(sides).astype(jnp.int32)
        self.spot = sum(side << (self.bits - 1 - step) for step, side in enumerate(sides))

    def begin(self, send, keep):
        self.keep, self.step = keep, 0
        self.sent = swap(send, "dp", self.size, self.flips[0])

    def begin_pairs(self, arrays, after):
        shape = arrays[0].shape[-2:]
        send, keep = run(
            functools.partial(begin_pair, len(arrays) == 2), "begin_pair", [self.sides] + list(arrays),
            [(shape, BF16)] * 2, after, scalars=1,
        )
        self.begin(send, keep)
        return keep

    def fold(self, after):
        if self.step >= self.bits:
            return after
        self.step += 1
        last = self.step == self.bits
        rows, columns = self.sent.shape
        kernel = functools.partial(fold, self.step, last)
        outs = [((rows, columns), BF16)] if last else [((rows // 2, columns), BF16)] * 2
        out = run(kernel, "fold", [self.sides, self.keep, self.sent], outs, after, scalars=1, cost=60)
        self.keep = out if last else out[1]
        send = out if last else out[0]
        self.sent = swap(send, "dp", self.size, self.flips[min(self.step, self.bits - 1)])
        return self.keep

    def spread(self, after):
        if self.step < self.bits:
            return after
        bit = 2 * self.bits - 2 - self.step
        rows, columns = self.keep.shape
        self.keep = run(join, "join", [self.keep, self.sent], [((2 * rows, columns), BF16)], after)
        self.sent = swap(self.keep, "dp", self.size, self.flips[bit])
        self.step += 1
        return self.keep

    def complete(self, after):
        while self.step < self.bits:
            after = self.fold(after)
        while self.step < 2 * self.bits - 1:
            after = self.spread(after)
        return after

    def place(self, after):
        after = self.complete(after)
        rows, columns = self.keep.shape
        piece = rows * 2 // self.size
        placed, token = run(
            functools.partial(place, piece),
            "place",
            [self.spot.reshape(1).astype(jnp.int32), self.keep, self.sent],
            [((2 * rows, columns), F32)],
            after,
            grid=(2,),
            size=1,
            token=True,
            in_specs=[
                pl.BlockSpec(memory_space=pltpu.SMEM),
                pl.BlockSpec((rows, columns), lambda i: (0, 0)),
                pl.BlockSpec((rows, columns), lambda i: (0, 0)),
            ],
            out_specs=[pl.BlockSpec((rows, columns), lambda i: (i, 0))],
        )
        return placed[: self.height], token

    def place_out(self, after):
        after = self.complete(after)
        rows, columns = self.keep.shape
        return run(
            functools.partial(place_turned, self.size // 2),
            "place_turned",
            [self.spot.reshape(1).astype(jnp.int32), self.keep, self.sent],
            [((columns, rows), F32), ((3 * rows, columns), F32)],
            after,
            grid=(1,),
            size=1,
            token=True,
            in_specs=[pl.BlockSpec(memory_space=pltpu.SMEM)]
            + [pl.BlockSpec((rows, columns), lambda i: (0, 0))] * 2,
            out_specs=[
                pl.BlockSpec((columns, rows), lambda i: (0, 0)),
                pl.BlockSpec((rows, columns), lambda i: (0, 0)),
            ],
        )

    def place_rest(self, into, after):
        after = self.complete(after)
        rows, columns = self.keep.shape
        return run(
            functools.partial(place_two, self.size // 2),
            "place_two",
            [self.spot.reshape(1).astype(jnp.int32), self.keep, self.sent, into],
            [((3 * rows, columns), F32)],
            after,
            grid=(2,),
            size=1,
            in_specs=[pl.BlockSpec(memory_space=pltpu.SMEM)]
            + [pl.BlockSpec((rows, columns), lambda i: (0, 0))] * 2
            + [pl.BlockSpec(memory_space=pl.ANY)],
            out_specs=[pl.BlockSpec((rows, columns), lambda i: (i + 1, 0))],
            aliases={3: 0},
        )


def gelu_and_slope(up):
    size = jnp.abs(up)
    t = 1.0 / (1.0 + (0.3275911 * 0.7071067811865476) * size)
    bell = jnp.exp(-0.5 * up * up)
    poly = t * (
        0.5 * 0.254829592
        + t * (0.5 * -0.284496736 + t * (0.5 * 1.421413741 + t * (0.5 * -1.453152027 + t * (0.5 * 1.061405429))))
    )
    tail = poly * bell
    cdf = jnp.where(up >= 0.0, 1.0 - tail, tail)
    return up * cdf, cdf + up * bell * 0.3989422804014327


def feed(count, piece, *refs):
    n2_refs, (gd_ref, ok_ref, w_up_ref, b_up_ref, w_down_ref, gn2_ref, act_ref, gup_ref, gb_ref) = refs[:count], refs[count:]
    hidden, rows, step = w_up_ref.shape[1], n2_refs[0].shape[0], 256

    def products(block, at):
        part = slice(at, at + step)
        given = slice((piece + block) * rows, (piece + block + 1) * rows)
        up = mm(n2_refs[block][...], w_up_ref[:, part]) + b_up_ref[:, part].astype(F32)
        return up, mm(gd_ref[given, :], w_down_ref[part, :], NT), ok_ref[given, :]

    def rest(block, at, up, grad_act, ok):
        part, into = slice(at, at + step), slice(block * rows, (block + 1) * rows)
        act, slope = gelu_and_slope(up)
        grad_up = (slope * (grad_act * ok)).astype(BF16)
        act_ref[into, part] = (act * ok).astype(BF16)
        gup_ref[into, part] = grad_up
        total = jnp.sum(grad_up.astype(F32).reshape(rows // 8, 8, step), axis=0)
        gb_ref[:, part] = total if block == 0 else gb_ref[:, part] + total
        if at + step == hidden:
            gn2_ref[into, :] = mm(gup_ref[into, :], w_up_ref[...], NT).astype(BF16)

    waiting = None
    for block in range(count):
        for at in range(0, hidden, step):
            made = products(block, at)
            if waiting is not None:
                rest(*waiting)
            waiting = (block, at) + made
    rest(*waiting)


def feed_call(n2_pieces, gd, ok, piece, w_up, b_up, w_down, after):
    hidden, count = w_up.shape[1], len(n2_pieces)
    rows = n2_pieces[0].shape[0] * count
    return run(
        functools.partial(feed, count, piece),
        "feed",
        list(n2_pieces) + [gd, ok, w_up, b_up, w_down],
        [((rows, D), BF16), ((rows, hidden), BF16), ((rows, hidden), BF16), ((8, hidden), F32)],
        after,
    )


def swap(value, axis, size, flip):
    return lax.ppermute(value, axis, [(i, i ^ flip) for i in range(size)])


def add_low(left, right):
    return (left.astype(F32) + right.astype(F32)).astype(BF16)


def sum_over(value, axis, size):
    flip = 1
    while flip < size:
        value = value + swap(value, axis, size, flip)
        flip *= 2
    return value


def on_device(
    dp_size,
    mp_size,
    tokens,
    segment_ids,
    valid_mask,
    patch_index,
    gsd_index,
    w_qkv,
    bias_qv,
    w_out,
    b_out,
    gain_one,
    shift_one,
    gain_two,
    shift_two,
    w_up,
    b_up,
    w_down,
    b_down,
    cotangent,
):
    own_rows = tokens.shape[0]
    mp = lax.axis_index("mp")
    core = mp % 2
    row = mp // 2

    def near(value):
        return swap(value, "mp", mp_size, 1)

    def far(value):
        return swap(value, "mp", mp_size, 2)

    core_s = core.reshape(1).astype(jnp.int32)
    down_sum, up_sum = Sum(dp_size, w_down.shape[0]), Sum(dp_size, w_up.shape[0])
    first_sum, second_sum = Sum(dp_size, 2 * D), Sum(dp_size, 2 * D)
    sides = down_sum.sides

    cot_near = near(cotangent)
    inputs = [segment_ids, valid_mask, patch_index, gsd_index]
    shape = (3, D // 4, w_qkv.shape[2])
    piece_a, piece_b = run(cut, "cut", [sides, w_qkv], [(shape, BF16)] * 2, None, scalars=1, size=1)
    segment_ids, valid_mask, patch_index, gsd_index = run(
        hand_on_all, "hand_on_all", inputs, [(part.shape, part.dtype) for part in inputs], piece_b, size=1
    )
    far_bias = far(bias_qv)
    far_a, far_b = far(piece_a), far(piece_b)

    own_start = mp * own_rows
    level = image_levels(segment_ids, gsd_index)
    codes = jnp.stack([patch_index // GRID, patch_index % GRID]) * GSDS + level
    own_codes = lax.dynamic_slice_in_dim(codes.reshape(2, -1, 1), own_start, own_rows, axis=1)
    all_valid = valid_mask.reshape(-1, 1).astype(F32)

    def valid_of(flip):
        at = jnp.bitwise_xor(mp, flip) * own_rows
        return lax.dynamic_slice_in_dim(all_valid, at, own_rows)

    own_valid = valid_of(0)

    row_seg = lax.dynamic_index_in_dim(segment_ids, row, 0, keepdims=True)
    row_ok = lax.dynamic_index_in_dim(valid_mask, row, 0, keepdims=True)
    seg_k = jnp.where(row_ok == 1, row_seg, -1)
    seg_q = row_seg.reshape(-1, 1)

    start_sum, normed = by_rows(
        front, "front",
        [tokens, own_codes[0], own_codes[1], code_table(), gain_one[None], shift_one[None]],
        [(tokens.shape, F32), (tokens.shape, BF16)], [segment_ids, cot_near],
    )
    half = (own_rows, D)
    w_out_sent, a_pass = run(
        hand_on_all, "hand_on_all", [w_out, far_a], [(w_out.shape, BF16), (far_a.shape, BF16)], normed, cost=60
    )
    far_out = far(w_out_sent)
    other_a = swap(a_pass, "dp", dp_size, 1)
    normed_row = run(in_row, "in_row", [core_s, normed, near(normed)], [((2 * own_rows, D), BF16)], a_pass, scalars=1)
    b_pass, cot_sent = run(
        hand_on_all, "hand_on_all", [far_b, cotangent], [(far_b.shape, BF16), (half, BF16)], normed_row
    )
    other_b = swap(b_pass, "dp", dp_size, 1)
    cot_far = far(cot_sent)

    qkv_a, mixed_a, lse_a = forward_call(sides, seg_q, seg_k, normed_row, bias_qv, [w_qkv], cot_sent)
    pieces_b = [a_pass, b_pass, other_a, other_b]
    qkv_b, mixed_b, lse_b = forward_call(sides, seg_q, seg_k, normed_row, far_bias, pieces_b, lse_a)
    operands = [core_s, mixed_a, mixed_b, w_out, far_out]
    attn_near = run(functools.partial(project_out, 1), "project_out", operands, [(half, BF16)], lse_b, scalars=1)
    attn_own = run(functools.partial(project_out, 0), "project_out", operands, [(half, F32)], attn_near, scalars=1)
    attn_got = near(attn_near)
    quarter = own_rows // 2
    piece_shape = (quarter, D)
    wide = w_qkv.shape[2]
    turned = [((D, wide), BF16)]
    tile = [((8, D), F32)]
    flips = [1 << b for b in range(dp_size.bit_length() - 1)]
    b_up_row = b_up[None, :]
    ffn = [w_up, b_up_row, w_down]
    last = attn_own

    def norm_two(piece, last):
        return by_rows(
            second_norm, "second_norm",
            [start_sum, attn_own, attn_got, b_out[None], gain_two[None], shift_two[None]],
            [(piece_shape, F32), (piece_shape, BF16)], last, rows=quarter, piece=piece,
        )

    def norm_two_back(piece, from_far, after_attn, last):
        return by_rows(
            second_norm_back, "second_norm_back",
            [gn2_o, from_near, from_far, after_attn, cotangent, own_valid, gain_two[None]],
            [(piece_shape, F32), (piece_shape, BF16), ((4, 8, D), F32)], last, rows=quarter, piece=piece,
        )

    operands = [core_s, None, None, w_qkv, None]
    after1, n2_1 = norm_two(0, last)
    far1, near1 = far(n2_1), near(n2_1)
    last = n2_1
    after2, n2_2 = norm_two(1, last)
    far2, near2 = far(n2_2), near(n2_2)
    last = n2_2
    gn2_o, act_o, gup_o, gb_o = feed_call([n2_1, n2_2], cotangent, own_valid, 0, *ffn, last)
    last = gb_o
    last = cot_pass = handed(cot_far, last)
    cot_cross = near(cot_pass)
    gn2_n, act_n, gup_n, gb_n = feed_call([near1, near2], cot_near, valid_of(1), 0, *ffn, last)
    from_near = near(gn2_n)
    last = gb_n
    here = [(act_o, 0, cotangent, 0, own_rows), (act_n, 0, cot_near, 0, own_rows)]
    last = down_here = token_call(sides, here, True, last)
    last = far1_pass = handed(far1, last)
    cross1 = near(far1_pass)
    gn2_f1, act_f1, gup_f1, gb_f1 = feed_call([far1_pass], cot_pass, valid_of(2), 0, *ffn, last)
    last = gb_f1
    gn2_c1, act_c1, gup_c1, gb_c1 = feed_call([cross1], cot_cross, valid_of(3), 0, *ffn, last)
    got1 = near(gn2_c1)
    last = gb_c1
    last = far2_pass = handed(far2, last)
    cross2 = near(far2_pass)
    last = sent1 = by_rows(add_two, "add_two", [gn2_f1, got1], [(piece_shape, BF16)], last)
    back1 = far(sent1)
    gn2_f2, act_f2, gup_f2, gb_f2 = feed_call([far2_pass], cot_pass, valid_of(2), 1, *ffn, last)
    last = gb_f2
    gn2_c2, act_c2, gup_c2, gb_c2 = feed_call([cross2], cot_cross, valid_of(3), 1, *ffn, last)
    got2 = near(gn2_c2)
    last = gb_c2
    there = [(act_f1, 0, cot_pass, 0, quarter), (act_c1, 0, cot_cross, 0, quarter)]
    there += [(act_f2, 0, cot_pass, 1, quarter), (act_c2, 0, cot_cross, 1, quarter)]
    down_send, down_keep = token_call(sides, there, down_here, last)
    down_sum.begin(down_send, down_keep)
    last = down_keep
    last = sent2 = by_rows(add_two, "add_two", [gn2_f2, got2], [(piece_shape, BF16)], last)
    back2 = far(sent2)
    mid1, ga1, sums_two = norm_two_back(0, back1, after1, last)
    ga1_near = near(ga1)
    last = ga1
    pairs = [(n2_1, 0, gup_o, 0, quarter), (n2_2, 0, gup_o, 1, quarter)]
    pairs += [(near1, 0, gup_n, 0, quarter), (near2, 0, gup_n, 1, quarter)]
    pairs += [(far1_pass, 0, gup_f1, 0, quarter), (cross1, 0, gup_c1, 0, quarter)]
    pairs += [(far2_pass, 0, gup_f2, 0, quarter), (cross2, 0, gup_c2, 0, quarter)]
    up_send, up_keep = token_call(sides, pairs, None, last)
    up_sum.begin(up_send, up_keep)
    last = up_keep
    mid2, ga2, sums_more = norm_two_back(1, back2, after2, last)
    ga2_near = near(ga2)
    last = ga2
    last = x_turned = run(turn, "turn", [normed_row], [((D, 2 * own_rows), BF16)], last, cost=60)
    last = far_qkv = run(assemble, "assemble", [sides] + pieces_b, [(w_qkv.shape, BF16)], last, scalars=1, cost=60)
    last = ga_row = run(
        in_row_pieces, "in_row", [core_s, ga1, ga2, ga1_near, ga2_near], [((2 * own_rows, D), BF16)], last, scalars=1
    )
    last = gw_out_b = run(turned_product, "turned_product", [mixed_b, ga_row], turned, last)
    far_out_grad = far(gw_out_b)
    last = gw_out_a = run(turned_product, "turned_product", [mixed_a, ga_row], turned, last)
    last = down_sum.fold(last)
    gp_b, bias_b = backward_call(seg_q, seg_k, ga_row, far_out, qkv_b, lse_b, last)
    last = bias_b
    q_b, kv_b = three_call(x_turned, gp_b, last)
    far_q, far_kv = far(q_b), far(kv_b)
    last = q_b
    last = out_both = by_rows(add_two, "add_two", [gw_out_a, far_out_grad], [((D, wide), BF16)], last, block=512)
    last = down_sum.fold(last)
    gp_a, bias_a = backward_call(seg_q, seg_k, ga_row, w_out, qkv_a, lse_a, last)
    last = bias_a
    last = up_sum.fold(last)
    q_a, kv_a = three_call(x_turned, gp_a, last)
    last = q_a
    last = down_sum.fold(last)
    last = first_sum.begin_pairs([out_both, q_a, far_q], last)
    operands[1:3] = gp_a, gp_b
    operands[4] = far_qkv
    last = gn_near = run(functools.partial(back_project, 1), "back_project", operands, [(half, BF16)], last, scalars=1)
    operands[1:3] = gp_a, gp_b
    operands[4] = far_qkv
    last = gn_own = run(functools.partial(back_project, 0), "back_project", operands, [(half, F32)], last, scalars=1)
    grad_tokens, sums_one = by_rows(
        first_norm_back, "first_norm_back",
        [gn_own, near(gn_near), start_sum, mid1, mid2, gain_one[None]],
        [(half, BF16), ((2, 8, D), F32)], last, halves=(3, 4),
    )
    last = sums_one
    last = down_sent = run(down_out, "down_out", [act_n, act_c1, act_c2, w_down], [((2,) + half, BF16)], last)
    down_near = near(down_sent)
    last = up_sum.fold(last)
    last = down_sum.spread(last)
    last = second_sum.begin_pairs([kv_a, far_kv], last)
    down_base, down_far = run(
        down_in, "down_in", [act_o, act_f1, act_f2, after1, after2, down_near, b_down[None], w_down],
        [(half, F32), (half, BF16)], last,
    )
    last = down_base
    last = first_sum.fold(last)
    last = small = run(small_first, "small_first", [sums_two, sums_more, sums_one], tile, last)
    small_got = near(small)
    last = up_sum.fold(last)
    last = down_sum.spread(last)
    last = first_sum.fold(last)
    last = second_sum.fold(last)
    send, small = run(small_second, "small_second", [small, small_got, bias_a, bias_b], tile * 2, last)
    small_got = far(send)
    last = small
    last = up_sum.spread(last)
    last = second_sum.fold(last)
    gbs = [gb_o, gb_n, gb_f1, gb_c1, gb_f2, gb_c2]
    last = small = run(small_third, "small_third", [small, small_got] + gbs, tile, last)
    small_got = swap(small, "dp", dp_size, flips[0])
    last = first_sum.fold(last)
    last = up_sum.spread(last)
    grad_w_down, last = down_sum.place(last)
    last = first_sum.spread(last)
    last = second_sum.fold(last)
    last = first_sum.spread(last)
    last = down_sent = handed(down_far, last)
    down_got = far(down_sent)
    last = second_sum.spread(last)
    last = small = run(small_add, "small_add", [small, small_got], tile, last)
    small_got = swap(small, "dp", dp_size, flips[1])
    last = second_sum.spread(last)
    last = small = run(small_add, "small_add", [small, small_got], tile, last)
    small_got = swap(small, "dp", dp_size, flips[2])
    grad_w_up, last = up_sum.place(last)
    layer_out, last = by_rows(
        finish, "finish", [down_base, down_got, own_valid], [(half, BF16)], last, token=True
    )
    for flip in flips[3:]:
        last = small = run(small_add, "small_add", [small, small_got], tile, last)
        small_got = swap(small, "dp", dp_size, flip)
    last = small = run(small_add, "small_add", [small, small_got], tile, last)
    grad_w_out, grad_w_qkv, last = first_sum.place_out(last)
    grad_w_qkv = second_sum.place_rest(grad_w_qkv, last).reshape(w_qkv.shape)
    grad_bias_qv = small[6, : 2 * wide].reshape(2, wide)
    grad_b_up = small[7]
    return (
        layer_out,
        grad_tokens,
        grad_w_qkv,
        grad_bias_qv,
        grad_w_out,
        small[0],
        small[1],
        small[2],
        small[3],
        small[4],
        grad_w_up,
        grad_b_up,
        grad_w_down,
        small[5],
    )


def solution(mesh):
    return jax.shard_map(
        functools.partial(on_device, mesh.shape["dp"], mesh.shape["mp"]),
        mesh=mesh,
        in_specs=(
            P(("dp", "mp"), None),
            P("dp", None),
            P("dp", None),
            P("dp", None),
            P("dp", None),
            P(None, None, "mp"),
            P(None, "mp"),
            P("mp", None),
            P(),
            P(),
            P(),
            P(),
            P(),
            P(None, "mp"),
            P("mp"),
            P("mp", None),
            P(),
            P(("dp", "mp"), None),
        ),
        out_specs=(
            P(("dp", "mp"), None),
            P(("dp", "mp"), None),
            P(None, None, "mp"),
            P(None, "mp"),
            P("mp", None),
            P(),
            P(),
            P(),
            P(),
            P(),
            P(None, "mp"),
            P("mp"),
            P("mp", None),
            P(),
        ),
        check_vma=False,
    )
```

```python
import functools
import jax
import jax.numpy as jnp
from jax import lax
from jax.experimental import pallas as pl
from jax.experimental.pallas import tpu as pltpu
from jax.sharding import PartitionSpec as P

D = 1024
HEAD = 64
SEGS = 16
GRID = 14
GSDS = 8
EPSILON = 1e-06
MASKED = -1000000000.0
SCALE = HEAD ** (-0.5)
BQ = 128
PAIR = 2 * HEAD
F32 = jnp.float32
BF16 = jnp.bfloat16
NN = (((1,), (0,)), ((), ()))
NT = (((1,), (1,)), ((), ()))
TN = (((0,), (0,)), ((), ()))


def mm(left, right, dims=NN):
    return lax.dot_general(left, right, dims, preferred_element_type=F32)


def image_levels(segment_ids, gsd_index):
    in_image = segment_ids[..., None] == jnp.arange(SEGS, dtype=jnp.int32)
    return jnp.sum(jnp.where(in_image, gsd_index[:, None, :], 0), axis=-1)


def code_table():
    quarter = D // 4
    frequency = 1.0 / 10000.0 ** (jnp.arange(quarter, dtype=jnp.float32) / quarter)
    ratio = 2.0 ** (0.5 * jnp.arange(GSDS, dtype=jnp.float32) - 1.0)
    place = jnp.arange(16, dtype=jnp.float32)
    angle = (place[:, None] * ratio[None, :]).reshape(-1, 1) * frequency
    return jnp.concatenate([jnp.sin(angle), jnp.cos(angle)], axis=-1)


def front(tokens_ref, row_ref, col_ref, table_ref, gain_ref, shift_ref, start_ref, normed_ref):
    high = table_ref[...].astype(BF16)
    rest = table_ref[...] - high.astype(F32)
    middle = rest.astype(BF16)
    low = (rest - middle.astype(F32)).astype(BF16)
    spots = lax.broadcasted_iota(jnp.int32, (tokens_ref.shape[0], table_ref.shape[0]), 1)
    half = table_ref.shape[1]
    for at, index_ref in ((0, row_ref), (half, col_ref)):
        chosen = (spots == index_ref[...]).astype(F32).astype(BF16)
        code = (mm(chosen, low) + mm(chosen, middle)) + mm(chosen, high)
        start_ref[:, at:at + half] = tokens_ref[:, at:at + half].astype(F32) + code
    xhat, _ = normalize(start_ref[...])
    normed_ref[...] = (xhat * gain_ref[...].astype(F32) + shift_ref[...].astype(F32)).astype(BF16)


def normalize(values):
    row_mean = jnp.mean(values, axis=-1, keepdims=True)
    centred = values - row_mean
    row_var = jnp.mean(centred * centred, axis=-1, keepdims=True)
    rstd = lax.rsqrt(row_var + EPSILON)
    return centred * rstd, rstd


def norm_back(grad, gain, xhat, rstd):
    scaled = grad * gain
    mean_scaled = jnp.mean(scaled, axis=-1, keepdims=True)
    mean_along = jnp.mean(scaled * xhat, axis=-1, keepdims=True)
    return rstd * (scaled - mean_scaled - xhat * mean_along)


def window_start(block, seq, width):
    return min(max(block * BQ - BQ, 0), seq - width)


def fill_bias(seg_q_ref, seg_k_ref, bias_ref, seq, width):
    for block in range(seq // BQ):
        start = window_start(block, seq, width)
        seg_q = seg_q_ref[block * BQ:(block + 1) * BQ, :]
        seg_k = seg_k_ref[:, start:start + width]
        row = lax.broadcasted_iota(jnp.int32, (BQ, width), 0) + block * BQ
        col = lax.broadcasted_iota(jnp.int32, (BQ, width), 1) + start
        allowed = (seg_q == seg_k) | (row == col)
        bias_ref[block] = jnp.where(allowed, 0.0, MASKED)


def split_heads(tile):
    low = lax.broadcasted_iota(jnp.int32, tile.shape, 1) < HEAD
    zero = jnp.zeros_like(tile)
    return jnp.concatenate([jnp.where(low, tile, zero), jnp.where(low, zero, tile)], axis=0)


def join_heads(stacked):
    half = stacked.shape[0] // 2
    low = lax.broadcasted_iota(jnp.int32, (half, PAIR), 1) < HEAD
    return jnp.where(low, stacked[:half], stacked[half:])


def piece_places(side_ref, w_refs, depth):
    if len(w_refs) == 1:
        return [(slice(None), w_refs[0])]
    rows = depth // 4
    starts = [side_ref[0] * 2, side_ref[0] * 2 + 1, (1 - side_ref[0]) * 2, (1 - side_ref[0]) * 2 + 1]
    return [(pl.ds(pl.multiple_of(at * rows, rows), rows), w_ref) for at, w_ref in zip(starts, w_refs)]


def assemble(side_ref, *refs):
    out_ref = refs[-1]
    for at, w_ref in piece_places(side_ref, refs[:-1], out_ref.shape[1]):
        out_ref[:, at, :] = w_ref[...]


def turn(in_ref, out_ref):
    out_ref[...] = in_ref[...].T


def cut(side_ref, w_ref, *out_refs):
    rows = w_ref.shape[1] // 4
    for piece, out_ref in enumerate(out_refs):
        at = pl.ds(pl.multiple_of((side_ref[0] * 2 + piece) * rows, rows), rows)
        out_ref[...] = w_ref[:, at, :]


def in_row(core_ref, own_ref, other_ref, out_ref):
    rows = own_ref.shape[0]
    for side, in_ref in ((core_ref[0], own_ref), (1 - core_ref[0], other_ref)):
        out_ref[pl.ds(pl.multiple_of(side * rows, rows), rows), :] = in_ref[...]


def in_row_pieces(core_ref, own1_ref, own2_ref, other1_ref, other2_ref, out_ref):
    rows = own1_ref.shape[0]
    for side, refs in ((core_ref[0], (own1_ref, own2_ref)), (1 - core_ref[0], (other1_ref, other2_ref))):
        for piece, in_ref in enumerate(refs):
            at = (side * 2 + piece) * rows
            out_ref[pl.ds(pl.multiple_of(at, rows), rows), :] = in_ref[...]


def attend_forward(side_ref, seg_q_ref, seg_k_ref, x_ref, b_ref, *refs):
    w_refs, (qkv_ref, mixed_ref, lse_ref, bias_ref) = refs[:-4], refs[-4:]
    seq = x_ref.shape[0]
    width = bias_ref.shape[2]
    wide = w_refs[0].shape[2]
    fill_bias(seg_q_ref, seg_k_ref, bias_ref, seq, width)
    for c in range(3):
        for r in range(0, seq, 256):
            out = sum(
                mm(x_ref[r:r + 256, at], w_ref[c]) for at, w_ref in piece_places(side_ref, w_refs, x_ref.shape[1])
            )
            if c != 1:
                out = out + b_ref[c // 2:c // 2 + 1, :].astype(F32)
            qkv_ref[c, r:r + 256, :] = out.astype(BF16)
    lane = lax.broadcasted_iota(jnp.int32, (BQ, PAIR), 1)
    pairs = range(wide // PAIR)
    for block in range(seq // BQ):
        start = window_start(block, seq, width)
        rows = slice(block * BQ, (block + 1) * BQ)
        keys = slice(start, start + width)
        bias = bias_ref[block]
        bias = jnp.concatenate([bias, bias], axis=0)
        lanes = [slice(pair * PAIR, (pair + 1) * PAIR) for pair in pairs]
        queries = [split_heads(qkv_ref[0, rows, at] * SCALE) for at in lanes]
        scores = [mm(queries[p], qkv_ref[1, keys, lanes[p]], NT) + bias for p in pairs]
        row_max = [jnp.max(part, axis=-1, keepdims=True) for part in scores]
        weight = [jnp.exp(scores[p] - row_max[p]) for p in pairs]
        mixed = [mm(weight[p].astype(BF16), qkv_ref[2, keys, lanes[p]]) for p in pairs]
        total = [jnp.sum(part, axis=-1, keepdims=True) for part in weight]
        lse_tile = jnp.zeros((BQ, PAIR), F32)
        for p in pairs:
            mixed_ref[rows, lanes[p]] = join_heads(mixed[p] * (1.0 / total[p])).astype(BF16)
            lse = row_max[p] + jnp.log(total[p])
            lse_tile = jnp.where(lane == 2 * p, lse[:BQ], lse_tile)
            lse_tile = jnp.where(lane == 2 * p + 1, lse[BQ:], lse_tile)
        lse_ref[rows, :] = lse_tile


def attend_backward(
    seg_q_ref, seg_k_ref, ga_ref, w_out_ref, qkv_ref, lse_ref, out_ref, sums_ref, bias_ref, gm_ref, acc_ref
):
    seq = ga_ref.shape[0]
    width = bias_ref.shape[2]
    wide = w_out_ref.shape[0]
    fill_bias(seg_q_ref, seg_k_ref, bias_ref, seq, width)
    for r in range(0, seq, 256):
        gm_ref[r:r + 256, :] = mm(ga_ref[r:r + 256, :], w_out_ref[...], NT).astype(BF16)
    acc_ref[...] = jnp.zeros_like(acc_ref)
    for block in range(seq // BQ):
        start = window_start(block, seq, width)
        rows = slice(block * BQ, (block + 1) * BQ)
        keys = slice(start, start + width)
        bias = bias_ref[block]
        bias = jnp.concatenate([bias, bias], axis=0)
        lse_tile = lse_ref[rows, :]
        pairs = range(wide // PAIR)
        lanes = [slice(pair * PAIR, (pair + 1) * PAIR) for pair in pairs]
        queries = [split_heads(qkv_ref[0, rows, at] * SCALE) for at in lanes]
        grad_mixed = [split_heads(gm_ref[rows, at]) for at in lanes]
        key_rows = [qkv_ref[1, keys, at] for at in lanes]
        scores = [mm(queries[p], key_rows[p], NT) + bias for p in pairs]
        grad_prob = [mm(grad_mixed[p], qkv_ref[2, keys, lanes[p]], NT) for p in pairs]
        lse = [
            jnp.concatenate([lse_tile[:, 2 * p:2 * p + 1], lse_tile[:, 2 * p + 1:2 * p + 2]], axis=0)
            for p in pairs
        ]
        prob = [jnp.exp(scores[p] - lse[p]) for p in pairs]
        along = [jnp.sum(prob[p] * grad_prob[p], axis=-1, keepdims=True) for p in pairs]
        grad_scores = [(prob[p] * (grad_prob[p] - along[p])).astype(BF16) for p in pairs]
        for p in pairs:
            acc_ref[1, keys, lanes[p]] += mm(prob[p].astype(BF16), grad_mixed[p], TN)
        for p in pairs:
            out_ref[0, rows, lanes[p]] = (join_heads(mm(grad_scores[p], key_rows[p])) * SCALE).astype(BF16)
            acc_ref[0, keys, lanes[p]] += mm(grad_scores[p], queries[p], TN)
    out_ref[1] = acc_ref[0].astype(BF16)
    out_ref[2] = acc_ref[1].astype(BF16)
    for at, c in enumerate((0, 2)):
        total = jnp.sum(out_ref[c].astype(F32), axis=0, keepdims=True)
        sums_ref[4 * at:4 * at + 4, :] = jnp.concatenate([total, jnp.zeros((3, wide), F32)], axis=0)


def chained(kernel, count, extra=1):
    def body(*refs):
        kernel(*refs[:count], *refs[count + extra:])

    return body


def with_token(kernel):
    def body(*refs):
        kernel(*refs[:-1])
        refs[-1][...] = jnp.zeros_like(refs[-1])

    return body


def run(kernel, name, args, outs, after, scalars=0, grid=None, in_specs=None, out_specs=None, scratch=(), aliases=None, cost=15, size=10**9, token=False):
    vmem = pl.BlockSpec(memory_space=pltpu.VMEM)
    if in_specs is None:
        in_specs = [pl.BlockSpec(memory_space=pltpu.SMEM)] * scalars + [vmem] * (len(args) - scalars)
    if out_specs is None:
        out_specs = [vmem] * len(outs)
    outs, out_specs = list(outs), list(out_specs)
    if token:
        outs.append(((8, 128), F32))
        out_specs.append(pl.BlockSpec((8, 128), lambda *_: (0, 0)) if grid is not None else vmem)
        kernel = with_token(kernel)
    if after is not None:
        behind = list(after) if isinstance(after, (list, tuple)) else [after]
        kernel = chained(kernel, len(args), len(behind))
        args = list(args) + behind
        in_specs = list(in_specs) + [pl.BlockSpec(memory_space=pl.ANY)] * len(behind)
    result = pl.pallas_call(
        kernel,
        name=name,
        grid=grid if grid is not None else (),
        out_shape=tuple(jax.ShapeDtypeStruct(shape, dtype) for shape, dtype in outs),
        in_specs=in_specs,
        out_specs=tuple(out_specs),
        scratch_shapes=list(scratch),
        input_output_aliases=aliases or {},
        compiler_params=pltpu.CompilerParams(vmem_limit_bytes=26 * 2**20),
        cost_estimate=pl.CostEstimate(flops=cost * 10**9, bytes_accessed=size, transcendentals=0),
    )(*args)
    return result if len(outs) > 1 else result[0]


def forward_call(sides, seg_q, seg_k, x, b, pieces_of, after):
    seq, wide = x.shape[0], pieces_of[0].shape[2]
    width = min(3 * BQ, seq)
    return run(
        attend_forward,
        "attend_forward",
        [sides, seg_q, seg_k, x, b] + list(pieces_of),
        [((3, seq, wide), BF16), ((seq, wide), BF16), ((seq, PAIR), F32)],
        after,
        cost=60,
        scalars=1,
        scratch=[pltpu.VMEM((seq // BQ, BQ, width), F32)],
    )


def backward_call(seg_q, seg_k, ga, w_out, qkv, lse, after):
    seq, wide = ga.shape[0], w_out.shape[0]
    width = min(3 * BQ, seq)
    return run(
        attend_backward,
        "attend_backward",
        [seg_q, seg_k, ga, w_out, qkv, lse],
        [((3, seq, wide), BF16), ((8, wide), F32)],
        after,
        scratch=[
            pltpu.VMEM((seq // BQ, BQ, width), F32),
            pltpu.VMEM((seq, wide), BF16),
            pltpu.VMEM((2, seq, wide), F32),
        ],
    )


def eight(values):
    return jnp.sum(values.reshape(values.shape[0] // 8, 8, values.shape[1]), axis=0)


def project_out(flip, core_ref, mixed_a_ref, mixed_b_ref, w_a_ref, w_b_ref, out_ref):
    rows = out_ref.shape[0]
    at = pl.ds(pl.multiple_of(jnp.bitwise_xor(core_ref[0], flip) * rows, rows), rows)
    out = mm(mixed_a_ref[at, :], w_a_ref[...]) + mm(mixed_b_ref[at, :], w_b_ref[...])
    out_ref[...] = out.astype(out_ref.dtype)


def second_norm(start_ref, own_ref, near_ref, b_ref, gain_ref, shift_ref, after_ref, n2_ref):
    value = start_ref[...] + (own_ref[...] + near_ref[...].astype(F32)) + b_ref[...].astype(F32)
    after_ref[...] = value
    xhat, _ = normalize(value)
    n2_ref[...] = (xhat * gain_ref[...].astype(F32) + shift_ref[...].astype(F32)).astype(BF16)


def second_norm_back(here_ref, near_ref, far_ref, after_ref, cot_ref, ok_ref, gain_ref, mid_ref, ga_ref, sums_ref):
    @pl.when(pl.program_id(0) == 0)
    def _():
        sums_ref[...] = jnp.zeros_like(sums_ref)

    grad = here_ref[...].astype(F32) + near_ref[...].astype(F32) + far_ref[...].astype(F32)
    xhat, rstd = normalize(after_ref[...])
    grad_after = cot_ref[...].astype(F32) * ok_ref[...]
    mid = grad_after + norm_back(grad, gain_ref[...].astype(F32), xhat, rstd)
    mid_ref[...] = mid
    ga_ref[...] = mid.astype(BF16)
    sums_ref[0] += eight(mid)
    sums_ref[1] += eight(grad * xhat)
    sums_ref[2] += eight(grad)
    sums_ref[3] += eight(grad_after)


def first_norm_back(own_ref, near_ref, start_ref, mid1_ref, mid2_ref, gain_ref, out_ref, sums_ref):
    @pl.when(pl.program_id(0) == 0)
    def _():
        sums_ref[...] = jnp.zeros_like(sums_ref)

    grad = own_ref[...] + near_ref[...].astype(F32)
    xhat, rstd = normalize(start_ref[...])
    mid = jnp.where(pl.program_id(0) * 2 < pl.num_programs(0), mid1_ref[...], mid2_ref[...])
    out_ref[...] = (mid + norm_back(grad, gain_ref[...].astype(F32), xhat, rstd)).astype(BF16)
    sums_ref[0] += eight(grad * xhat)
    sums_ref[1] += eight(grad)


def down_out(act_n_ref, act_c1_ref, act_c2_ref, w_ref, out_ref):
    half = act_c1_ref.shape[0]
    out_ref[0] = mm(act_n_ref[...], w_ref[...]).astype(BF16)
    out_ref[1, :half, :] = mm(act_c1_ref[...], w_ref[...]).astype(BF16)
    out_ref[1, half:, :] = mm(act_c2_ref[...], w_ref[...]).astype(BF16)


def down_in(act_o_ref, act_f1_ref, act_f2_ref, after1_ref, after2_ref, got_ref, b_ref, w_ref, base_ref, far_ref):
    half = act_f1_ref.shape[0]
    for piece, act_ref, after_ref in ((0, act_f1_ref, after1_ref), (1, act_f2_ref, after2_ref)):
        at = slice(piece * half, (piece + 1) * half)
        down = mm(act_o_ref[at, :], w_ref[...]) + got_ref[0, at, :].astype(F32)
        base_ref[at, :] = after_ref[...] + down + b_ref[...].astype(F32)
        far_ref[at, :] = (mm(act_ref[...], w_ref[...]) + got_ref[1, at, :].astype(F32)).astype(BF16)


def finish(base_ref, far_ref, ok_ref, out_ref):
    out_ref[...] = ((base_ref[...] + far_ref[...].astype(F32)) * ok_ref[...]).astype(BF16)


def hand_on(in_ref, out_ref):
    out_ref[...] = in_ref[...]


def hand_on_all(*refs):
    count = len(refs) // 2
    for in_ref, out_ref in zip(refs[:count], refs[count:]):
        out_ref[...] = in_ref[...]


def handed(value, after):
    return run(hand_on, "hand_on", [value], [(value.shape, value.dtype)], after)


def small_first(two_ref, more_ref, one_ref, out_ref):
    out_ref[...] = jnp.zeros_like(out_ref)
    two = [two_ref[at] + more_ref[at] for at in range(4)]
    rows = [two[0], one_ref[0], one_ref[1], two[1], two[2], two[3]]
    for at, part in enumerate(rows):
        out_ref[at:at + 1, :] = jnp.sum(part, axis=0, keepdims=True)


def small_second(own_ref, near_ref, bias_a_ref, bias_b_ref, send_ref, keep_ref):
    total = own_ref[...] + near_ref[...]
    wide = bias_a_ref.shape[1]
    for out_ref, bias_ref in ((send_ref, bias_b_ref), (keep_ref, bias_a_ref)):
        out_ref[...] = total
        out_ref[6:7, :wide] = bias_ref[0:1, :]
        out_ref[6:7, wide:2 * wide] = bias_ref[4:5, :]


def small_third(own_ref, far_ref, *refs):
    out_ref = refs[-1]
    out_ref[...] = own_ref[...] + far_ref[...]
    out_ref[7:8, :] = sum(jnp.sum(part[...], axis=0, keepdims=True) for part in refs[:-1])


def small_add(own_ref, far_ref, out_ref):
    out_ref[...] = own_ref[...] + far_ref[...]


def add_two(left_ref, right_ref, out_ref):
    out_ref[...] = add_low(left_ref[...], right_ref[...])


def token_products(pieces_of, form, side_ref, *refs):
    count = len(pieces_of)
    lefts, rights, rest = refs[:count], refs[count:2 * count], refs[2 * count:]
    block = 256
    steps = lefts[0].shape[1] // block
    for i in range(steps):
        first = i < steps // 2
        if form == "base":
            row = i
        else:
            row = i % (steps // 2) + (1 - side_ref[0] if first else side_ref[0]) * (steps // 2)
        at = pl.ds(row * block if form == "base" else pl.multiple_of(row * block, block), block)
        total = sum(
            mm(
                left[lp * tokens:(lp + 1) * tokens, at],
                right[rp * tokens:(rp + 1) * tokens, :],
                TN,
            )
            for left, right, (lp, rp, tokens) in zip(lefts, rights, pieces_of)
        )
        into = slice(i % (steps // 2) * block, (i % (steps // 2) + 1) * block)
        if form == "base":
            rest[0][at, :] = total
            continue
        if form == "based":
            total = total + rest[0][at, :]
        rest[-2 if first else -1][into, :] = total.astype(BF16)


def token_call(sides, pairs, base, after):
    tall, wide = pairs[0][0].shape[1], pairs[0][2].shape[1]
    form = "base" if base is True else "full" if base is None else "based"
    args = [sides] + [pair[0] for pair in pairs] + [pair[2] for pair in pairs]
    if form == "based":
        args.append(base)
    outs = [((tall, wide), F32)] if form == "base" else [((tall // 2, wide), BF16)] * 2
    pieces_of = [(pair[1], pair[3], pair[4]) for pair in pairs]
    kernel = functools.partial(token_products, pieces_of, form)
    return run(kernel, "token_products", args, outs, after, scalars=1, cost=60)


def three_products(x_ref, gp_ref, q_ref, kv_ref):
    q_ref[...] = mm(x_ref[...], gp_ref[0]).astype(BF16)
    for c in range(2):
        kv_ref[c] = mm(x_ref[...], gp_ref[c + 1]).astype(BF16)


def three_call(x_turned, gp, after):
    tall, seq = x_turned.shape
    wide = gp.shape[2]
    block = 256
    return run(
        three_products,
        "three_products",
        [x_turned, gp],
        [((tall, wide), BF16), ((2, tall, wide), BF16)],
        after,
        grid=(tall // block,),
        in_specs=[pl.BlockSpec((block, seq), lambda i: (i, 0)), pl.BlockSpec(gp.shape, lambda i: (0, 0, 0))],
        out_specs=[
            pl.BlockSpec((block, wide), lambda i: (i, 0)),
            pl.BlockSpec((2, block, wide), lambda i: (0, i, 0)),
        ],
    )


def turned_product(mixed_ref, ga_ref, out_ref):
    out_ref[...] = mm(ga_ref[...], mixed_ref[...], TN).astype(BF16)


def back_project(flip, core_ref, gp_a_ref, gp_b_ref, w_a_ref, w_b_ref, out_ref):
    rows = out_ref.shape[0]
    at = pl.ds(pl.multiple_of(jnp.bitwise_xor(core_ref[0], flip) * rows, rows), rows)
    out = sum(
        mm(gp_ref[c, at, :], w_ref[c], NT)
        for c in range(3)
        for gp_ref, w_ref in ((gp_a_ref, w_a_ref), (gp_b_ref, w_b_ref))
    )
    out_ref[...] = out.astype(out_ref.dtype)


def by_rows(kernel, name, args, outs, after, block=128, rows=None, piece=0, halves=(), token=False):
    rows = rows or args[0].shape[0]
    steps = rows // block

    def spec(shape, at=None):
        rest = (0,) * (len(shape) - 1)
        cut = (block,) + tuple(shape[1:])
        if at in halves:
            first = halves.index(at) * steps // 2
            return pl.BlockSpec(cut, lambda i: (jnp.clip(i - first, 0, steps // 2 - 1),) + rest)
        if shape[0] == rows:
            return pl.BlockSpec(cut, lambda i: (i,) + rest)
        if shape[0] == 2 * rows:
            return pl.BlockSpec(cut, lambda i: (i + piece * steps,) + rest)
        return pl.BlockSpec(tuple(shape), lambda i: (0,) * len(shape))

    return run(
        kernel,
        name,
        args,
        outs,
        after,
        grid=(steps,),
        in_specs=[spec(arg.shape, at) for at, arg in enumerate(args)],
        out_specs=[spec(shape) for shape, _ in outs],
        size=1,
        token=token,
    )


def fold(bit, last, side_ref, cur_ref, got_ref, *out_refs):
    if last:
        out_refs[0][...] = add_low(cur_ref[...], got_ref[...])
        return
    half = got_ref.shape[0] // 2
    for side, out_ref in ((1 - side_ref[bit], out_refs[0]), (side_ref[bit], out_refs[1])):
        at = pl.ds(pl.multiple_of(side * half, half), half)
        out_ref[...] = add_low(cur_ref[at, :], got_ref[at, :])


def begin_pair(paired, side_ref, *refs):
    send_ref, keep_ref = refs[-2:]
    if paired:
        parts = [(refs[0].at[c], refs[1].at[c]) for c in range(2)]
    else:
        parts = [refs[0:1], refs[1:3]]
    for side in range(2):

        @pl.when(side_ref[0] == side)
        def _():
            for part, out_ref in ((parts[1 - side], send_ref), (parts[side], keep_ref)):
                out_ref[...] = part[0][...] if len(part) == 1 else add_low(part[0][...], part[1][...])


def join(left_ref, right_ref, out_ref):
    rows = left_ref.shape[0]
    out_ref[:rows, :] = left_ref[...]
    out_ref[rows:, :] = right_ref[...]


def place(piece, spot_ref, own_ref, other_ref, out_ref):
    count = own_ref.shape[0] // piece
    steps = out_ref.shape[0] // piece
    for at in range(steps):
        apart = jnp.bitwise_xor(pl.program_id(0) * steps + at, spot_ref[0])
        rows = pl.ds(pl.multiple_of(jnp.bitwise_and(apart, count - 1) * piece, piece), piece)
        far_side = apart >= count
        into = slice(at * piece, (at + 1) * piece)

        @pl.when(far_side)
        def _():
            out_ref[into, :] = other_ref[rows, :].astype(F32)

        @pl.when(jnp.logical_not(far_side))
        def _():
            out_ref[into, :] = own_ref[rows, :].astype(F32)


def pieces(count, spot, own_ref, other_ref, first, steps):
    piece = own_ref.shape[0] // count
    for at in range(steps):
        apart = jnp.bitwise_xor(first + at, spot)
        rows = pl.ds(pl.multiple_of(jnp.bitwise_and(apart, count - 1) * piece, piece), piece)
        mine, others = own_ref[rows, :].astype(F32), other_ref[rows, :].astype(F32)
        yield at * piece, piece, jnp.where(apart >= count, others, mine)


def place_turned(count, spot_ref, own_ref, other_ref, w_out_ref, part_ref):
    for at, piece, value in pieces(count, spot_ref[0], own_ref, other_ref, 0, count):
        w_out_ref[:, at:at + piece] = value.T
    for at, piece, value in pieces(count, spot_ref[0], own_ref, other_ref, count, count):
        part_ref[at:at + piece, :] = value


def place_two(count, spot_ref, own_ref, other_ref, _, out_ref):
    for at, piece, value in pieces(count, spot_ref[0], own_ref, other_ref, pl.program_id(0) * count, count):
        out_ref[at:at + piece, :] = value


class Sum:
    def __init__(self, size, height, first=0):
        self.size, self.bits, self.height = size, size.bit_length() - 1, height
        me = lax.axis_index("dp")
        order = [(first + step) % self.bits for step in range(self.bits)]
        self.flips = [1 << b for b in order]
        sides = [(me // flip) % 2 for flip in self.flips]
        self.sides = jnp.stack(sides).astype(jnp.int32)
        self.spot = sum(side << (self.bits - 1 - step) for step, side in enumerate(sides))

    def begin(self, send, keep):
        self.keep, self.step = keep, 0
        self.sent = swap(send, "dp", self.size, self.flips[0])

    def begin_pairs(self, arrays, after):
        shape = arrays[0].shape[-2:]
        send, keep = run(
            functools.partial(begin_pair, len(arrays) == 2), "begin_pair", [self.sides] + list(arrays),
            [(shape, BF16)] * 2, after, scalars=1,
        )
        self.begin(send, keep)
        return keep

    def fold(self, after):
        if self.step >= self.bits:
            return after
        self.step += 1
        last = self.step == self.bits
        rows, columns = self.sent.shape
        kernel = functools.partial(fold, self.step, last)
        outs = [((rows, columns), BF16)] if last else [((rows // 2, columns), BF16)] * 2
        out = run(kernel, "fold", [self.sides, self.keep, self.sent], outs, after, scalars=1, cost=60)
        self.keep = out if last else out[1]
        send = out if last else out[0]
        self.sent = swap(send, "dp", self.size, self.flips[min(self.step, self.bits - 1)])
        return self.keep

    def spread(self, after):
        if self.step < self.bits:
            return after
        bit = 2 * self.bits - 2 - self.step
        rows, columns = self.keep.shape
        self.keep = run(join, "join", [self.keep, self.sent], [((2 * rows, columns), BF16)], after)
        self.sent = swap(self.keep, "dp", self.size, self.flips[bit])
        self.step += 1
        return self.keep

    def complete(self, after):
        while self.step < self.bits:
            after = self.fold(after)
        while self.step < 2 * self.bits - 1:
            after = self.spread(after)
        return after

    def place(self, after):
        after = self.complete(after)
        rows, columns = self.keep.shape
        piece = rows * 2 // self.size
        placed, token = run(
            functools.partial(place, piece),
            "place",
            [self.spot.reshape(1).astype(jnp.int32), self.keep, self.sent],
            [((2 * rows, columns), F32)],
            after,
            grid=(2,),
            size=1,
            token=True,
            in_specs=[
                pl.BlockSpec(memory_space=pltpu.SMEM),
                pl.BlockSpec((rows, columns), lambda i: (0, 0)),
                pl.BlockSpec((rows, columns), lambda i: (0, 0)),
            ],
            out_specs=[pl.BlockSpec((rows, columns), lambda i: (i, 0))],
        )
        return placed[: self.height], token

    def place_out(self, after):
        after = self.complete(after)
        rows, columns = self.keep.shape
        return run(
            functools.partial(place_turned, self.size // 2),
            "place_turned",
            [self.spot.reshape(1).astype(jnp.int32), self.keep, self.sent],
            [((columns, rows), F32), ((3 * rows, columns), F32)],
            after,
            grid=(1,),
            size=1,
            token=True,
            in_specs=[pl.BlockSpec(memory_space=pltpu.SMEM)]
            + [pl.BlockSpec((rows, columns), lambda i: (0, 0))] * 2,
            out_specs=[
                pl.BlockSpec((columns, rows), lambda i: (0, 0)),
                pl.BlockSpec((rows, columns), lambda i: (0, 0)),
            ],
        )

    def place_rest(self, into, after):
        after = self.complete(after)
        rows, columns = self.keep.shape
        return run(
            functools.partial(place_two, self.size // 2),
            "place_two",
            [self.spot.reshape(1).astype(jnp.int32), self.keep, self.sent, into],
            [((3 * rows, columns), F32)],
            after,
            grid=(2,),
            size=1,
            in_specs=[pl.BlockSpec(memory_space=pltpu.SMEM)]
            + [pl.BlockSpec((rows, columns), lambda i: (0, 0))] * 2
            + [pl.BlockSpec(memory_space=pl.ANY)],
            out_specs=[pl.BlockSpec((rows, columns), lambda i: (i + 1, 0))],
            aliases={3: 0},
        )


def gelu_and_slope(up):
    size = jnp.abs(up)
    t = 1.0 / (1.0 + (0.3275911 * 0.7071067811865476) * size)
    bell = jnp.exp(-0.5 * up * up)
    poly = t * (
        0.5 * 0.254829592
        + t * (0.5 * -0.284496736 + t * (0.5 * 1.421413741 + t * (0.5 * -1.453152027 + t * (0.5 * 1.061405429))))
    )
    tail = poly * bell
    cdf = jnp.where(up >= 0.0, 1.0 - tail, tail)
    return up * cdf, cdf + up * bell * 0.3989422804014327


def feed(count, piece, *refs):
    n2_refs, (gd_ref, ok_ref, w_up_ref, b_up_ref, w_down_ref, gn2_ref, act_ref, gup_ref, gb_ref) = refs[:count], refs[count:]
    hidden, rows, step = w_up_ref.shape[1], n2_refs[0].shape[0], 256

    def products(block, at):
        part = slice(at, at + step)
        given = slice((piece + block) * rows, (piece + block + 1) * rows)
        up = mm(n2_refs[block][...], w_up_ref[:, part]) + b_up_ref[:, part].astype(F32)
        return up, mm(gd_ref[given, :], w_down_ref[part, :], NT), ok_ref[given, :]

    def rest(block, at, up, grad_act, ok):
        part, into = slice(at, at + step), slice(block * rows, (block + 1) * rows)
        act, slope = gelu_and_slope(up)
        grad_up = (slope * (grad_act * ok)).astype(BF16)
        act_ref[into, part] = (act * ok).astype(BF16)
        gup_ref[into, part] = grad_up
        total = jnp.sum(grad_up.astype(F32).reshape(rows // 8, 8, step), axis=0)
        gb_ref[:, part] = total if block == 0 else gb_ref[:, part] + total
        if at + step == hidden:
            gn2_ref[into, :] = mm(gup_ref[into, :], w_up_ref[...], NT).astype(BF16)

    waiting = None
    for block in range(count):
        for at in range(0, hidden, step):
            made = products(block, at)
            if waiting is not None:
                rest(*waiting)
            waiting = (block, at) + made
    rest(*waiting)


def feed_call(n2_pieces, gd, ok, piece, w_up, b_up, w_down, after):
    hidden, count = w_up.shape[1], len(n2_pieces)
    rows = n2_pieces[0].shape[0] * count
    return run(
        functools.partial(feed, count, piece),
        "feed",
        list(n2_pieces) + [gd, ok, w_up, b_up, w_down],
        [((rows, D), BF16), ((rows, hidden), BF16), ((rows, hidden), BF16), ((8, hidden), F32)],
        after,
    )


def swap(value, axis, size, flip):
    return lax.ppermute(value, axis, [(i, i ^ flip) for i in range(size)])


def add_low(left, right):
    return (left.astype(F32) + right.astype(F32)).astype(BF16)


def sum_over(value, axis, size):
    flip = 1
    while flip < size:
        value = value + swap(value, axis, size, flip)
        flip *= 2
    return value


def on_device(
    dp_size,
    mp_size,
    tokens,
    segment_ids,
    valid_mask,
    patch_index,
    gsd_index,
    w_qkv,
    bias_qv,
    w_out,
    b_out,
    gain_one,
    shift_one,
    gain_two,
    shift_two,
    w_up,
    b_up,
    w_down,
    b_down,
    cotangent,
):
    own_rows = tokens.shape[0]
    mp = lax.axis_index("mp")
    core = mp % 2
    row = mp // 2

    def near(value):
        return swap(value, "mp", mp_size, 1)

    def far(value):
        return swap(value, "mp", mp_size, 2)

    core_s = core.reshape(1).astype(jnp.int32)
    down_sum, up_sum = Sum(dp_size, w_down.shape[0]), Sum(dp_size, w_up.shape[0])
    first_sum, second_sum = Sum(dp_size, 2 * D), Sum(dp_size, 2 * D)
    sides = down_sum.sides

    cot_near = near(cotangent)
    inputs = [segment_ids, valid_mask, patch_index, gsd_index]
    shape = (3, D // 4, w_qkv.shape[2])
    piece_a, piece_b = run(cut, "cut", [sides, w_qkv], [(shape, BF16)] * 2, None, scalars=1, size=1)
    segment_ids, valid_mask, patch_index, gsd_index = run(
        hand_on_all, "hand_on_all", inputs, [(part.shape, part.dtype) for part in inputs], piece_b, size=1
    )
    far_bias = far(bias_qv)
    far_a, far_b = far(piece_a), far(piece_b)

    own_start = mp * own_rows
    level = image_levels(segment_ids, gsd_index)
    codes = jnp.stack([patch_index // GRID, patch_index % GRID]) * GSDS + level
    own_codes = lax.dynamic_slice_in_dim(codes.reshape(2, -1, 1), own_start, own_rows, axis=1)
    all_valid = valid_mask.reshape(-1, 1).astype(F32)

    def valid_of(flip):
        at = jnp.bitwise_xor(mp, flip) * own_rows
        return lax.dynamic_slice_in_dim(all_valid, at, own_rows)

    own_valid = valid_of(0)

    row_seg = lax.dynamic_index_in_dim(segment_ids, row, 0, keepdims=True)
    row_ok = lax.dynamic_index_in_dim(valid_mask, row, 0, keepdims=True)
    seg_k = jnp.where(row_ok == 1, row_seg, -1)
    seg_q = row_seg.reshape(-1, 1)

    start_sum, normed = by_rows(
        front, "front",
        [tokens, own_codes[0], own_codes[1], code_table(), gain_one[None], shift_one[None]],
        [(tokens.shape, F32), (tokens.shape, BF16)], [segment_ids, cot_near],
    )
    half = (own_rows, D)
    w_out_sent, a_pass = run(
        hand_on_all, "hand_on_all", [w_out, far_a], [(w_out.shape, BF16), (far_a.shape, BF16)], normed, cost=60
    )
    far_out = far(w_out_sent)
    other_a = swap(a_pass, "dp", dp_size, 1)
    normed_row = run(in_row, "in_row", [core_s, normed, near(normed)], [((2 * own_rows, D), BF16)], a_pass, scalars=1)
    b_pass, cot_sent = run(
        hand_on_all, "hand_on_all", [far_b, cotangent], [(far_b.shape, BF16), (half, BF16)], normed_row
    )
    other_b = swap(b_pass, "dp", dp_size, 1)
    cot_far = far(cot_sent)

    qkv_a, mixed_a, lse_a = forward_call(sides, seg_q, seg_k, normed_row, bias_qv, [w_qkv], cot_sent)
    pieces_b = [a_pass, b_pass, other_a, other_b]
    qkv_b, mixed_b, lse_b = forward_call(sides, seg_q, seg_k, normed_row, far_bias, pieces_b, lse_a)
    operands = [core_s, mixed_a, mixed_b, w_out, far_out]
    attn_near = run(functools.partial(project_out, 1), "project_out", operands, [(half, BF16)], lse_b, scalars=1)
    attn_own = run(functools.partial(project_out, 0), "project_out", operands, [(half, F32)], attn_near, scalars=1)
    attn_got = near(attn_near)
    quarter = own_rows // 2
    piece_shape = (quarter, D)
    wide = w_qkv.shape[2]
    turned = [((D, wide), BF16)]
    tile = [((8, D), F32)]
    flips = [1 << b for b in range(dp_size.bit_length() - 1)]
    b_up_row = b_up[None, :]
    ffn = [w_up, b_up_row, w_down]
    last = attn_own

    def norm_two(piece, last):
        return by_rows(
            second_norm, "second_norm",
            [start_sum, attn_own, attn_got, b_out[None], gain_two[None], shift_two[None]],
            [(piece_shape, F32), (piece_shape, BF16)], last, rows=quarter, piece=piece,
        )

    def norm_two_back(piece, from_far, after_attn, last):
        return by_rows(
            second_norm_back, "second_norm_back",
            [gn2_o, from_near, from_far, after_attn, cotangent, own_valid, gain_two[None]],
            [(piece_shape, F32), (piece_shape, BF16), ((4, 8, D), F32)], last, rows=quarter, piece=piece,
        )

    operands = [core_s, None, None, w_qkv, None]
    after1, n2_1 = norm_two(0, last)
    far1, near1 = far(n2_1), near(n2_1)
    last = n2_1
    after2, n2_2 = norm_two(1, last)
    far2, near2 = far(n2_2), near(n2_2)
    last = n2_2
    gn2_o, act_o, gup_o, gb_o = feed_call([n2_1, n2_2], cotangent, own_valid, 0, *ffn, last)
    last = gb_o
    last = cot_pass = handed(cot_far, last)
    cot_cross = near(cot_pass)
    gn2_n, act_n, gup_n, gb_n = feed_call([near1, near2], cot_near, valid_of(1), 0, *ffn, last)
    from_near = near(gn2_n)
    last = gb_n
    here = [(act_o, 0, cotangent, 0, own_rows), (act_n, 0, cot_near, 0, own_rows)]
    last = down_here = token_call(sides, here, True, last)
    last = far1_pass = handed(far1, last)
    cross1 = near(far1_pass)
    gn2_f1, act_f1, gup_f1, gb_f1 = feed_call([far1_pass], cot_pass, valid_of(2), 0, *ffn, last)
    last = gb_f1
    gn2_c1, act_c1, gup_c1, gb_c1 = feed_call([cross1], cot_cross, valid_of(3), 0, *ffn, last)
    got1 = near(gn2_c1)
    last = gb_c1
    last = far2_pass = handed(far2, last)
    cross2 = near(far2_pass)
    last = sent1 = by_rows(add_two, "add_two", [gn2_f1, got1], [(piece_shape, BF16)], last)
    back1 = far(sent1)
    gn2_f2, act_f2, gup_f2, gb_f2 = feed_call([far2_pass], cot_pass, valid_of(2), 1, *ffn, last)
    last = gb_f2
    gn2_c2, act_c2, gup_c2, gb_c2 = feed_call([cross2], cot_cross, valid_of(3), 1, *ffn, last)
    got2 = near(gn2_c2)
    last = gb_c2
    there = [(act_f1, 0, cot_pass, 0, quarter), (act_c1, 0, cot_cross, 0, quarter)]
    there += [(act_f2, 0, cot_pass, 1, quarter), (act_c2, 0, cot_cross, 1, quarter)]
    down_send, down_keep = token_call(sides, there, down_here, last)
    down_sum.begin(down_send, down_keep)
    last = down_keep
    last = sent2 = by_rows(add_two, "add_two", [gn2_f2, got2], [(piece_shape, BF16)], last)
    back2 = far(sent2)
    mid1, ga1, sums_two = norm_two_back(0, back1, after1, last)
    ga1_near = near(ga1)
    last = ga1
    pairs = [(n2_1, 0, gup_o, 0, quarter), (n2_2, 0, gup_o, 1, quarter)]
    pairs += [(near1, 0, gup_n, 0, quarter), (near2, 0, gup_n, 1, quarter)]
    pairs += [(far1_pass, 0, gup_f1, 0, quarter), (cross1, 0, gup_c1, 0, quarter)]
    pairs += [(far2_pass, 0, gup_f2, 0, quarter), (cross2, 0, gup_c2, 0, quarter)]
    up_send, up_keep = token_call(sides, pairs, None, last)
    up_sum.begin(up_send, up_keep)
    last = up_keep
    mid2, ga2, sums_more = norm_two_back(1, back2, after2, last)
    ga2_near = near(ga2)
    last = ga2
    last = x_turned = run(turn, "turn", [normed_row], [((D, 2 * own_rows), BF16)], last, cost=60)
    last = far_qkv = run(assemble, "assemble", [sides] + pieces_b, [(w_qkv.shape, BF16)], last, scalars=1, cost=60)
    last = ga_row = run(
        in_row_pieces, "in_row", [core_s, ga1, ga2, ga1_near, ga2_near], [((2 * own_rows, D), BF16)], last, scalars=1
    )
    last = gw_out_b = run(turned_product, "turned_product", [mixed_b, ga_row], turned, last)
    far_out_grad = far(gw_out_b)
    last = gw_out_a = run(turned_product, "turned_product", [mixed_a, ga_row], turned, last)
    last = down_sum.fold(last)
    gp_b, bias_b = backward_call(seg_q, seg_k, ga_row, far_out, qkv_b, lse_b, last)
    last = bias_b
    q_b, kv_b = three_call(x_turned, gp_b, last)
    far_q, far_kv = far(q_b), far(kv_b)
    last = q_b
    last = out_both = by_rows(add_two, "add_two", [gw_out_a, far_out_grad], [((D, wide), BF16)], last, block=512)
    last = down_sum.fold(last)
    gp_a, bias_a = backward_call(seg_q, seg_k, ga_row, w_out, qkv_a, lse_a, last)
    last = bias_a
    last = up_sum.fold(last)
    q_a, kv_a = three_call(x_turned, gp_a, last)
    last = q_a
    last = down_sum.fold(last)
    last = first_sum.begin_pairs([out_both, q_a, far_q], last)
    operands[1:3] = gp_a, gp_b
    operands[4] = far_qkv
    last = gn_near = run(functools.partial(back_project, 1), "back_project", operands, [(half, BF16)], last, scalars=1)
    operands[1:3] = gp_a, gp_b
    operands[4] = far_qkv
    last = gn_own = run(functools.partial(back_project, 0), "back_project", operands, [(half, F32)], last, scalars=1)
    grad_tokens, sums_one = by_rows(
        first_norm_back, "first_norm_back",
        [gn_own, near(gn_near), start_sum, mid1, mid2, gain_one[None]],
        [(half, BF16), ((2, 8, D), F32)], last, halves=(3, 4),
    )
    last = sums_one
    last = down_sent = run(down_out, "down_out", [act_n, act_c1, act_c2, w_down], [((2,) + half, BF16)], last)
    down_near = near(down_sent)
    last = up_sum.fold(last)
    last = down_sum.spread(last)
    last = second_sum.begin_pairs([kv_a, far_kv], last)
    down_base, down_far = run(
        down_in, "down_in", [act_o, act_f1, act_f2, after1, after2, down_near, b_down[None], w_down],
        [(half, F32), (half, BF16)], last,
    )
    last = down_base
    last = small = run(small_first, "small_first", [sums_two, sums_more, sums_one], tile, last)
    small_got = near(small)
    last = up_sum.fold(last)
    last = first_sum.fold(last)
    last = down_sum.spread(last)
    last = second_sum.fold(last)
    send, small = run(small_second, "small_second", [small, small_got, bias_a, bias_b], tile * 2, last)
    small_got = far(send)
    last = small
    last = up_sum.spread(last)
    last = first_sum.fold(last)
    last = second_sum.fold(last)
    gbs = [gb_o, gb_n, gb_f1, gb_c1, gb_f2, gb_c2]
    last = small = run(small_third, "small_third", [small, small_got] + gbs, tile, last)
    small_got = swap(small, "dp", dp_size, flips[0])
    last = first_sum.fold(last)
    last = up_sum.spread(last)
    last = second_sum.fold(last)
    last = first_sum.spread(last)
    last = down_sent = handed(down_far, last)
    down_got = far(down_sent)
    last = second_sum.spread(last)
    grad_w_down, last = down_sum.place(last)
    last = first_sum.spread(last)
    last = small = run(small_add, "small_add", [small, small_got], tile, last)
    small_got = swap(small, "dp", dp_size, flips[1])
    last = second_sum.spread(last)
    last = small = run(small_add, "small_add", [small, small_got], tile, last)
    small_got = swap(small, "dp", dp_size, flips[2])
    grad_w_up, last = up_sum.place(last)
    layer_out, last = by_rows(
        finish, "finish", [down_base, down_got, own_valid], [(half, BF16)], last, token=True
    )
    for flip in flips[3:]:
        last = small = run(small_add, "small_add", [small, small_got], tile, last)
        small_got = swap(small, "dp", dp_size, flip)
    last = small = run(small_add, "small_add", [small, small_got], tile, last)
    grad_w_out, grad_w_qkv, last = first_sum.place_out(last)
    grad_w_qkv = second_sum.place_rest(grad_w_qkv, last).reshape(w_qkv.shape)
    grad_bias_qv = small[6, : 2 * wide].reshape(2, wide)
    grad_b_up = small[7]
    return (
        layer_out,
        grad_tokens,
        grad_w_qkv,
        grad_bias_qv,
        grad_w_out,
        small[0],
        small[1],
        small[2],
        small[3],
        small[4],
        grad_w_up,
        grad_b_up,
        grad_w_down,
        small[5],
    )


def solution(mesh):
    return jax.shard_map(
        functools.partial(on_device, mesh.shape["dp"], mesh.shape["mp"]),
        mesh=mesh,
        in_specs=(
            P(("dp", "mp"), None),
            P("dp", None),
            P("dp", None),
            P("dp", None),
            P("dp", None),
            P(None, None, "mp"),
            P(None, "mp"),
            P("mp", None),
            P(),
            P(),
            P(),
            P(),
            P(),
            P(None, "mp"),
            P("mp"),
            P("mp", None),
            P(),
            P(("dp", "mp"), None),
        ),
        out_specs=(
            P(("dp", "mp"), None),
            P(("dp", "mp"), None),
            P(None, None, "mp"),
            P(None, "mp"),
            P("mp", None),
            P(),
            P(),
            P(),
            P(),
            P(),
            P(None, "mp"),
            P("mp"),
            P("mp", None),
            P(),
        ),
        check_vma=False,
    )
```

```python
import functools
import jax
import jax.numpy as jnp
from jax import lax
from jax.experimental import pallas as pl
from jax.experimental.pallas import tpu as pltpu
from jax.sharding import PartitionSpec as P

D = 1024
HEAD = 64
SEGS = 16
GRID = 14
GSDS = 8
EPSILON = 1e-06
MASKED = -1000000000.0
SCALE = HEAD ** (-0.5)
BQ = 128
PAIR = 2 * HEAD
F32 = jnp.float32
BF16 = jnp.bfloat16
NN = (((1,), (0,)), ((), ()))
NT = (((1,), (1,)), ((), ()))
TN = (((0,), (0,)), ((), ()))


def mm(left, right, dims=NN):
    return lax.dot_general(left, right, dims, preferred_element_type=F32)


def image_levels(segment_ids, gsd_index):
    in_image = segment_ids[..., None] == jnp.arange(SEGS, dtype=jnp.int32)
    return jnp.sum(jnp.where(in_image, gsd_index[:, None, :], 0), axis=-1)


def code_table():
    quarter = D // 4
    frequency = 1.0 / 10000.0 ** (jnp.arange(quarter, dtype=jnp.float32) / quarter)
    ratio = 2.0 ** (0.5 * jnp.arange(GSDS, dtype=jnp.float32) - 1.0)
    place = jnp.arange(16, dtype=jnp.float32)
    angle = (place[:, None] * ratio[None, :]).reshape(-1, 1) * frequency
    return jnp.concatenate([jnp.sin(angle), jnp.cos(angle)], axis=-1)


def front(tokens_ref, row_ref, col_ref, table_ref, gain_ref, shift_ref, start_ref, normed_ref):
    high = table_ref[...].astype(BF16)
    rest = table_ref[...] - high.astype(F32)
    middle = rest.astype(BF16)
    low = (rest - middle.astype(F32)).astype(BF16)
    spots = lax.broadcasted_iota(jnp.int32, (tokens_ref.shape[0], table_ref.shape[0]), 1)
    half = table_ref.shape[1]
    for at, index_ref in ((0, row_ref), (half, col_ref)):
        chosen = (spots == index_ref[...]).astype(F32).astype(BF16)
        code = (mm(chosen, low) + mm(chosen, middle)) + mm(chosen, high)
        start_ref[:, at:at + half] = tokens_ref[:, at:at + half].astype(F32) + code
    xhat, _ = normalize(start_ref[...])
    normed_ref[...] = (xhat * gain_ref[...].astype(F32) + shift_ref[...].astype(F32)).astype(BF16)


def normalize(values):
    row_mean = jnp.mean(values, axis=-1, keepdims=True)
    centred = values - row_mean
    row_var = jnp.mean(centred * centred, axis=-1, keepdims=True)
    rstd = lax.rsqrt(row_var + EPSILON)
    return centred * rstd, rstd


def norm_back(grad, gain, xhat, rstd):
    scaled = grad * gain
    mean_scaled = jnp.mean(scaled, axis=-1, keepdims=True)
    mean_along = jnp.mean(scaled * xhat, axis=-1, keepdims=True)
    return rstd * (scaled - mean_scaled - xhat * mean_along)


def window_start(block, seq, width):
    return min(max(block * BQ - BQ, 0), seq - width)


def fill_bias(seg_q_ref, seg_k_ref, bias_ref, seq, width):
    for block in range(seq // BQ):
        start = window_start(block, seq, width)
        seg_q = seg_q_ref[block * BQ:(block + 1) * BQ, :]
        seg_k = seg_k_ref[:, start:start + width]
        row = lax.broadcasted_iota(jnp.int32, (BQ, width), 0) + block * BQ
        col = lax.broadcasted_iota(jnp.int32, (BQ, width), 1) + start
        allowed = (seg_q == seg_k) | (row == col)
        bias_ref[block] = jnp.where(allowed, 0.0, MASKED)


def split_heads(tile):
    low = lax.broadcasted_iota(jnp.int32, tile.shape, 1) < HEAD
    zero = jnp.zeros_like(tile)
    return jnp.concatenate([jnp.where(low, tile, zero), jnp.where(low, zero, tile)], axis=0)


def join_heads(stacked):
    half = stacked.shape[0] // 2
    low = lax.broadcasted_iota(jnp.int32, (half, PAIR), 1) < HEAD
    return jnp.where(low, stacked[:half], stacked[half:])


def piece_places(side_ref, w_refs, depth):
    if len(w_refs) == 1:
        return [(slice(None), w_refs[0])]
    rows = depth // 4
    starts = [side_ref[0] * 2, side_ref[0] * 2 + 1, (1 - side_ref[0]) * 2, (1 - side_ref[0]) * 2 + 1]
    return [(pl.ds(pl.multiple_of(at * rows, rows), rows), w_ref) for at, w_ref in zip(starts, w_refs)]


def assemble(side_ref, *refs):
    out_ref = refs[-1]
    for at, w_ref in piece_places(side_ref, refs[:-1], out_ref.shape[1]):
        out_ref[:, at, :] = w_ref[...]


def turn(in_ref, out_ref):
    out_ref[...] = in_ref[...].T


def cut(side_ref, w_ref, *out_refs):
    rows = w_ref.shape[1] // 4
    for piece, out_ref in enumerate(out_refs):
        at = pl.ds(pl.multiple_of((side_ref[0] * 2 + piece) * rows, rows), rows)
        out_ref[...] = w_ref[:, at, :]


def in_row(core_ref, own_ref, other_ref, out_ref):
    rows = own_ref.shape[0]
    for side, in_ref in ((core_ref[0], own_ref), (1 - core_ref[0], other_ref)):
        out_ref[pl.ds(pl.multiple_of(side * rows, rows), rows), :] = in_ref[...]


def in_row_pieces(core_ref, own1_ref, own2_ref, other1_ref, other2_ref, out_ref):
    rows = own1_ref.shape[0]
    for side, refs in ((core_ref[0], (own1_ref, own2_ref)), (1 - core_ref[0], (other1_ref, other2_ref))):
        for piece, in_ref in enumerate(refs):
            at = (side * 2 + piece) * rows
            out_ref[pl.ds(pl.multiple_of(at, rows), rows), :] = in_ref[...]


def attend_forward(side_ref, seg_q_ref, seg_k_ref, x_ref, b_ref, *refs):
    w_refs, (qkv_ref, mixed_ref, lse_ref, bias_ref) = refs[:-4], refs[-4:]
    seq = x_ref.shape[0]
    width = bias_ref.shape[2]
    wide = w_refs[0].shape[2]
    fill_bias(seg_q_ref, seg_k_ref, bias_ref, seq, width)
    for c in range(3):
        for r in range(0, seq, 256):
            out = sum(
                mm(x_ref[r:r + 256, at], w_ref[c]) for at, w_ref in piece_places(side_ref, w_refs, x_ref.shape[1])
            )
            if c != 1:
                out = out + b_ref[c // 2:c // 2 + 1, :].astype(F32)
            qkv_ref[c, r:r + 256, :] = out.astype(BF16)
    lane = lax.broadcasted_iota(jnp.int32, (BQ, PAIR), 1)
    pairs = range(wide // PAIR)
    for block in range(seq // BQ):
        start = window_start(block, seq, width)
        rows = slice(block * BQ, (block + 1) * BQ)
        keys = slice(start, start + width)
        bias = bias_ref[block]
        bias = jnp.concatenate([bias, bias], axis=0)
        lanes = [slice(pair * PAIR, (pair + 1) * PAIR) for pair in pairs]
        queries = [split_heads(qkv_ref[0, rows, at] * SCALE) for at in lanes]
        scores = [mm(queries[p], qkv_ref[1, keys, lanes[p]], NT) + bias for p in pairs]
        row_max = [jnp.max(part, axis=-1, keepdims=True) for part in scores]
        weight = [jnp.exp(scores[p] - row_max[p]) for p in pairs]
        mixed = [mm(weight[p].astype(BF16), qkv_ref[2, keys, lanes[p]]) for p in pairs]
        total = [jnp.sum(part, axis=-1, keepdims=True) for part in weight]
        lse_tile = jnp.zeros((BQ, PAIR), F32)
        for p in pairs:
            mixed_ref[rows, lanes[p]] = join_heads(mixed[p] * (1.0 / total[p])).astype(BF16)
            lse = row_max[p] + jnp.log(total[p])
            lse_tile = jnp.where(lane == 2 * p, lse[:BQ], lse_tile)
            lse_tile = jnp.where(lane == 2 * p + 1, lse[BQ:], lse_tile)
        lse_ref[rows, :] = lse_tile


def attend_backward(
    seg_q_ref, seg_k_ref, ga_ref, w_out_ref, qkv_ref, lse_ref, out_ref, sums_ref, bias_ref, gm_ref, acc_ref
):
    seq = ga_ref.shape[0]
    width = bias_ref.shape[2]
    wide = w_out_ref.shape[0]
    fill_bias(seg_q_ref, seg_k_ref, bias_ref, seq, width)
    for r in range(0, seq, 256):
        gm_ref[r:r + 256, :] = mm(ga_ref[r:r + 256, :], w_out_ref[...], NT).astype(BF16)
    acc_ref[...] = jnp.zeros_like(acc_ref)
    for block in range(seq // BQ):
        start = window_start(block, seq, width)
        rows = slice(block * BQ, (block + 1) * BQ)
        keys = slice(start, start + width)
        bias = bias_ref[block]
        bias = jnp.concatenate([bias, bias], axis=0)
        lse_tile = lse_ref[rows, :]
        pairs = range(wide // PAIR)
        lanes = [slice(pair * PAIR, (pair + 1) * PAIR) for pair in pairs]
        queries = [split_heads(qkv_ref[0, rows, at] * SCALE) for at in lanes]
        grad_mixed = [split_heads(gm_ref[rows, at]) for at in lanes]
        key_rows = [qkv_ref[1, keys, at] for at in lanes]
        scores = [mm(queries[p], key_rows[p], NT) + bias for p in pairs]
        grad_prob = [mm(grad_mixed[p], qkv_ref[2, keys, lanes[p]], NT) for p in pairs]
        lse = [
            jnp.concatenate([lse_tile[:, 2 * p:2 * p + 1], lse_tile[:, 2 * p + 1:2 * p + 2]], axis=0)
            for p in pairs
        ]
        prob = [jnp.exp(scores[p] - lse[p]) for p in pairs]
        along = [jnp.sum(prob[p] * grad_prob[p], axis=-1, keepdims=True) for p in pairs]
        grad_scores = [(prob[p] * (grad_prob[p] - along[p])).astype(BF16) for p in pairs]
        for p in pairs:
            acc_ref[1, keys, lanes[p]] += mm(prob[p].astype(BF16), grad_mixed[p], TN)
        for p in pairs:
            out_ref[0, rows, lanes[p]] = (join_heads(mm(grad_scores[p], key_rows[p])) * SCALE).astype(BF16)
            acc_ref[0, keys, lanes[p]] += mm(grad_scores[p], queries[p], TN)
    out_ref[1] = acc_ref[0].astype(BF16)
    out_ref[2] = acc_ref[1].astype(BF16)
    for at, c in enumerate((0, 2)):
        total = jnp.sum(out_ref[c].astype(F32), axis=0, keepdims=True)
        sums_ref[4 * at:4 * at + 4, :] = jnp.concatenate([total, jnp.zeros((3, wide), F32)], axis=0)


def chained(kernel, count, extra=1):
    def body(*refs):
        kernel(*refs[:count], *refs[count + extra:])

    return body


def with_token(kernel):
    def body(*refs):
        kernel(*refs[:-1])
        refs[-1][...] = jnp.zeros_like(refs[-1])

    return body


def run(kernel, name, args, outs, after, scalars=0, grid=None, in_specs=None, out_specs=None, scratch=(), aliases=None, cost=15, size=10**9, token=False):
    vmem = pl.BlockSpec(memory_space=pltpu.VMEM)
    if in_specs is None:
        in_specs = [pl.BlockSpec(memory_space=pltpu.SMEM)] * scalars + [vmem] * (len(args) - scalars)
    if out_specs is None:
        out_specs = [vmem] * len(outs)
    outs, out_specs = list(outs), list(out_specs)
    if token:
        outs.append(((8, 128), F32))
        out_specs.append(pl.BlockSpec((8, 128), lambda *_: (0, 0)) if grid is not None else vmem)
        kernel = with_token(kernel)
    if after is not None:
        behind = list(after) if isinstance(after, (list, tuple)) else [after]
        kernel = chained(kernel, len(args), len(behind))
        args = list(args) + behind
        in_specs = list(in_specs) + [pl.BlockSpec(memory_space=pl.ANY)] * len(behind)
    result = pl.pallas_call(
        kernel,
        name=name,
        grid=grid if grid is not None else (),
        out_shape=tuple(jax.ShapeDtypeStruct(shape, dtype) for shape, dtype in outs),
        in_specs=in_specs,
        out_specs=tuple(out_specs),
        scratch_shapes=list(scratch),
        input_output_aliases=aliases or {},
        compiler_params=pltpu.CompilerParams(vmem_limit_bytes=26 * 2**20),
        cost_estimate=pl.CostEstimate(flops=cost * 10**9, bytes_accessed=size, transcendentals=0),
    )(*args)
    return result if len(outs) > 1 else result[0]


def forward_call(sides, seg_q, seg_k, x, b, pieces_of, after):
    seq, wide = x.shape[0], pieces_of[0].shape[2]
    width = min(3 * BQ, seq)
    return run(
        attend_forward,
        "attend_forward",
        [sides, seg_q, seg_k, x, b] + list(pieces_of),
        [((3, seq, wide), BF16), ((seq, wide), BF16), ((seq, PAIR), F32)],
        after,
        cost=60,
        scalars=1,
        scratch=[pltpu.VMEM((seq // BQ, BQ, width), F32)],
    )


def backward_call(seg_q, seg_k, ga, w_out, qkv, lse, after):
    seq, wide = ga.shape[0], w_out.shape[0]
    width = min(3 * BQ, seq)
    return run(
        attend_backward,
        "attend_backward",
        [seg_q, seg_k, ga, w_out, qkv, lse],
        [((3, seq, wide), BF16), ((8, wide), F32)],
        after,
        scratch=[
            pltpu.VMEM((seq // BQ, BQ, width), F32),
            pltpu.VMEM((seq, wide), BF16),
            pltpu.VMEM((2, seq, wide), F32),
        ],
    )


def eight(values):
    return jnp.sum(values.reshape(values.shape[0] // 8, 8, values.shape[1]), axis=0)


def project_out(flip, core_ref, mixed_a_ref, mixed_b_ref, w_a_ref, w_b_ref, out_ref):
    rows = out_ref.shape[0]
    at = pl.ds(pl.multiple_of(jnp.bitwise_xor(core_ref[0], flip) * rows, rows), rows)
    out = mm(mixed_a_ref[at, :], w_a_ref[...]) + mm(mixed_b_ref[at, :], w_b_ref[...])
    out_ref[...] = out.astype(out_ref.dtype)


def second_norm(start_ref, own_ref, near_ref, b_ref, gain_ref, shift_ref, after_ref, n2_ref):
    value = start_ref[...] + (own_ref[...] + near_ref[...].astype(F32)) + b_ref[...].astype(F32)
    after_ref[...] = value
    xhat, _ = normalize(value)
    n2_ref[...] = (xhat * gain_ref[...].astype(F32) + shift_ref[...].astype(F32)).astype(BF16)


def second_norm_back(here_ref, near_ref, far_ref, after_ref, cot_ref, ok_ref, gain_ref, mid_ref, ga_ref, sums_ref):
    @pl.when(pl.program_id(0) == 0)
    def _():
        sums_ref[...] = jnp.zeros_like(sums_ref)

    grad = here_ref[...].astype(F32) + near_ref[...].astype(F32) + far_ref[...].astype(F32)
    xhat, rstd = normalize(after_ref[...])
    grad_after = cot_ref[...].astype(F32) * ok_ref[...]
    mid = grad_after + norm_back(grad, gain_ref[...].astype(F32), xhat, rstd)
    mid_ref[...] = mid
    ga_ref[...] = mid.astype(BF16)
    sums_ref[0] += eight(mid)
    sums_ref[1] += eight(grad * xhat)
    sums_ref[2] += eight(grad)
    sums_ref[3] += eight(grad_after)


def first_norm_back(own_ref, near_ref, start_ref, mid1_ref, mid2_ref, gain_ref, out_ref, sums_ref):
    @pl.when(pl.program_id(0) == 0)
    def _():
        sums_ref[...] = jnp.zeros_like(sums_ref)

    grad = own_ref[...] + near_ref[...].astype(F32)
    xhat, rstd = normalize(start_ref[...])
    mid = jnp.where(pl.program_id(0) * 2 < pl.num_programs(0), mid1_ref[...], mid2_ref[...])
    out_ref[...] = (mid + norm_back(grad, gain_ref[...].astype(F32), xhat, rstd)).astype(BF16)
    sums_ref[0] += eight(grad * xhat)
    sums_ref[1] += eight(grad)


def down_out(act_n_ref, act_c1_ref, act_c2_ref, w_ref, out_ref):
    half = act_c1_ref.shape[0]
    out_ref[0] = mm(act_n_ref[...], w_ref[...]).astype(BF16)
    out_ref[1, :half, :] = mm(act_c1_ref[...], w_ref[...]).astype(BF16)
    out_ref[1, half:, :] = mm(act_c2_ref[...], w_ref[...]).astype(BF16)


def down_in(act_o_ref, act_f1_ref, act_f2_ref, after1_ref, after2_ref, got_ref, b_ref, w_ref, base_ref, far_ref):
    half = act_f1_ref.shape[0]
    for piece, act_ref, after_ref in ((0, act_f1_ref, after1_ref), (1, act_f2_ref, after2_ref)):
        at = slice(piece * half, (piece + 1) * half)
        down = mm(act_o_ref[at, :], w_ref[...]) + got_ref[0, at, :].astype(F32)
        base_ref[at, :] = after_ref[...] + down + b_ref[...].astype(F32)
        far_ref[at, :] = (mm(act_ref[...], w_ref[...]) + got_ref[1, at, :].astype(F32)).astype(BF16)


def finish(base_ref, far_ref, ok_ref, out_ref):
    out_ref[...] = ((base_ref[...] + far_ref[...].astype(F32)) * ok_ref[...]).astype(BF16)


def hand_on(in_ref, out_ref):
    out_ref[...] = in_ref[...]


def hand_on_all(*refs):
    count = len(refs) // 2
    for in_ref, out_ref in zip(refs[:count], refs[count:]):
        out_ref[...] = in_ref[...]


def handed(value, after):
    return run(hand_on, "hand_on", [value], [(value.shape, value.dtype)], after)


def small_first(two_ref, more_ref, one_ref, out_ref):
    out_ref[...] = jnp.zeros_like(out_ref)
    two = [two_ref[at] + more_ref[at] for at in range(4)]
    rows = [two[0], one_ref[0], one_ref[1], two[1], two[2], two[3]]
    for at, part in enumerate(rows):
        out_ref[at:at + 1, :] = jnp.sum(part, axis=0, keepdims=True)


def small_second(own_ref, near_ref, bias_a_ref, bias_b_ref, send_ref, keep_ref):
    total = own_ref[...] + near_ref[...]
    wide = bias_a_ref.shape[1]
    for out_ref, bias_ref in ((send_ref, bias_b_ref), (keep_ref, bias_a_ref)):
        out_ref[...] = total
        out_ref[6:7, :wide] = bias_ref[0:1, :]
        out_ref[6:7, wide:2 * wide] = bias_ref[4:5, :]


def small_third(own_ref, far_ref, *refs):
    out_ref = refs[-1]
    out_ref[...] = own_ref[...] + far_ref[...]
    out_ref[7:8, :] = sum(jnp.sum(part[...], axis=0, keepdims=True) for part in refs[:-1])


def small_add(own_ref, far_ref, out_ref):
    out_ref[...] = own_ref[...] + far_ref[...]


def add_two(left_ref, right_ref, out_ref):
    out_ref[...] = add_low(left_ref[...], right_ref[...])


def token_products(pieces_of, form, side_ref, *refs):
    count = len(pieces_of)
    lefts, rights, rest = refs[:count], refs[count:2 * count], refs[2 * count:]
    block = 256
    steps = lefts[0].shape[1] // block
    for i in range(steps):
        first = i < steps // 2
        if form == "base":
            row = i
        else:
            row = i % (steps // 2) + (1 - side_ref[0] if first else side_ref[0]) * (steps // 2)
        at = pl.ds(row * block if form == "base" else pl.multiple_of(row * block, block), block)
        total = sum(
            mm(
                left[lp * tokens:(lp + 1) * tokens, at],
                right[rp * tokens:(rp + 1) * tokens, :],
                TN,
            )
            for left, right, (lp, rp, tokens) in zip(lefts, rights, pieces_of)
        )
        into = slice(i % (steps // 2) * block, (i % (steps // 2) + 1) * block)
        if form == "base":
            rest[0][at, :] = total
            continue
        if form == "based":
            total = total + rest[0][at, :]
        rest[-2 if first else -1][into, :] = total.astype(BF16)


def token_call(sides, pairs, base, after):
    tall, wide = pairs[0][0].shape[1], pairs[0][2].shape[1]
    form = "base" if base is True else "full" if base is None else "based"
    args = [sides] + [pair[0] for pair in pairs] + [pair[2] for pair in pairs]
    if form == "based":
        args.append(base)
    outs = [((tall, wide), F32)] if form == "base" else [((tall // 2, wide), BF16)] * 2
    pieces_of = [(pair[1], pair[3], pair[4]) for pair in pairs]
    kernel = functools.partial(token_products, pieces_of, form)
    return run(kernel, "token_products", args, outs, after, scalars=1, cost=60)


def three_products(x_ref, gp_ref, q_ref, kv_ref):
    q_ref[...] = mm(x_ref[...], gp_ref[0]).astype(BF16)
    for c in range(2):
        kv_ref[c] = mm(x_ref[...], gp_ref[c + 1]).astype(BF16)


def three_call(x_turned, gp, after):
    tall, seq = x_turned.shape
    wide = gp.shape[2]
    block = 256
    return run(
        three_products,
        "three_products",
        [x_turned, gp],
        [((tall, wide), BF16), ((2, tall, wide), BF16)],
        after,
        grid=(tall // block,),
        in_specs=[pl.BlockSpec((block, seq), lambda i: (i, 0)), pl.BlockSpec(gp.shape, lambda i: (0, 0, 0))],
        out_specs=[
            pl.BlockSpec((block, wide), lambda i: (i, 0)),
            pl.BlockSpec((2, block, wide), lambda i: (0, i, 0)),
        ],
    )


def turned_product(mixed_ref, ga_ref, out_ref):
    out_ref[...] = mm(ga_ref[...], mixed_ref[...], TN).astype(BF16)


def back_project(flip, core_ref, gp_a_ref, gp_b_ref, w_a_ref, w_b_ref, out_ref):
    rows = out_ref.shape[0]
    at = pl.ds(pl.multiple_of(jnp.bitwise_xor(core_ref[0], flip) * rows, rows), rows)
    out = sum(
        mm(gp_ref[c, at, :], w_ref[c], NT)
        for c in range(3)
        for gp_ref, w_ref in ((gp_a_ref, w_a_ref), (gp_b_ref, w_b_ref))
    )
    out_ref[...] = out.astype(out_ref.dtype)


def by_rows(kernel, name, args, outs, after, block=128, rows=None, piece=0, halves=(), token=False):
    rows = rows or args[0].shape[0]
    steps = rows // block

    def spec(shape, at=None):
        rest = (0,) * (len(shape) - 1)
        cut = (block,) + tuple(shape[1:])
        if at in halves:
            first = halves.index(at) * steps // 2
            return pl.BlockSpec(cut, lambda i: (jnp.clip(i - first, 0, steps // 2 - 1),) + rest)
        if shape[0] == rows:
            return pl.BlockSpec(cut, lambda i: (i,) + rest)
        if shape[0] == 2 * rows:
            return pl.BlockSpec(cut, lambda i: (i + piece * steps,) + rest)
        return pl.BlockSpec(tuple(shape), lambda i: (0,) * len(shape))

    return run(
        kernel,
        name,
        args,
        outs,
        after,
        grid=(steps,),
        in_specs=[spec(arg.shape, at) for at, arg in enumerate(args)],
        out_specs=[spec(shape) for shape, _ in outs],
        size=1,
        token=token,
    )


def fold(bit, last, side_ref, cur_ref, got_ref, *out_refs):
    if last:
        out_refs[0][...] = add_low(cur_ref[...], got_ref[...])
        return
    half = got_ref.shape[0] // 2
    for side, out_ref in ((1 - side_ref[bit], out_refs[0]), (side_ref[bit], out_refs[1])):
        at = pl.ds(pl.multiple_of(side * half, half), half)
        out_ref[...] = add_low(cur_ref[at, :], got_ref[at, :])


def begin_pair(paired, side_ref, *refs):
    send_ref, keep_ref = refs[-2:]
    if paired:
        parts = [(refs[0].at[c], refs[1].at[c]) for c in range(2)]
    else:
        parts = [refs[0:1], refs[1:3]]
    for side in range(2):

        @pl.when(side_ref[0] == side)
        def _():
            for part, out_ref in ((parts[1 - side], send_ref), (parts[side], keep_ref)):
                out_ref[...] = part[0][...] if len(part) == 1 else add_low(part[0][...], part[1][...])


def join(left_ref, right_ref, out_ref):
    rows = left_ref.shape[0]
    out_ref[:rows, :] = left_ref[...]
    out_ref[rows:, :] = right_ref[...]


def place(piece, spot_ref, own_ref, other_ref, out_ref):
    count = own_ref.shape[0] // piece
    steps = out_ref.shape[0] // piece
    for at in range(steps):
        apart = jnp.bitwise_xor(pl.program_id(0) * steps + at, spot_ref[0])
        rows = pl.ds(pl.multiple_of(jnp.bitwise_and(apart, count - 1) * piece, piece), piece)
        far_side = apart >= count
        into = slice(at * piece, (at + 1) * piece)

        @pl.when(far_side)
        def _():
            out_ref[into, :] = other_ref[rows, :].astype(F32)

        @pl.when(jnp.logical_not(far_side))
        def _():
            out_ref[into, :] = own_ref[rows, :].astype(F32)


def pieces(count, spot, own_ref, other_ref, first, steps):
    piece = own_ref.shape[0] // count
    for at in range(steps):
        apart = jnp.bitwise_xor(first + at, spot)
        rows = pl.ds(pl.multiple_of(jnp.bitwise_and(apart, count - 1) * piece, piece), piece)
        mine, others = own_ref[rows, :].astype(F32), other_ref[rows, :].astype(F32)
        yield at * piece, piece, jnp.where(apart >= count, others, mine)


def place_turned(count, spot_ref, own_ref, other_ref, w_out_ref, part_ref):
    for at, piece, value in pieces(count, spot_ref[0], own_ref, other_ref, 0, count):
        w_out_ref[:, at:at + piece] = value.T
    for at, piece, value in pieces(count, spot_ref[0], own_ref, other_ref, count, count):
        part_ref[at:at + piece, :] = value


def place_two(count, spot_ref, own_ref, other_ref, _, out_ref):
    for at, piece, value in pieces(count, spot_ref[0], own_ref, other_ref, pl.program_id(0) * count, count):
        out_ref[at:at + piece, :] = value


class Sum:
    def __init__(self, size, height, first=0):
        self.size, self.bits, self.height = size, size.bit_length() - 1, height
        me = lax.axis_index("dp")
        order = [(first + step) % self.bits for step in range(self.bits)]
        self.flips = [1 << b for b in order]
        sides = [(me // flip) % 2 for flip in self.flips]
        self.sides = jnp.stack(sides).astype(jnp.int32)
        self.spot = sum(side << (self.bits - 1 - step) for step, side in enumerate(sides))

    def begin(self, send, keep):
        self.keep, self.step = keep, 0
        self.sent = swap(send, "dp", self.size, self.flips[0])

    def begin_pairs(self, arrays, after):
        shape = arrays[0].shape[-2:]
        send, keep = run(
            functools.partial(begin_pair, len(arrays) == 2), "begin_pair", [self.sides] + list(arrays),
            [(shape, BF16)] * 2, after, scalars=1,
        )
        self.begin(send, keep)
        return keep

    def fold(self, after):
        if self.step >= self.bits:
            return after
        self.step += 1
        last = self.step == self.bits
        rows, columns = self.sent.shape
        kernel = functools.partial(fold, self.step, last)
        outs = [((rows, columns), BF16)] if last else [((rows // 2, columns), BF16)] * 2
        out = run(kernel, "fold", [self.sides, self.keep, self.sent], outs, after, scalars=1, cost=60)
        self.keep = out if last else out[1]
        send = out if last else out[0]
        self.sent = swap(send, "dp", self.size, self.flips[min(self.step, self.bits - 1)])
        return self.keep

    def spread(self, after):
        if self.step < self.bits:
            return after
        bit = 2 * self.bits - 2 - self.step
        rows, columns = self.keep.shape
        self.keep = run(join, "join", [self.keep, self.sent], [((2 * rows, columns), BF16)], after)
        self.sent = swap(self.keep, "dp", self.size, self.flips[bit])
        self.step += 1
        return self.keep

    def complete(self, after):
        while self.step < self.bits:
            after = self.fold(after)
        while self.step < 2 * self.bits - 1:
            after = self.spread(after)
        return after

    def place(self, after):
        after = self.complete(after)
        rows, columns = self.keep.shape
        piece = rows * 2 // self.size
        placed, token = run(
            functools.partial(place, piece),
            "place",
            [self.spot.reshape(1).astype(jnp.int32), self.keep, self.sent],
            [((2 * rows, columns), F32)],
            after,
            grid=(2,),
            size=1,
            token=True,
            in_specs=[
                pl.BlockSpec(memory_space=pltpu.SMEM),
                pl.BlockSpec((rows, columns), lambda i: (0, 0)),
                pl.BlockSpec((rows, columns), lambda i: (0, 0)),
            ],
            out_specs=[pl.BlockSpec((rows, columns), lambda i: (i, 0))],
        )
        return placed[: self.height], token

    def place_out(self, after):
        after = self.complete(after)
        rows, columns = self.keep.shape
        return run(
            functools.partial(place_turned, self.size // 2),
            "place_turned",
            [self.spot.reshape(1).astype(jnp.int32), self.keep, self.sent],
            [((columns, rows), F32), ((3 * rows, columns), F32)],
            after,
            grid=(1,),
            size=1,
            token=True,
            in_specs=[pl.BlockSpec(memory_space=pltpu.SMEM)]
            + [pl.BlockSpec((rows, columns), lambda i: (0, 0))] * 2,
            out_specs=[
                pl.BlockSpec((columns, rows), lambda i: (0, 0)),
                pl.BlockSpec((rows, columns), lambda i: (0, 0)),
            ],
        )

    def place_rest(self, into, after):
        after = self.complete(after)
        rows, columns = self.keep.shape
        return run(
            functools.partial(place_two, self.size // 2),
            "place_two",
            [self.spot.reshape(1).astype(jnp.int32), self.keep, self.sent, into],
            [((3 * rows, columns), F32)],
            after,
            grid=(2,),
            size=1,
            in_specs=[pl.BlockSpec(memory_space=pltpu.SMEM)]
            + [pl.BlockSpec((rows, columns), lambda i: (0, 0))] * 2
            + [pl.BlockSpec(memory_space=pl.ANY)],
            out_specs=[pl.BlockSpec((rows, columns), lambda i: (i + 1, 0))],
            aliases={3: 0},
        )


def gelu_and_slope(up):
    size = jnp.abs(up)
    t = 1.0 / (1.0 + (0.3275911 * 0.7071067811865476) * size)
    bell = jnp.exp(-0.5 * up * up)
    poly = t * (
        0.5 * 0.254829592
        + t * (0.5 * -0.284496736 + t * (0.5 * 1.421413741 + t * (0.5 * -1.453152027 + t * (0.5 * 1.061405429))))
    )
    tail = poly * bell
    cdf = jnp.where(up >= 0.0, 1.0 - tail, tail)
    return up * cdf, cdf + up * bell * 0.3989422804014327


def feed(count, piece, *refs):
    n2_refs, (gd_ref, ok_ref, w_up_ref, b_up_ref, w_down_ref, gn2_ref, act_ref, gup_ref, gb_ref) = refs[:count], refs[count:]
    hidden, rows, step = w_up_ref.shape[1], n2_refs[0].shape[0], 256

    def products(block, at):
        part = slice(at, at + step)
        given = slice((piece + block) * rows, (piece + block + 1) * rows)
        up = mm(n2_refs[block][...], w_up_ref[:, part]) + b_up_ref[:, part].astype(F32)
        return up, mm(gd_ref[given, :], w_down_ref[part, :], NT), ok_ref[given, :]

    def rest(block, at, up, grad_act, ok):
        part, into = slice(at, at + step), slice(block * rows, (block + 1) * rows)
        act, slope = gelu_and_slope(up)
        grad_up = (slope * (grad_act * ok)).astype(BF16)
        act_ref[into, part] = (act * ok).astype(BF16)
        gup_ref[into, part] = grad_up
        total = jnp.sum(grad_up.astype(F32).reshape(rows // 8, 8, step), axis=0)
        gb_ref[:, part] = total if block == 0 else gb_ref[:, part] + total
        if at + step == hidden:
            gn2_ref[into, :] = mm(gup_ref[into, :], w_up_ref[...], NT).astype(BF16)

    waiting = None
    for block in range(count):
        for at in range(0, hidden, step):
            made = products(block, at)
            if waiting is not None:
                rest(*waiting)
            waiting = (block, at) + made
    rest(*waiting)


def feed_call(n2_pieces, gd, ok, piece, w_up, b_up, w_down, after):
    hidden, count = w_up.shape[1], len(n2_pieces)
    rows = n2_pieces[0].shape[0] * count
    return run(
        functools.partial(feed, count, piece),
        "feed",
        list(n2_pieces) + [gd, ok, w_up, b_up, w_down],
        [((rows, D), BF16), ((rows, hidden), BF16), ((rows, hidden), BF16), ((8, hidden), F32)],
        after,
    )


def swap(value, axis, size, flip):
    return lax.ppermute(value, axis, [(i, i ^ flip) for i in range(size)])


def add_low(left, right):
    return (left.astype(F32) + right.astype(F32)).astype(BF16)


def sum_over(value, axis, size):
    flip = 1
    while flip < size:
        value = value + swap(value, axis, size, flip)
        flip *= 2
    return value


def on_device(
    dp_size,
    mp_size,
    tokens,
    segment_ids,
    valid_mask,
    patch_index,
    gsd_index,
    w_qkv,
    bias_qv,
    w_out,
    b_out,
    gain_one,
    shift_one,
    gain_two,
    shift_two,
    w_up,
    b_up,
    w_down,
    b_down,
    cotangent,
):
    own_rows = tokens.shape[0]
    mp = lax.axis_index("mp")
    core = mp % 2
    row = mp // 2

    def near(value):
        return swap(value, "mp", mp_size, 1)

    def far(value):
        return swap(value, "mp", mp_size, 2)

    core_s = core.reshape(1).astype(jnp.int32)
    down_sum, up_sum = Sum(dp_size, w_down.shape[0]), Sum(dp_size, w_up.shape[0])
    first_sum, second_sum = Sum(dp_size, 2 * D), Sum(dp_size, 2 * D)
    sides = down_sum.sides

    cot_near = near(cotangent)
    inputs = [segment_ids, valid_mask, patch_index, gsd_index]
    shape = (3, D // 4, w_qkv.shape[2])
    piece_a, piece_b = run(cut, "cut", [sides, w_qkv], [(shape, BF16)] * 2, None, scalars=1, size=1)
    segment_ids, valid_mask, patch_index, gsd_index = run(
        hand_on_all, "hand_on_all", inputs, [(part.shape, part.dtype) for part in inputs], piece_b, size=1
    )
    far_bias = far(bias_qv)
    far_a, far_b = far(piece_a), far(piece_b)

    own_start = mp * own_rows
    level = image_levels(segment_ids, gsd_index)
    codes = jnp.stack([patch_index // GRID, patch_index % GRID]) * GSDS + level
    own_codes = lax.dynamic_slice_in_dim(codes.reshape(2, -1, 1), own_start, own_rows, axis=1)
    all_valid = valid_mask.reshape(-1, 1).astype(F32)

    def valid_of(flip):
        at = jnp.bitwise_xor(mp, flip) * own_rows
        return lax.dynamic_slice_in_dim(all_valid, at, own_rows)

    own_valid = valid_of(0)

    row_seg = lax.dynamic_index_in_dim(segment_ids, row, 0, keepdims=True)
    row_ok = lax.dynamic_index_in_dim(valid_mask, row, 0, keepdims=True)
    seg_k = jnp.where(row_ok == 1, row_seg, -1)
    seg_q = row_seg.reshape(-1, 1)

    start_sum, normed = by_rows(
        front, "front",
        [tokens, own_codes[0], own_codes[1], code_table(), gain_one[None], shift_one[None]],
        [(tokens.shape, F32), (tokens.shape, BF16)], [segment_ids, cot_near],
    )
    half = (own_rows, D)
    w_out_sent, a_pass = run(
        hand_on_all, "hand_on_all", [w_out, far_a], [(w_out.shape, BF16), (far_a.shape, BF16)], normed, cost=60
    )
    far_out = far(w_out_sent)
    other_a = swap(a_pass, "dp", dp_size, 1)
    normed_row = run(in_row, "in_row", [core_s, normed, near(normed)], [((2 * own_rows, D), BF16)], a_pass, scalars=1)
    b_pass, cot_sent = run(
        hand_on_all, "hand_on_all", [far_b, cotangent], [(far_b.shape, BF16), (half, BF16)], normed_row
    )
    other_b = swap(b_pass, "dp", dp_size, 1)
    cot_far = far(cot_sent)

    qkv_a, mixed_a, lse_a = forward_call(sides, seg_q, seg_k, normed_row, bias_qv, [w_qkv], cot_sent)
    pieces_b = [a_pass, b_pass, other_a, other_b]
    qkv_b, mixed_b, lse_b = forward_call(sides, seg_q, seg_k, normed_row, far_bias, pieces_b, lse_a)
    operands = [core_s, mixed_a, mixed_b, w_out, far_out]
    attn_near = run(functools.partial(project_out, 1), "project_out", operands, [(half, BF16)], lse_b, scalars=1)
    attn_own = run(functools.partial(project_out, 0), "project_out", operands, [(half, F32)], attn_near, scalars=1)
    attn_got = near(attn_near)
    quarter = own_rows // 2
    piece_shape = (quarter, D)
    wide = w_qkv.shape[2]
    turned = [((D, wide), BF16)]
    tile = [((8, D), F32)]
    flips = [1 << b for b in range(dp_size.bit_length() - 1)]
    b_up_row = b_up[None, :]
    ffn = [w_up, b_up_row, w_down]
    last = attn_own

    def norm_two(piece, last):
        return by_rows(
            second_norm, "second_norm",
            [start_sum, attn_own, attn_got, b_out[None], gain_two[None], shift_two[None]],
            [(piece_shape, F32), (piece_shape, BF16)], last, rows=quarter, piece=piece,
        )

    def norm_two_back(piece, from_far, after_attn, last):
        return by_rows(
            second_norm_back, "second_norm_back",
            [gn2_o, from_near, from_far, after_attn, cotangent, own_valid, gain_two[None]],
            [(piece_shape, F32), (piece_shape, BF16), ((4, 8, D), F32)], last, rows=quarter, piece=piece,
        )

    operands = [core_s, None, None, w_qkv, None]
    after1, n2_1 = norm_two(0, last)
    far1, near1 = far(n2_1), near(n2_1)
    last = n2_1
    after2, n2_2 = norm_two(1, last)
    far2, near2 = far(n2_2), near(n2_2)
    last = n2_2
    gn2_o, act_o, gup_o, gb_o = feed_call([n2_1, n2_2], cotangent, own_valid, 0, *ffn, last)
    last = gb_o
    last = cot_pass = handed(cot_far, last)
    cot_cross = near(cot_pass)
    gn2_n, act_n, gup_n, gb_n = feed_call([near1, near2], cot_near, valid_of(1), 0, *ffn, last)
    from_near = near(gn2_n)
    last = gb_n
    last = far1_pass = handed(far1, last)
    cross1 = near(far1_pass)
    gn2_f1, act_f1, gup_f1, gb_f1 = feed_call([far1_pass], cot_pass, valid_of(2), 0, *ffn, last)
    last = gb_f1
    gn2_c1, act_c1, gup_c1, gb_c1 = feed_call([cross1], cot_cross, valid_of(3), 0, *ffn, last)
    got1 = near(gn2_c1)
    last = gb_c1
    here = [(act_o, 0, cotangent, 0, own_rows), (act_n, 0, cot_near, 0, own_rows)]
    last = down_here = token_call(sides, here, True, last)
    last = sent1 = by_rows(add_two, "add_two", [gn2_f1, got1], [(piece_shape, BF16)], last)
    back1 = far(sent1)
    last = far2_pass = handed(far2, last)
    cross2 = near(far2_pass)
    gn2_f2, act_f2, gup_f2, gb_f2 = feed_call([far2_pass], cot_pass, valid_of(2), 1, *ffn, last)
    last = gb_f2
    gn2_c2, act_c2, gup_c2, gb_c2 = feed_call([cross2], cot_cross, valid_of(3), 1, *ffn, last)
    got2 = near(gn2_c2)
    last = gb_c2
    there = [(act_f1, 0, cot_pass, 0, quarter), (act_c1, 0, cot_cross, 0, quarter)]
    there += [(act_f2, 0, cot_pass, 1, quarter), (act_c2, 0, cot_cross, 1, quarter)]
    down_send, down_keep = token_call(sides, there, down_here, last)
    down_sum.begin(down_send, down_keep)
    last = down_keep
    last = sent2 = by_rows(add_two, "add_two", [gn2_f2, got2], [(piece_shape, BF16)], last)
    back2 = far(sent2)
    mid1, ga1, sums_two = norm_two_back(0, back1, after1, last)
    ga1_near = near(ga1)
    last = ga1
    pairs = [(n2_1, 0, gup_o, 0, quarter), (n2_2, 0, gup_o, 1, quarter)]
    pairs += [(near1, 0, gup_n, 0, quarter), (near2, 0, gup_n, 1, quarter)]
    pairs += [(far1_pass, 0, gup_f1, 0, quarter), (cross1, 0, gup_c1, 0, quarter)]
    pairs += [(far2_pass, 0, gup_f2, 0, quarter), (cross2, 0, gup_c2, 0, quarter)]
    up_send, up_keep = token_call(sides, pairs, None, last)
    up_sum.begin(up_send, up_keep)
    last = up_keep
    mid2, ga2, sums_more = norm_two_back(1, back2, after2, last)
    ga2_near = near(ga2)
    last = ga2
    last = x_turned = run(turn, "turn", [normed_row], [((D, 2 * own_rows), BF16)], last, cost=60)
    last = far_qkv = run(assemble, "assemble", [sides] + pieces_b, [(w_qkv.shape, BF16)], last, scalars=1, cost=60)
    last = ga_row = run(
        in_row_pieces, "in_row", [core_s, ga1, ga2, ga1_near, ga2_near], [((2 * own_rows, D), BF16)], last, scalars=1
    )
    last = gw_out_b = run(turned_product, "turned_product", [mixed_b, ga_row], turned, last)
    far_out_grad = far(gw_out_b)
    last = gw_out_a = run(turned_product, "turned_product", [mixed_a, ga_row], turned, last)
    last = down_sum.fold(last)
    gp_b, bias_b = backward_call(seg_q, seg_k, ga_row, far_out, qkv_b, lse_b, last)
    last = bias_b
    q_b, kv_b = three_call(x_turned, gp_b, last)
    far_q, far_kv = far(q_b), far(kv_b)
    last = q_b
    last = out_both = by_rows(add_two, "add_two", [gw_out_a, far_out_grad], [((D, wide), BF16)], last, block=512)
    last = down_sum.fold(last)
    gp_a, bias_a = backward_call(seg_q, seg_k, ga_row, w_out, qkv_a, lse_a, last)
    last = bias_a
    last = up_sum.fold(last)
    q_a, kv_a = three_call(x_turned, gp_a, last)
    last = q_a
    last = down_sum.fold(last)
    last = first_sum.begin_pairs([out_both, q_a, far_q], last)
    operands[1:3] = gp_a, gp_b
    operands[4] = far_qkv
    last = gn_near = run(functools.partial(back_project, 1), "back_project", operands, [(half, BF16)], last, scalars=1)
    operands[1:3] = gp_a, gp_b
    operands[4] = far_qkv
    last = gn_own = run(functools.partial(back_project, 0), "back_project", operands, [(half, F32)], last, scalars=1)
    grad_tokens, sums_one = by_rows(
        first_norm_back, "first_norm_back",
        [gn_own, near(gn_near), start_sum, mid1, mid2, gain_one[None]],
        [(half, BF16), ((2, 8, D), F32)], last, halves=(3, 4),
    )
    last = sums_one
    last = down_sent = run(down_out, "down_out", [act_n, act_c1, act_c2, w_down], [((2,) + half, BF16)], last)
    down_near = near(down_sent)
    last = up_sum.fold(last)
    last = down_sum.spread(last)
    last = second_sum.begin_pairs([kv_a, far_kv], last)
    down_base, down_far = run(
        down_in, "down_in", [act_o, act_f1, act_f2, after1, after2, down_near, b_down[None], w_down],
        [(half, F32), (half, BF16)], last,
    )
    last = down_base
    last = small = run(small_first, "small_first", [sums_two, sums_more, sums_one], tile, last)
    small_got = near(small)
    last = up_sum.fold(last)
    last = first_sum.fold(last)
    last = down_sum.spread(last)
    last = second_sum.fold(last)
    send, small = run(small_second, "small_second", [small, small_got, bias_a, bias_b], tile * 2, last)
    small_got = far(send)
    last = small
    last = up_sum.spread(last)
    last = first_sum.fold(last)
    last = second_sum.fold(last)
    gbs = [gb_o, gb_n, gb_f1, gb_c1, gb_f2, gb_c2]
    last = small = run(small_third, "small_third", [small, small_got] + gbs, tile, last)
    small_got = swap(small, "dp", dp_size, flips[0])
    last = first_sum.fold(last)
    last = up_sum.spread(last)
    last = second_sum.fold(last)
    last = first_sum.spread(last)
    last = down_sent = handed(down_far, last)
    down_got = far(down_sent)
    last = second_sum.spread(last)
    grad_w_down, last = down_sum.place(last)
    last = first_sum.spread(last)
    last = small = run(small_add, "small_add", [small, small_got], tile, last)
    small_got = swap(small, "dp", dp_size, flips[1])
    last = second_sum.spread(last)
    last = small = run(small_add, "small_add", [small, small_got], tile, last)
    small_got = swap(small, "dp", dp_size, flips[2])
    grad_w_up, last = up_sum.place(last)
    layer_out, last = by_rows(
        finish, "finish", [down_base, down_got, own_valid], [(half, BF16)], last, token=True
    )
    for flip in flips[3:]:
        last = small = run(small_add, "small_add", [small, small_got], tile, last)
        small_got = swap(small, "dp", dp_size, flip)
    last = small = run(small_add, "small_add", [small, small_got], tile, last)
    grad_w_out, grad_w_qkv, last = first_sum.place_out(last)
    grad_w_qkv = second_sum.place_rest(grad_w_qkv, last).reshape(w_qkv.shape)
    grad_bias_qv = small[6, : 2 * wide].reshape(2, wide)
    grad_b_up = small[7]
    return (
        layer_out,
        grad_tokens,
        grad_w_qkv,
        grad_bias_qv,
        grad_w_out,
        small[0],
        small[1],
        small[2],
        small[3],
        small[4],
        grad_w_up,
        grad_b_up,
        grad_w_down,
        small[5],
    )


def solution(mesh):
    return jax.shard_map(
        functools.partial(on_device, mesh.shape["dp"], mesh.shape["mp"]),
        mesh=mesh,
        in_specs=(
            P(("dp", "mp"), None),
            P("dp", None),
            P("dp", None),
            P("dp", None),
            P("dp", None),
            P(None, None, "mp"),
            P(None, "mp"),
            P("mp", None),
            P(),
            P(),
            P(),
            P(),
            P(),
            P(None, "mp"),
            P("mp"),
            P("mp", None),
            P(),
            P(("dp", "mp"), None),
        ),
        out_specs=(
            P(("dp", "mp"), None),
            P(("dp", "mp"), None),
            P(None, None, "mp"),
            P(None, "mp"),
            P("mp", None),
            P(),
            P(),
            P(),
            P(),
            P(),
            P(None, "mp"),
            P("mp"),
            P("mp", None),
            P(),
        ),
        check_vma=False,
    )
```
